32 devices in a mesh: lon: 16 (over z, y, x), lat: 2 (over core).
Axes of the slice: x: 2, y: 2, z: 4, core: 2. Of those that a mesh axis runs over, the one named last changes fastest.
Arguments:
- thermal_anomaly: float32 [16, 128, 256], P(None, 'lon', 'lat'), may hold values from -6 to 6
- saltiness_anomaly: float32 [16, 128, 256], P(None, 'lon', 'lat'), may hold values from -6 to 6
- zonal_current: float32 [16, 128, 256], P(None, 'lon', 'lat'), may hold values from -3 to 3
- meridional_current: float32 [16, 128, 256], P(None, 'lon', 'lat'), may hold values from -3 to 3
- bottom_ocean_layer: int32 [128, 256], P('lon', 'lat'), may hold values from 0 to 16
- seam_axis_meridian: int32 [1], replicated, may hold values from 0 to 255
- interface_diffusivity: float32 [15, 128, 256], P(None, 'lon', 'lat'), may hold values from 0.1 to 10
- atmospheric_forcing: float32 [2, 128, 256], P(None, 'lon', 'lat'), may hold values from -6 to 6
Outputs:
- temperature_next: float32 [16, 128, 256], P(None, 'lon', 'lat')
- salinity_next: float32 [16, 128, 256], P(None, 'lon', 'lat')
- zonal_next: float32 [16, 128, 256], P(None, 'lon', 'lat')
- meridional_next: float32 [16, 128, 256], P(None, 'lon', 'lat')
The draws below stay inside these ranges and needn't reach their ends.
Inputs may be any that keep to these rules, and one draw needn't show every extreme that they name: `seam_axis_meridian`: an even code folds about a cell centre, an odd one about a cell corner.
All inputs are finite; a program needn't handle non-finite values.
Results may differ from the reference program's by a relative error of at most 0.0003.
Values sent between devices are 32-bit elements; how exact they have to be, the bound alone decides.
No kernel may reach another device: no remote copies, remote signals or barrier semaphores. Data moves between devices by JAX's collectives and lax.ppermute only.
A program may use at most 64 MiB of HBM per device.

```python
import math
import jax
import jax.numpy as jnp
from jax import lax

SEA_LAYERS = 16
CY = 128
PARALLEL_SPAN = 128
MERIDIAN_SPAN = 256
N_LAT = 2


def banded_field(key, scale, bound, band_rows, band_low, band_high):
    field_shape = (SEA_LAYERS, PARALLEL_SPAN, MERIDIAN_SPAN)
    key_first, key_second, key_third = jax.random.split(key, 3)
    background = jnp.clip(scale * jax.random.normal(key_first, field_shape, jnp.float32), -bound, bound)
    magnitude = jax.random.uniform(key_second, field_shape, jnp.float32, band_low, band_high)
    sign_value = (2 * jax.random.randint(key_third, field_shape, 0, 2) - 1).astype(jnp.float32)
    row_index = jnp.arange(MERIDIAN_SPAN)
    in_band = (row_index >= MERIDIAN_SPAN - band_rows)[None, None, :]
    return jnp.where(in_band, sign_value * magnitude, background).astype(jnp.float32)


def draw_thermal_anomaly(key, part):
    return banded_field(jax.random.fold_in(key, 101), 1.0, 6.0, 4, 4.0, 6.0)


def draw_saltiness_anomaly(key, part):
    return banded_field(jax.random.fold_in(key, 202), 1.0, 6.0, 4, 4.0, 6.0)


def draw_meridional_current(key, part):
    return banded_field(jax.random.fold_in(key, 303), 0.5, 3.0, 3, 2.0, 3.0)


def set_ends(array, own_key, low, high):
    extent = array.shape
    index_at = [jax.random.randint(jax.random.fold_in(own_key, axis), (), 0, extent[axis]) for axis in range(len(extent))]
    array = array.at[tuple(index_at)].set(low)
    longest = extent.index(max(extent))
    index_at[longest] = (index_at[longest] + 1) % extent[longest]
    return array.at[tuple(index_at)].set(high)


def levels(key, dims, shards, least, largest):
    def one(dim, parts):
        heights = jax.random.uniform(jax.random.fold_in(jax.random.fold_in(key, 6), dim), (parts,), jnp.float32, least / len(shards), largest / len(shards))
        return jnp.repeat(jnp.exp(heights), dims[dim] // parts).reshape((-1,) + (1,) * (len(dims) - dim - 1))

    gain = one(*shards[0])
    for cut in shards[1:]:
        gain = gain * one(*cut)
    return gain


def bell_draw(stream_key, extent, width, reach, pieces=(), held_as=jnp.bfloat16):
    values = width * jax.random.normal(stream_key, extent, jnp.float32)
    if pieces:
        values = values * levels(stream_key, extent, pieces, -0.22, 0.18)
    return jnp.clip(values, -reach, reach).astype(held_as)


def setup_inputs(seed: int = 0) -> dict:
    seeds = jax.random.split(jax.random.key(seed), 9)
    thermal_anomaly = draw_thermal_anomaly(jax.random.fold_in(seeds[8], 71), 0)
    saltiness_anomaly = draw_saltiness_anomaly(jax.random.fold_in(seeds[8], 71), 0)
    zonal_current = bell_draw(seeds[2], (SEA_LAYERS, PARALLEL_SPAN, MERIDIAN_SPAN), 0.5, 3.0, ((1, 16), (2, 2)), jnp.float32)
    meridional_current = draw_meridional_current(jax.random.fold_in(seeds[8], 71), 0)
    bottom_ocean_layer = set_ends(jax.random.randint(seeds[4], (PARALLEL_SPAN, MERIDIAN_SPAN), 0, SEA_LAYERS + 1), jax.random.fold_in(seeds[4], 1), 0, SEA_LAYERS).astype(jnp.int32)
    seam_axis_meridian = jax.random.randint(seeds[5], (1,), 0, 2 * PARALLEL_SPAN).astype(jnp.int32)
    interface_diffusivity = jnp.clip(jnp.exp(math.log(10.0) - 4.6051702 * jax.random.uniform(seeds[6], (SEA_LAYERS - 1, PARALLEL_SPAN, MERIDIAN_SPAN), jnp.float32) ** levels(seeds[6], (SEA_LAYERS - 1, PARALLEL_SPAN, MERIDIAN_SPAN), ((1, 16), (2, 2)), -0.2, 0.2)), 0.1, 10.0)
    atmospheric_forcing = bell_draw(seeds[7], (2, PARALLEL_SPAN, MERIDIAN_SPAN), 1.0, 6.0, ((1, 16), (2, 2)), jnp.float32)
    return dict(thermal_anomaly=thermal_anomaly, saltiness_anomaly=saltiness_anomaly, zonal_current=zonal_current, meridional_current=meridional_current, bottom_ocean_layer=bottom_ocean_layer, seam_axis_meridian=seam_axis_meridian, interface_diffusivity=interface_diffusivity, atmospheric_forcing=atmospheric_forcing)


TIME_STEP = 0.2
TRACER_DIFF = 0.2
MOMENTUM_VISC = 0.2
THERMAL_EXPANSION = 0.5
HALINE_CONTRACTION = 0.4
WIND_GAIN = 2.0
VERTICAL_VISC = 1.0
NEIGHBOURS = ((1, 0), (-1, 0), (0, 1), (0, -1))


def implicit(right_side, coupling):
    count = right_side.shape[-3]
    ratios = []
    values = []
    for level_k in range(count):
        below = coupling[level_k] if level_k < count - 1 else 0.0
        above = coupling[level_k - 1] if level_k > 0 else 0.0
        if level_k == 0:
            denom = 1.0 + below
            values.append(right_side[..., 0, :, :] / denom)
        else:
            denom = 1.0 + above + below + above * ratios[level_k - 1]
            values.append((right_side[..., level_k, :, :] + above * values[level_k - 1]) / denom)
        ratios.append(-below / denom)
    result = [values[count - 1]]
    for level_k in range(count - 2, -1, -1):
        result.insert(0, values[level_k] - ratios[level_k] * result[0])
    return jnp.stack(result, axis=-3)


def choose_rows(source, fold_type, sign_column):
    upper = jnp.where(fold_type == 1, source[..., 2], source[..., 1])
    outer = jnp.where(fold_type == 1, source[..., 1], source[..., 0])
    return jnp.stack([upper, outer], axis=-1) * sign_column


def advance(grid_ext, interface_diffusivity, atmospheric_forcing, row_start, rows_total):
    layer_number = (grid_ext.shape[0] - 1) // 4
    cols_n = grid_ext.shape[1] - 4
    rows_n = grid_ext.shape[2] - 4

    def view(source_array, shift_x, shift_y):
        return source_array[..., 2 + shift_x:2 + shift_x + cols_n, 2 + shift_y:2 + shift_y + rows_n]

    tracers = grid_ext[:2 * layer_number].reshape(2, layer_number, cols_n + 4, rows_n + 4)
    zonal = grid_ext[2 * layer_number:3 * layer_number]
    merid = grid_ext[3 * layer_number:4 * layer_number]
    depth_count = grid_ext[4 * layer_number]
    level_ids = jnp.arange(layer_number).astype(jnp.float32)[:, None, None]
    wet_mask = jnp.where(level_ids < depth_count[None], 1.0, 0.0).astype(jnp.float32)

    def face_x(shift_x):
        interp = (7.0 * (view(tracers, shift_x, 0) + view(tracers, shift_x + 1, 0)) - (view(tracers, shift_x - 1, 0) + view(tracers, shift_x + 2, 0))) / 12.0
        return view(zonal, shift_x, 0) * view(wet_mask, shift_x, 0) * view(wet_mask, shift_x + 1, 0) * interp

    def face_y(shift_y):
        interp = (7.0 * (view(tracers, 0, shift_y) + view(tracers, 0, shift_y + 1)) - (view(tracers, 0, shift_y - 1) + view(tracers, 0, shift_y + 2))) / 12.0
        return view(merid, 0, shift_y) * view(wet_mask, 0, shift_y) * view(wet_mask, 0, shift_y + 1) * interp

    advect = -(face_x(0) - face_x(-1)) - (face_y(0) - face_y(-1))
    centre = view(tracers, 0, 0)
    wet_centre = view(wet_mask, 0, 0)
    spread = jnp.zeros_like(centre)
    for shift_x, shift_y in NEIGHBOURS:
        spread = spread + view(wet_mask, shift_x, shift_y) * wet_centre * (view(tracers, shift_x, shift_y) - centre)
    tracer_star = centre + TIME_STEP * (advect + TRACER_DIFF * spread) * wet_centre

    buoyancy = (THERMAL_EXPANSION * grid_ext[:layer_number] - HALINE_CONTRACTION * grid_ext[layer_number:2 * layer_number]) * wet_mask
    pressure = jnp.cumsum(buoyancy, axis=0) - 0.5 * buoyancy
    u_mask = wet_centre * view(wet_mask, 1, 0)
    v_mask = wet_centre * view(wet_mask, 0, 1)
    row_ids = (row_start + jnp.arange(rows_n)).astype(jnp.float32)
    cor_u = 2.0 * (row_ids + 0.5) / rows_total - 1.0
    cor_v = 2.0 * (row_ids + 1.0) / rows_total - 1.0
    v_at_u = 0.25 * (view(merid, 0, 0) + view(merid, 0, -1) + view(merid, 1, 0) + view(merid, 1, -1))
    u_at_v = 0.25 * (view(zonal, 0, 0) + view(zonal, -1, 0) + view(zonal, 0, 1) + view(zonal, -1, 1))
    u_centre = view(zonal, 0, 0)
    v_centre = view(merid, 0, 0)
    u_visc = jnp.zeros_like(u_centre)
    v_visc = jnp.zeros_like(v_centre)
    for shift_x, shift_y in NEIGHBOURS:
        u_visc = u_visc + view(wet_mask, shift_x, shift_y) * view(wet_mask, shift_x + 1, shift_y) * u_mask * (view(zonal, shift_x, shift_y) - u_centre)
        v_visc = v_visc + view(wet_mask, shift_x, shift_y) * view(wet_mask, shift_x, shift_y + 1) * v_mask * (view(merid, shift_x, shift_y) - v_centre)
    u_star = (u_centre + TIME_STEP * (cor_u * v_at_u - (view(pressure, 1, 0) - view(pressure, 0, 0)) + MOMENTUM_VISC * u_visc)) * u_mask
    v_star = (v_centre + TIME_STEP * (-cor_v * u_at_v - (view(pressure, 0, 1) - view(pressure, 0, 0)) + MOMENTUM_VISC * v_visc)) * v_mask
    u_star = u_star.at[0].add(TIME_STEP * WIND_GAIN * atmospheric_forcing[0] * u_mask[0])
    v_star = v_star.at[0].add(TIME_STEP * WIND_GAIN * atmospheric_forcing[1] * v_mask[0])

    tracer_next = implicit(tracer_star, TIME_STEP * interface_diffusivity * wet_centre[:-1] * wet_centre[1:])
    u_next = implicit(u_star, TIME_STEP * VERTICAL_VISC * u_mask[:-1] * u_mask[1:])
    v_next = implicit(v_star, TIME_STEP * VERTICAL_VISC * v_mask[:-1] * v_mask[1:])
    return tracer_next[0], tracer_next[1], u_next, v_next


def reference(thermal_anomaly, saltiness_anomaly, zonal_current, meridional_current, bottom_ocean_layer, seam_axis_meridian, interface_diffusivity, atmospheric_forcing):
    layer_number = thermal_anomaly.shape[0]
    combined_arrays = jnp.concatenate([thermal_anomaly, saltiness_anomaly, zonal_current, meridional_current, bottom_ocean_layer.astype(jnp.float32)[None]], axis=0)
    layer_count = combined_arrays.shape[0]
    fold_code = seam_axis_meridian[0]
    fold_type = jnp.mod(fold_code, 2).astype(jnp.int32)
    sign_column = jnp.concatenate([jnp.ones((2 * layer_number,), jnp.float32), -jnp.ones((2 * layer_number,), jnp.float32), jnp.ones((1,), jnp.float32)])[:, None, None]
    top_rows = combined_arrays[:, :, MERIDIAN_SPAN - 3:]
    mirror_cols = jnp.mod(fold_code - jnp.arange(PARALLEL_SPAN).astype(jnp.int32), PARALLEL_SPAN).astype(jnp.int32)
    source = jnp.take(top_rows, mirror_cols, axis=1)
    ghost = choose_rows(source, fold_type, sign_column)
    padded = jnp.concatenate([jnp.zeros((layer_count, PARALLEL_SPAN, 2), jnp.float32), combined_arrays, ghost], axis=2)
    grid_ext = jnp.concatenate([padded[:, PARALLEL_SPAN - 2:], padded, padded[:, :2]], axis=1)

    def band(band_index):
        first = (band_index * CY).astype(jnp.int32)
        piece = lax.dynamic_slice_in_dim(grid_ext, first, CY + 4, 2)
        mix_piece = lax.dynamic_slice_in_dim(interface_diffusivity, first, CY, 2)
        wind_piece = lax.dynamic_slice_in_dim(atmospheric_forcing, first, CY, 2)
        return advance(piece, mix_piece, wind_piece, first, MERIDIAN_SPAN)

    results = lax.map(band, jnp.arange(N_LAT).astype(jnp.int32))
    outputs = [jnp.transpose(item, (1, 2, 0, 3)).reshape(layer_number, PARALLEL_SPAN, MERIDIAN_SPAN) for item in results]
    return (outputs[0], outputs[1], outputs[2], outputs[3])
```

```python
import jax
import jax.numpy as jnp
from jax import lax
from jax.experimental import pallas as pl
from jax.experimental.pallas import tpu as pltpu
from jax.sharding import PartitionSpec as P

TIME_STEP = 0.2
TRACER_DIFF = 0.2
MOMENTUM_VISC = 0.2
THERMAL_EXPANSION = 0.5
HALINE_CONTRACTION = 0.4
WIND_GAIN = 2.0
VERTICAL_VISC = 1.0

VMEM = pl.BlockSpec(memory_space=pltpu.VMEM)
SMEM = pl.BlockSpec(memory_space=pltpu.SMEM)
SUB = 8


def lane_of(lanes):
    return lax.broadcasted_iota(jnp.int32, (SUB, lanes), 1)


def row_of(lanes):
    return lax.broadcasted_iota(jnp.int32, (SUB, lanes), 0)


def tall(value):
    missing = SUB - value.shape[0]
    if missing == 0:
        return value
    return jnp.concatenate([value, jnp.zeros((missing, value.shape[1]), value.dtype)], axis=0)


def edge_rows_kernel(t_ref, s_ref, u_ref, v_ref, depth_ref, seam_ref, top_ref, bottom_ref):
    levels, width, lanes = t_ref.shape
    is_top = lax.axis_index("lat") == lax.axis_size("lat") - 1
    skip = jnp.where(jnp.logical_and(is_top, lax.rem(seam_ref[0], 2) == 0), 1, 0)
    lane = lane_of(lanes)
    top = jnp.zeros((SUB, lanes), jnp.float32)
    bottom = jnp.zeros((SUB, lanes), jnp.float32)

    def put(value, target, second, top, bottom):
        top = jnp.where(lane == target, pltpu.roll(value, target + 1 + second + skip, 1), top)
        bottom = jnp.where(lane == target, pltpu.roll(value, (target - second) % lanes, 1), bottom)
        return top, bottom

    for k in range(levels):
        for place, ref in ((0, t_ref), (2, s_ref)):
            value = tall(ref[k])
            top, bottom = put(value, place * levels + k, 0, top, bottom)
            top, bottom = put(value, (place + 1) * levels + k, 1, top, bottom)
        for place, ref in ((4, u_ref), (5, v_ref)):
            top, bottom = put(tall(ref[k]), place * levels + k, 0, top, bottom)
    depth = tall(depth_ref[...].astype(jnp.float32))
    top, bottom = put(depth, 6 * levels, 0, top, bottom)
    top, bottom = put(depth, 6 * levels + 1, 1, top, bottom)
    top_ref[...] = top[:width]
    bottom_ref[...] = bottom[:width]


def edge_columns_kernel(
    t_ref, s_ref, u_ref, v_ref, depth_ref, north_ref, south_ref, east_ref, west_ref
):
    levels, width, lanes = t_ref.shape
    for ref, message, near, far in (
        (east_ref, east_ref, width - 1, width - 2),
        (west_ref, west_ref, 0, 1),
    ):
        for place, field, column in (
            (0, t_ref, near),
            (1, t_ref, far),
            (2, s_ref, near),
            (3, s_ref, far),
            (4, u_ref, near),
            (5, v_ref, near),
        ):
            message[pl.ds(place * levels, levels), :] = field[:, column, :]
    depth = depth_ref[...].astype(jnp.float32)
    base = 6 * levels
    east_ref[pl.ds(base, 8), :] = jnp.concatenate(
        [
            depth[width - 1 : width],
            depth[width - 2 : width - 1],
            north_ref[width - 1 : width],
            south_ref[width - 1 : width],
        ]
        * 2,
        axis=0,
    )
    east_ref[pl.ds(base + 8, 8), :] = jnp.zeros((8, lanes), jnp.float32)
    west_ref[pl.ds(base, 8), :] = jnp.concatenate(
        [depth[0:1], depth[1:2], north_ref[0:1], south_ref[0:1]] * 2, axis=0
    )


def mixing_constants(levels):
    gain = TIME_STEP * VERTICAL_VISC
    inner, last, ratio = [], [], 0.0
    for k in range(levels):
        above = gain if k > 0 else 0.0
        last.append(1.0 / (1.0 + above + above * ratio))
        pivot = 1.0 + above + gain + above * ratio
        inner.append(1.0 / pivot)
        ratio = -gain / pivot
    return inner, last


def step_kernel(
    t_ref,
    s_ref,
    u_ref,
    v_ref,
    depth_ref,
    seam_ref,
    mix_ref,
    wind_ref,
    bottom_ref,
    north_ref,
    south_ref,
    west_ref,
    east_ref,
    fold_a_ref,
    fold_b_ref,
    fold_c_ref,
    t_out,
    s_out,
    u_out,
    v_out,
    fold_ref,
    mirror_ref,
    gx_t_ref,
    gx_s_ref,
    u2_ref,
    v2_ref,
    val_ref,
):
    levels, width, lanes = t_ref.shape
    lat = lax.axis_index("lat")
    lat_count = lax.axis_size("lat")
    is_top = lat == lat_count - 1
    lane = lane_of(lanes)
    row = row_of(lanes)
    depth_at = 6 * levels

    rest = lax.rem(seam_ref[0], width)
    fold_ref[pl.ds(0, width), :] = fold_a_ref[...]
    fold_ref[pl.ds(width, width), :] = fold_b_ref[...]
    fold_ref[pl.ds(2 * width, width), :] = fold_c_ref[...]
    for i in range(-1, width + 1):
        mirror_ref[pl.ds(i + 1, 1), :] = fold_ref[pl.ds(width + rest - i, 1), :]
    sign = jnp.where(jnp.logical_and(lane >= 4 * levels, lane < 6 * levels), -1.0, 1.0)
    mirrored = tall(mirror_ref[pl.ds(1, width), :]) * sign
    north = jnp.where(is_top, mirrored, tall(north_ref[...]))
    south = tall(south_ref[...])
    bottom = tall(bottom_ref[...])

    def line(ref, index):
        return jnp.broadcast_to(ref[pl.ds(index, 1), :], (SUB, lanes))

    nw = jnp.where(is_top, line(mirror_ref, 0) * sign, line(west_ref, depth_at + 2))
    ne = jnp.where(is_top, line(mirror_ref, width + 1) * sign, line(east_ref, depth_at + 2))
    se = line(east_ref, depth_at + 3)

    def to_east(value, halo):
        return jnp.where(row == width - 1, halo, pltpu.roll(value, SUB - 1, 0))

    def to_west(value, halo):
        return jnp.where(row == 0, halo, pltpu.roll(value, 1, 0))

    def to_north(value, halo):
        return jnp.where(lane == lanes - 1, halo, pltpu.roll(value, lanes - 1, 1))

    def to_south(value, halo):
        return jnp.where(lane == 0, halo, pltpu.roll(value, 1, 1))

    def at_north(message, index):
        return pltpu.roll(message, lanes - 1 - index, 1)

    def at_south(message, index):
        return pltpu.roll(message, (lanes - index) % lanes, 1)

    depth = tall(depth_ref[...].astype(jnp.float32))
    d_n = to_north(depth, at_north(north, depth_at))
    d_nn = to_north(d_n, at_north(north, depth_at + 1))
    d_s = to_south(depth, at_south(south, depth_at))
    d_e = to_east(depth, line(east_ref, depth_at))
    d_ee = to_east(d_e, line(east_ref, depth_at + 1))
    d_w = to_west(depth, line(west_ref, depth_at))
    east_line = line(east_ref, depth_at)
    west_line = line(west_ref, depth_at)
    d_ne = to_east(d_n, to_north(east_line, at_north(ne, depth_at)))
    d_se = to_east(d_s, to_south(east_line, at_south(se, depth_at)))
    d_nw = to_west(d_n, to_north(west_line, at_north(nw, depth_at)))
    d_u = jnp.minimum(depth, d_e)
    d_v = jnp.minimum(depth, d_n)
    u_neighbours = [
        jnp.minimum(d_u, d)
        for d in (
            jnp.minimum(d_e, d_ee),
            d_w,
            jnp.minimum(d_n, d_ne),
            jnp.minimum(d_s, d_se),
        )
    ]
    v_neighbours = [
        jnp.minimum(d_v, d)
        for d in (
            jnp.minimum(d_e, d_ne),
            jnp.minimum(d_w, d_nw),
            jnp.minimum(d_n, d_nn),
            d_s,
        )
    ]

    level_row = lax.broadcasted_iota(jnp.int32, (levels, lanes), 0)
    level_lane = lax.broadcasted_iota(jnp.int32, (levels, lanes), 1)
    wet_row = jnp.minimum(
        west_ref[pl.ds(depth_at, 1), :], depth_ref[pl.ds(0, 1), :].astype(jnp.float32)
    )
    wet_face = level_row.astype(jnp.float32) < wet_row
    u_west = west_ref[pl.ds(4 * levels, levels), :]
    for place, field, target in ((0, t_ref, gx_t_ref), (2, s_ref, gx_s_ref)):
        near = west_ref[pl.ds(place * levels, levels), :]
        far = west_ref[pl.ds((place + 1) * levels, levels), :]
        own = field[:, 0, :]
        face = u_west * (1.0 / 12.0) * (7.0 * (near + own) - (far + field[:, 1, :]))
        target[...] = jnp.where(wet_face, face - TRACER_DIFF * (own - near), 0.0)

    def column(corner, place):
        picked = jnp.where(level_lane == place * levels + level_row, corner[0:1], 0.0)
        return jnp.sum(picked, axis=1, keepdims=True)

    u_corner = column(nw, 4)
    v_corner = column(se, 5)
    u2_ref[...] = u_west + jnp.where(
        level_lane == lanes - 1, u_corner, pltpu.roll(u_west, lanes - 1, 1)
    )
    v_east = east_ref[pl.ds(5 * levels, levels), :]
    v2_ref[...] = v_east + jnp.where(level_lane == 0, v_corner, pltpu.roll(v_east, 1, 1))

    v_s_lane = jnp.where(
        lane < levels, at_south(south, 5 * levels), at_south(south, 3 * levels)
    )
    both = south + bottom
    face = v_s_lane * (1.0 / 12.0) * (7.0 * both - at_south(both, levels))
    face = face - TRACER_DIFF * (bottom - south)
    wet_south = jnp.minimum(south[:, depth_at : depth_at + 1], bottom[:, depth_at : depth_at + 1])
    face_south = jnp.where(lax.rem(lane, levels).astype(jnp.float32) < wet_south, face, 0.0)

    row_id = (lat * lanes + lane).astype(jnp.float32)
    total = float(lat_count * lanes)
    cor_u = 2.0 * (row_id + 0.5) / total - 1.0
    cor_v = 2.0 * (row_id + 1.0) / total - 1.0
    inner, last = mixing_constants(levels)
    gain = TIME_STEP * VERTICAL_VISC

    def masked(k, count, value):
        return jnp.where(float(k) < count, value, 0.0)

    px = jnp.zeros((SUB, lanes), jnp.float32)
    py = jnp.zeros((SUB, lanes), jnp.float32)
    above = None
    ratio = None
    values = None
    for k in range(levels):
        u = tall(u_ref[k])
        v = tall(v_ref[k])
        u_face = masked(k, d_u, u * (1.0 / 12.0))
        u_diff = masked(k, d_u, TRACER_DIFF)
        v_face = masked(k, d_v, v * (1.0 / 12.0))
        v_diff = masked(k, d_v, TRACER_DIFF)
        stars = []
        seen = []
        for place, field, gx_ref in ((0, t_ref, gx_t_ref), (2, s_ref, gx_s_ref)):
            near, far = place * levels + k, (place + 1) * levels + k
            c = tall(field[k])
            c_e = to_east(c, line(east_ref, near))
            c_ee = to_east(c_e, line(east_ref, far))
            c_w = to_west(c, line(west_ref, near))
            c_n = to_north(c, at_north(north, near))
            c_nn = to_north(c_n, at_north(north, far))
            c_s = to_south(c, at_south(south, near))
            gx = u_face * (7.0 * (c + c_e) - (c_w + c_ee)) - u_diff * (c_e - c)
            gy = v_face * (7.0 * (c + c_n) - (c_s + c_nn)) - v_diff * (c_n - c)
            gx_w = to_west(gx, line(gx_ref, k))
            gy_s = to_south(gy, at_south(face_south, near))
            stars.append(c - TIME_STEP * masked(k, depth, (gx - gx_w) + (gy - gy_s)))
            seen.append((c, c_e, c_n))
        weights = THERMAL_EXPANSION, HALINE_CONTRACTION
        b, b_e, b_n = (
            masked(k, d, weights[0] * warm - weights[1] * salt)
            for d, warm, salt in zip((depth, d_e, d_n), seen[0], seen[1])
        )
        bx = b_e - b
        by = b_n - b
        px = px + bx
        py = py + by

        u_e = to_east(u, line(east_ref, 4 * levels + k))
        u_w = to_west(u, line(west_ref, 4 * levels + k))
        u_n = to_north(u, at_north(north, 4 * levels + k))
        u_s = to_south(u, at_south(south, 4 * levels + k))
        v_e = to_east(v, line(east_ref, 5 * levels + k))
        v_w = to_west(v, line(west_ref, 5 * levels + k))
        v_n = to_north(v, at_north(north, 5 * levels + k))
        v_s = to_south(v, at_south(south, 5 * levels + k))
        v2 = v + v_s
        u2 = u + u_n
        v_bar = 0.25 * (v2 + to_east(v2, line(v2_ref, k)))
        u_bar = 0.25 * (u2 + to_west(u2, line(u2_ref, k)))
        u_visc = sum(masked(k, d, n - u) for d, n in zip(u_neighbours, (u_e, u_w, u_n, u_s)))
        v_visc = sum(masked(k, d, n - v) for d, n in zip(v_neighbours, (v_e, v_w, v_n, v_s)))
        u_star = u + TIME_STEP * (cor_u * v_bar - (px - 0.5 * bx) + MOMENTUM_VISC * u_visc)
        v_star = v + TIME_STEP * (-cor_v * u_bar - (py - 0.5 * by) + MOMENTUM_VISC * v_visc)
        if k == 0:
            u_star = u_star + TIME_STEP * WIND_GAIN * tall(wind_ref[0])
            v_star = v_star + TIME_STEP * WIND_GAIN * tall(wind_ref[1])

        if k < levels - 1:
            below = masked(k + 1, depth, TIME_STEP * tall(mix_ref[k]))
        else:
            below = None
        pivot = 1.0
        if above is not None:
            pivot = pivot + above * (1.0 - ratio)
        if below is not None:
            pivot = pivot + below
        inverse = 1.0 / pivot

        def momentum_weight(count):
            weight = jnp.where(float(k) < count, last[k], 0.0)
            if k < levels - 1:
                weight = jnp.where(float(k + 1) < count, inner[k], weight)
            return weight

        rights = stars + [u_star, v_star]
        scales = [inverse, inverse, momentum_weight(d_u), momentum_weight(d_v)]
        if k > 0:
            gains = [above, above, gain, gain]
            rights = [right + g * value for right, g, value in zip(rights, gains, values)]
        values = [right * scale for right, scale in zip(rights, scales)]
        for index, value in enumerate(values):
            val_ref[index, k] = value
        if below is not None:
            ratio = below * inverse
            val_ref[4, k] = ratio
        above = below

    outs = (t_out, s_out, u_out, v_out)
    for k in range(levels - 1, -1, -1):
        if k < levels - 1:
            ratios = [val_ref[4, k], val_ref[4, k], gain * inner[k], gain * inner[k]]
            values = [val_ref[i, k] + ratios[i] * values[i] for i in range(4)]
        for out, value in zip(outs, values):
            out[k] = value[:width]


def shards(
    thermal_anomaly,
    saltiness_anomaly,
    zonal_current,
    meridional_current,
    bottom_ocean_layer,
    seam_axis_meridian,
    interface_diffusivity,
    atmospheric_forcing,
):
    levels, width, lanes = thermal_anomaly.shape
    lon_count = lax.axis_size("lon")
    lat_count = lax.axis_size("lat")
    lat = lax.axis_index("lat")
    fields = (thermal_anomaly, saltiness_anomaly, zonal_current, meridional_current)
    f32 = jnp.float32
    row_message = jax.ShapeDtypeStruct((width, lanes), f32)

    top, bottom = pl.pallas_call(
        edge_rows_kernel,
        out_shape=[row_message] * 2,
        in_specs=[VMEM] * 5 + [SMEM],
        out_specs=[VMEM] * 2,
    )(*fields, bottom_ocean_layer, seam_axis_meridian)

    even = lat % 2 == 0
    received = []
    for first in (0, 1):
        pairs = [
            (a, b) for i in range(first, lat_count - 1, 2) for a, b in ((i, i + 1), (i + 1, i))
        ]
        if pairs:
            sends_top = even if first == 0 else jnp.logical_not(even)
            received.append(lax.ppermute(jnp.where(sends_top, top, bottom), "lat", pairs))
        else:
            received.append(jnp.zeros((width, lanes), f32))
    north = jnp.where(even, received[0], received[1])
    south = jnp.where(even, received[1], received[0])

    east_message = jax.ShapeDtypeStruct((6 * levels + 16, lanes), f32)
    west_message = jax.ShapeDtypeStruct((6 * levels + 8, lanes), f32)
    eastward, westward = pl.pallas_call(
        edge_columns_kernel,
        out_shape=[east_message, west_message],
        in_specs=[VMEM] * 7,
        out_specs=[VMEM] * 2,
    )(*fields, bottom_ocean_layer, north, south)

    code = seam_axis_meridian[0]
    tile = lax.rem(code // width, lon_count)
    three = (code % width == width - 1).astype(jnp.int32)

    def exchange(first, count):
        def branch(eastward, westward, top):
            ring = [(i, (i + 1) % lon_count) for i in range(lon_count)]
            from_west = lax.ppermute(eastward, "lon", ring)
            from_east = lax.ppermute(westward, "lon", [(b, a) for a, b in ring])
            mirrored = [
                lax.ppermute(
                    top, "lon", [(i, (first - 1 + d - i) % lon_count) for i in range(lon_count)]
                )
                for d in range(count)
            ]
            mirrored = mirrored + [mirrored[-1]] * (3 - count)
            return (from_west, from_east, *mirrored)

        return branch

    branches = [exchange(first, count) for first in range(lon_count) for count in (2, 3)]
    from_west, from_east, fold_a, fold_b, fold_c = lax.switch(
        tile * 2 + three, branches, eastward, westward, top
    )

    whole = jax.ShapeDtypeStruct((levels, width, lanes), f32)
    return pl.pallas_call(
        step_kernel,
        out_shape=[whole] * 4,
        in_specs=[VMEM] * 5 + [SMEM] + [VMEM] * 10,
        out_specs=[VMEM] * 4,
        scratch_shapes=[
            pltpu.VMEM((max(24, 3 * width), lanes), f32),
            pltpu.VMEM((16, lanes), f32),
        ]
        + [pltpu.VMEM((levels, lanes), f32)] * 4
        + [pltpu.VMEM((5, levels, SUB, lanes), f32)],
    )(
        *fields,
        bottom_ocean_layer,
        seam_axis_meridian,
        interface_diffusivity,
        atmospheric_forcing,
        bottom,
        north,
        south,
        from_west,
        from_east,
        fold_a,
        fold_b,
        fold_c,
    )


def solution(mesh):
    split = P(None, "lon", "lat")
    return jax.shard_map(
        shards,
        mesh=mesh,
        in_specs=(split, split, split, split, P("lon", "lat"), P(), split, split),
        out_specs=(split, split, split, split),
        check_vma=False,
    )
```

```python
import jax
import jax.numpy as jnp
from jax import lax
from jax.experimental import pallas as pl
from jax.experimental.pallas import tpu as pltpu
from jax.sharding import PartitionSpec as P

TIME_STEP = 0.2
TRACER_DIFF = 0.2
MOMENTUM_VISC = 0.2
THERMAL_EXPANSION = 0.5
HALINE_CONTRACTION = 0.4
WIND_GAIN = 2.0
VERTICAL_VISC = 1.0

VMEM = pl.BlockSpec(memory_space=pltpu.VMEM)
SMEM = pl.BlockSpec(memory_space=pltpu.SMEM)
SUB = 8


def lane_of(lanes):
    return lax.broadcasted_iota(jnp.int32, (SUB, lanes), 1)


def row_of(lanes):
    return lax.broadcasted_iota(jnp.int32, (SUB, lanes), 0)


def tall(value):
    missing = SUB - value.shape[0]
    if missing == 0:
        return value
    return jnp.concatenate([value, jnp.zeros((missing, value.shape[1]), value.dtype)], axis=0)


def edges_kernel(t_ref, s_ref, u_ref, v_ref, depth_ref, *outs):
    top_ref, bottom_ref, east_ref, west_ref, first_ref, second_ref = outs
    levels, width, lanes = t_ref.shape
    even = lax.rem(lax.axis_index("lat"), 2) == 0
    lane = lane_of(lanes)
    for message, near, far in ((east_ref, width - 1, width - 2), (west_ref, 0, 1)):
        for place, field, column in (
            (0, t_ref, near),
            (1, t_ref, far),
            (2, s_ref, near),
            (3, s_ref, far),
            (4, u_ref, near),
            (5, v_ref, near),
        ):
            message[pl.ds(place * levels, levels), :] = field[:, column, :]
        depth = depth_ref[...].astype(jnp.float32)
        message[pl.ds(6 * levels, 8), :] = jnp.concatenate(
            [depth[near : near + 1], depth[far : far + 1]] * 4, axis=0
        )

    tops, bottoms = [], []
    for first, second, count in ((t_ref, s_ref, depth_ref), (u_ref, v_ref, None)):
        top = jnp.zeros((SUB, lanes), jnp.float32)
        bottom = jnp.zeros((SUB, lanes), jnp.float32)
        places = [(3 * k, first, k) for k in range(levels)]
        places += [(3 * (levels + k), second, k) for k in range(levels)]
        if count is not None:
            places.append((6 * levels, count, None))
        for start, ref, k in places:
            value = depth_ref[...].astype(jnp.float32) if k is None else ref[k]
            value = tall(value)
            here = jnp.logical_and(lane >= start, lane < start + 3)
            top = jnp.where(here, pltpu.roll(value, start + 3, 1), top)
            bottom = jnp.where(here, pltpu.roll(value, start, 1), bottom)
        bottom = jnp.where(lax.rem(lane, 3) == 2, pltpu.roll(bottom, 2, 1), bottom)
        tops.append(top[:width])
        bottoms.append(bottom[:width])
    for index in range(2):
        rows = pl.ds(index * width, width)
        top_ref[rows, :] = tops[index]
        bottom_ref[rows, :] = bottoms[index]
        first_ref[rows, :] = jnp.where(even, tops[index], bottoms[index])
        second_ref[rows, :] = jnp.where(even, bottoms[index], tops[index])


def corners_kernel(top_ref, base_ref, seam_ref, *refs):
    north_ref, south_ref, west_ref, fold_ref, rest_ref = refs[-5:]
    received = refs[:-5]
    lanes = top_ref.shape[1]
    width = top_ref.shape[0] // 2
    lat = lax.axis_index("lat")
    even = lax.rem(lat, 2) == 0
    first = received[0][...]
    second = received[1][...] if len(received) > 1 else jnp.zeros_like(first)
    north = jnp.where(even, first, second)
    south = jnp.where(even, second, first)
    north_ref[...] = north
    south_ref[...] = south
    base = base_ref.shape[0] - 8
    west_ref[pl.ds(0, base), :] = base_ref[pl.ds(0, base), :]
    west_ref[pl.ds(base, 8), :] = jnp.concatenate(
        [
            base_ref[pl.ds(base, 2), :],
            north[0:1],
            north[width : width + 1],
            south[0:1],
            south[width : width + 1],
            jnp.zeros((2, lanes), jnp.float32),
        ],
        axis=0,
    )
    is_top = lat == lax.axis_size("lat") - 1
    code = seam_ref[0]
    corner = lax.rem(code, 2) == 1
    for index in range(2):
        rows = pl.ds(index * width, width)
        top = tall(top_ref[rows, :])
        mirrored = jnp.where(corner, top, pltpu.roll(top, 1, 1))
        fold_ref[rows, :] = jnp.where(
            is_top, mirrored[:width], north[index * width : (index + 1) * width]
        )
    rest_ref[...] = jnp.full((SUB, lanes), lax.rem(code, width), jnp.int32)


def mixing_constants(levels):
    gain = TIME_STEP * VERTICAL_VISC
    inner, last, ratio = [], [], 0.0
    for k in range(levels):
        above = gain if k > 0 else 0.0
        last.append(1.0 / (1.0 + above + above * ratio))
        pivot = 1.0 + above + gain + above * ratio
        inner.append(1.0 / pivot)
        ratio = -gain / pivot
    return inner, last


def step_kernel(
    t_ref,
    s_ref,
    u_ref,
    v_ref,
    depth_ref,
    mix_ref,
    wind_ref,
    bottom_ref,
    north_ref,
    south_ref,
    rest_ref,
    west_ref,
    east_ref,
    fold_a_ref,
    fold_b_ref,
    fold_c_ref,
    t_out,
    s_out,
    u_out,
    v_out,
    fold_ref,
    mirror_ref,
    gx_t_ref,
    gx_s_ref,
    u2_ref,
    v2_ref,
    val_ref,
    near_north_ref,
    near_south_ref,
    face_south_ref,
):
    levels, width, lanes = t_ref.shape
    lat = lax.axis_index("lat")
    lat_count = lax.axis_size("lat")
    is_top = lat == lat_count - 1
    lane = lane_of(lanes)
    row = row_of(lanes)
    depth_at = 6 * levels
    count_at = 6 * levels + 2

    rest = rest_ref[0, 0]
    for index in range(2):
        for place, ref in enumerate((fold_a_ref, fold_b_ref, fold_c_ref)):
            fold_ref[index, pl.ds(place * width, width), :] = ref[pl.ds(index * width, width), :]
        for i in range(-1, width + 1):
            mirror_ref[index, pl.ds(i + 1, 1), :] = fold_ref[
                index, pl.ds(width + rest - i, 1), :
            ]

    def half(ref, index):
        return tall(ref[pl.ds(index * width, width), :])

    north, north_uv = (
        jnp.where(
            is_top, sign * tall(mirror_ref[index, pl.ds(1, width), :]), half(north_ref, index)
        )
        for index, sign in ((0, 1.0), (1, -1.0))
    )
    south, south_uv = half(south_ref, 0), half(south_ref, 1)
    bottom = half(bottom_ref, 0)

    def line(ref, index):
        return jnp.broadcast_to(ref[pl.ds(index, 1), :], (SUB, lanes))

    def mirror_line(index, i):
        return jnp.broadcast_to(mirror_ref[index, pl.ds(i + 1, 1), :], (SUB, lanes))

    nw = jnp.where(is_top, mirror_line(0, -1), line(fold_b_ref, width - 1))
    nw_uv = jnp.where(is_top, -mirror_line(1, -1), line(fold_b_ref, 2 * width - 1))
    ne = jnp.where(is_top, mirror_line(0, width), line(east_ref, depth_at + 2))
    se = line(east_ref, depth_at + 4)
    se_uv = line(east_ref, depth_at + 5)

    def to_east(value, halo):
        return jnp.where(row == width - 1, halo, pltpu.roll(value, SUB - 1, 0))

    def to_west(value, halo):
        return jnp.where(row == 0, halo, pltpu.roll(value, 1, 0))

    def to_north(value, halo):
        return jnp.where(lane == lanes - 1, halo, pltpu.roll(value, lanes - 1, 1))

    def to_south(value, halo):
        return jnp.where(lane == 0, halo, pltpu.roll(value, 1, 1))

    def at_north(message, index):
        return pltpu.roll(message, lanes - 1 - index, 1)

    def at_south(message, index):
        return pltpu.roll(message, (lanes - index) % lanes, 1)

    depth = tall(depth_ref[...].astype(jnp.float32))
    d_n = to_north(depth, at_north(north, count_at))
    d_nn = to_north(d_n, at_north(north, count_at - 1))
    d_s = to_south(depth, at_south(south, count_at))
    d_e = to_east(depth, line(east_ref, depth_at))
    d_ee = to_east(d_e, line(east_ref, depth_at + 1))
    d_w = to_west(depth, line(west_ref, depth_at))
    east_line = line(east_ref, depth_at)
    west_line = line(west_ref, depth_at)
    d_ne = to_east(d_n, to_north(east_line, at_north(ne, count_at)))
    d_se = to_east(d_s, to_south(east_line, at_south(se, count_at)))
    d_nw = to_west(d_n, to_north(west_line, at_north(nw, count_at)))
    d_u = jnp.minimum(depth, d_e)
    d_v = jnp.minimum(depth, d_n)
    u_neighbours = [
        jnp.minimum(d_u, d)
        for d in (
            jnp.minimum(d_e, d_ee),
            d_w,
            jnp.minimum(d_n, d_ne),
            jnp.minimum(d_s, d_se),
        )
    ]
    v_neighbours = [
        jnp.minimum(d_v, d)
        for d in (
            jnp.minimum(d_e, d_ne),
            jnp.minimum(d_w, d_nw),
            jnp.minimum(d_n, d_nn),
            d_s,
        )
    ]

    level_row = lax.broadcasted_iota(jnp.int32, (levels, lanes), 0)
    level_lane = lax.broadcasted_iota(jnp.int32, (levels, lanes), 1)
    wet_row = jnp.minimum(
        west_ref[pl.ds(depth_at, 1), :], depth_ref[pl.ds(0, 1), :].astype(jnp.float32)
    )
    wet_face = level_row.astype(jnp.float32) < wet_row
    u_west = west_ref[pl.ds(4 * levels, levels), :]
    for place, field, target in ((0, t_ref, gx_t_ref), (2, s_ref, gx_s_ref)):
        near = west_ref[pl.ds(place * levels, levels), :]
        far = west_ref[pl.ds((place + 1) * levels, levels), :]
        own = field[:, 0, :]
        face = u_west * (1.0 / 12.0) * (7.0 * (near + own) - (far + field[:, 1, :]))
        target[...] = jnp.where(wet_face, face - TRACER_DIFF * (own - near), 0.0)

    def column(corner, place):
        picked = jnp.where(level_lane == 3 * (place * levels + level_row) + 2, corner[0:1], 0.0)
        return jnp.sum(picked, axis=1, keepdims=True)

    u_corner = column(nw_uv, 0)
    v_corner = column(se_uv, 1)
    u2_ref[...] = u_west + jnp.where(
        level_lane == lanes - 1, u_corner, pltpu.roll(u_west, lanes - 1, 1)
    )
    v_east = east_ref[pl.ds(5 * levels, levels), :]
    v2_ref[...] = v_east + jnp.where(level_lane == 0, v_corner, pltpu.roll(v_east, 1, 1))

    in_block = jnp.where(lane < 3 * levels, lane, lane - 3 * levels).astype(jnp.float32)
    v_south = jnp.where(lane < 3 * levels, at_south(south_uv, 3 * levels), south_uv)
    both = south + bottom
    face = v_south * (1.0 / 12.0) * (7.0 * both - pltpu.roll(both, 1, 1))
    face = face - TRACER_DIFF * (bottom - south)
    wet_south = jnp.minimum(
        south[:, count_at : count_at + 1], bottom[:, count_at : count_at + 1]
    )
    face_south = jnp.where(in_block < 3.0 * wet_south, face, 0.0)

    for k in range(levels):
        for place, message in ((0, north), (2, north), (4, north_uv), (5, north_uv)):
            spot = 3 * k + 2 + (3 * levels if place in (2, 5) else 0)
            near_north_ref[place * levels + k] = at_north(message, spot)
            if place < 4:
                near_north_ref[(place + 1) * levels + k] = at_north(message, spot - 1)
    for k in range(levels):
        for place, message in ((0, south), (1, south), (2, south_uv), (3, south_uv)):
            spot = 3 * (place % 2 * levels + k) + 2
            near_south_ref[place * levels + k] = at_south(message, spot)
        for place in range(2):
            face_south_ref[place * levels + k] = at_south(
                face_south, 3 * (place * levels + k) + 2
            )

    row_id = (lat * lanes + lane).astype(jnp.float32)
    total = float(lat_count * lanes)
    cor_u = 2.0 * (row_id + 0.5) / total - 1.0
    cor_v = 2.0 * (row_id + 1.0) / total - 1.0
    inner, last = mixing_constants(levels)
    gain = TIME_STEP * VERTICAL_VISC

    def masked(k, count, value):
        return jnp.where(float(k) < count, value, 0.0)

    px = jnp.zeros((SUB, lanes), jnp.float32)
    py = jnp.zeros((SUB, lanes), jnp.float32)
    above = None
    ratio = None
    values = None
    for k in range(levels):
        u = tall(u_ref[k])
        v = tall(v_ref[k])
        u_face = masked(k, d_u, u * (1.0 / 12.0))
        u_diff = masked(k, d_u, TRACER_DIFF)
        v_face = masked(k, d_v, v * (1.0 / 12.0))
        v_diff = masked(k, d_v, TRACER_DIFF)
        stars = []
        seen = []
        for place, field, gx_ref in ((0, t_ref, gx_t_ref), (2, s_ref, gx_s_ref)):
            near, far = place * levels + k, (place + 1) * levels + k
            c = tall(field[k])
            c_e = to_east(c, line(east_ref, near))
            c_ee = to_east(c_e, line(east_ref, far))
            c_w = to_west(c, line(west_ref, near))
            c_n = to_north(c, near_north_ref[near])
            c_nn = to_north(c_n, near_north_ref[far])
            c_s = to_south(c, near_south_ref[place // 2 * levels + k])
            gx = u_face * (7.0 * (c + c_e) - (c_w + c_ee)) - u_diff * (c_e - c)
            gy = v_face * (7.0 * (c + c_n) - (c_s + c_nn)) - v_diff * (c_n - c)
            gx_w = to_west(gx, line(gx_ref, k))
            gy_s = to_south(gy, face_south_ref[place // 2 * levels + k])
            stars.append(c - TIME_STEP * masked(k, depth, (gx - gx_w) + (gy - gy_s)))
            seen.append((c, c_e, c_n))
        weights = THERMAL_EXPANSION, HALINE_CONTRACTION
        b, b_e, b_n = (
            masked(k, d, weights[0] * warm - weights[1] * salt)
            for d, warm, salt in zip((depth, d_e, d_n), seen[0], seen[1])
        )
        bx = b_e - b
        by = b_n - b
        px = px + bx
        py = py + by

        u_e = to_east(u, line(east_ref, 4 * levels + k))
        u_w = to_west(u, line(west_ref, 4 * levels + k))
        u_n = to_north(u, near_north_ref[4 * levels + k])
        u_s = to_south(u, near_south_ref[2 * levels + k])
        v_e = to_east(v, line(east_ref, 5 * levels + k))
        v_w = to_west(v, line(west_ref, 5 * levels + k))
        v_n = to_north(v, near_north_ref[5 * levels + k])
        v_s = to_south(v, near_south_ref[3 * levels + k])
        v2 = v + v_s
        u2 = u + u_n
        v_bar = 0.25 * (v2 + to_east(v2, line(v2_ref, k)))
        u_bar = 0.25 * (u2 + to_west(u2, line(u2_ref, k)))
        u_visc = sum(masked(k, d, n - u) for d, n in zip(u_neighbours, (u_e, u_w, u_n, u_s)))
        v_visc = sum(masked(k, d, n - v) for d, n in zip(v_neighbours, (v_e, v_w, v_n, v_s)))
        u_star = u + TIME_STEP * (cor_u * v_bar - (px - 0.5 * bx) + MOMENTUM_VISC * u_visc)
        v_star = v + TIME_STEP * (-cor_v * u_bar - (py - 0.5 * by) + MOMENTUM_VISC * v_visc)
        if k == 0:
            u_star = u_star + TIME_STEP * WIND_GAIN * tall(wind_ref[0])
            v_star = v_star + TIME_STEP * WIND_GAIN * tall(wind_ref[1])

        if k < levels - 1:
            below = masked(k + 1, depth, TIME_STEP * tall(mix_ref[k]))
        else:
            below = None
        pivot = 1.0
        if above is not None:
            pivot = pivot + above * (1.0 - ratio)
        if below is not None:
            pivot = pivot + below
        inverse = 1.0 / pivot

        def momentum_weight(count):
            weight = jnp.where(float(k) < count, last[k], 0.0)
            if k < levels - 1:
                weight = jnp.where(float(k + 1) < count, inner[k], weight)
            return weight

        rights = stars + [u_star, v_star]
        scales = [inverse, inverse, momentum_weight(d_u), momentum_weight(d_v)]
        if k > 0:
            gains = [above, above, gain, gain]
            rights = [right + g * value for right, g, value in zip(rights, gains, values)]
        values = [right * scale for right, scale in zip(rights, scales)]
        for index, value in enumerate(values):
            val_ref[index, k] = value
        if below is not None:
            ratio = below * inverse
            val_ref[4, k] = ratio
        above = below

    outs = (t_out, s_out, u_out, v_out)
    for k in range(levels - 1, -1, -1):
        if k < levels - 1:
            ratios = [val_ref[4, k], val_ref[4, k], gain * inner[k], gain * inner[k]]
            values = [val_ref[i, k] + ratios[i] * values[i] for i in range(4)]
        for out, value in zip(outs, values):
            out[k] = value[:width]


def shards(
    thermal_anomaly,
    saltiness_anomaly,
    zonal_current,
    meridional_current,
    bottom_ocean_layer,
    seam_axis_meridian,
    interface_diffusivity,
    atmospheric_forcing,
):
    levels, width, lanes = thermal_anomaly.shape
    lon_count = lax.axis_size("lon")
    lat_count = lax.axis_size("lat")
    fields = (thermal_anomaly, saltiness_anomaly, zonal_current, meridional_current)
    f32 = jnp.float32
    row_message = jax.ShapeDtypeStruct((2 * width, lanes), f32)
    column_message = jax.ShapeDtypeStruct((6 * levels + 8, lanes), f32)

    top, bottom, eastward, westward, first, second = pl.pallas_call(
        edges_kernel,
        out_shape=[row_message] * 2 + [column_message] * 2 + [row_message] * 2,
        in_specs=[VMEM] * 5,
        out_specs=[VMEM] * 6,
    )(*fields, bottom_ocean_layer)

    received = []
    for start, message in ((0, first), (1, second)):
        pairs = [
            (a, b) for i in range(start, lat_count - 1, 2) for a, b in ((i, i + 1), (i + 1, i))
        ]
        if pairs:
            received.append(lax.ppermute(message, "lat", pairs))

    north, south, westward, fold, rest = pl.pallas_call(
        corners_kernel,
        out_shape=[row_message] * 2
        + [column_message, row_message, jax.ShapeDtypeStruct((SUB, lanes), jnp.int32)],
        in_specs=[VMEM] * 2 + [SMEM] + [VMEM] * len(received),
        out_specs=[VMEM] * 5,
    )(top, westward, seam_axis_meridian, *received)

    code = seam_axis_meridian[0]
    tile = lax.rem(lax.div(code, width), lon_count)
    three = (lax.rem(code, width) == width - 1).astype(jnp.int32)
    ring = [(i, (i + 1) % lon_count) for i in range(lon_count)]
    stay = [(i, i) for i in range(lon_count)]
    last_row = lat_count - 1

    def over_both(mirror, others):
        return [
            (a * lat_count + row, b * lat_count + row)
            for row in range(lat_count)
            for a, b in (mirror if row == last_row else others)
        ]

    def exchange(first, count):
        mirrors = [
            [(i, (first - 1 + d - i) % lon_count) for i in range(lon_count)] for d in range(3)
        ]

        def branch(eastward, westward, fold):
            both = ("lon", "lat")
            return (
                lax.ppermute(eastward, "lon", ring),
                lax.ppermute(westward, "lon", [(b, a) for a, b in ring]),
                lax.ppermute(fold, both, over_both(mirrors[0], stay)),
                lax.ppermute(fold, both, over_both(mirrors[1], ring)),
                lax.ppermute(fold, both, over_both(mirrors[2] if count == 3 else stay, stay)),
            )

        return branch

    branches = [exchange(first, count) for first in range(lon_count) for count in (2, 3)]
    from_west, from_east, fold_a, fold_b, fold_c = lax.switch(
        tile * 2 + three, branches, eastward, westward, fold
    )

    whole = jax.ShapeDtypeStruct((levels, width, lanes), f32)
    return pl.pallas_call(
        step_kernel,
        out_shape=[whole] * 4,
        in_specs=[VMEM] * 16,
        out_specs=[VMEM] * 4,
        scratch_shapes=[
            pltpu.VMEM((2, max(24, 3 * width), lanes), f32),
            pltpu.VMEM((2, 16, lanes), f32),
        ]
        + [pltpu.VMEM((levels, lanes), f32)] * 4
        + [pltpu.VMEM((5, levels, SUB, lanes), f32)]
        + [pltpu.VMEM((count * levels, SUB, lanes), f32) for count in (6, 4, 2)],
    )(
        *fields,
        bottom_ocean_layer,
        interface_diffusivity,
        atmospheric_forcing,
        bottom,
        north,
        south,
        rest,
        from_west,
        from_east,
        fold_a,
        fold_b,
        fold_c,
    )


def solution(mesh):
    split = P(None, "lon", "lat")
    return jax.shard_map(
        shards,
        mesh=mesh,
        in_specs=(split, split, split, split, P("lon", "lat"), P(), split, split),
        out_specs=(split, split, split, split),
        check_vma=False,
    )
```

```python
import jax
import jax.numpy as jnp
from jax import lax
from jax.experimental import pallas as pl
from jax.experimental.pallas import tpu as pltpu
from jax.sharding import PartitionSpec as P

TIME_STEP = 0.2
TRACER_DIFF = 0.2
MOMENTUM_VISC = 0.2
THERMAL_EXPANSION = 0.5
HALINE_CONTRACTION = 0.4
WIND_GAIN = 2.0
VERTICAL_VISC = 1.0

VMEM = pl.BlockSpec(memory_space=pltpu.VMEM)
SMEM = pl.BlockSpec(memory_space=pltpu.SMEM)
SUB = 8
CORNER = 12
SMALL = pltpu.CompilerParams(vmem_limit_bytes=4 * 2**20)
FIRST = pltpu.CompilerParams(vmem_limit_bytes=4 * 2**20)
LARGE = pltpu.CompilerParams(vmem_limit_bytes=8 * 2**20)


def lane_of(lanes):
    return lax.broadcasted_iota(jnp.int32, (SUB, lanes), 1)


def row_of(lanes):
    return lax.broadcasted_iota(jnp.int32, (SUB, lanes), 0)


def tall(value):
    missing = SUB - value.shape[0]
    if missing == 0:
        return value
    return jnp.concatenate([value, jnp.zeros((missing, value.shape[1]), value.dtype)], axis=0)


def edges_kernel(t_ref, s_ref, u_ref, v_ref, depth_ref, stress_ref, *outs):
    top_ref, bottom_ref, east_ref, west_ref, first_ref, second_ref, count_ref, wind_ref = outs
    levels, width, lanes = t_ref.shape
    count_ref[...] = depth_ref[...].astype(jnp.float32)
    wind_ref[...] = stress_ref[...]
    even = lax.rem(lax.axis_index("lat"), 2) == 0
    lane = lane_of(lanes)
    for message, near, far in ((east_ref, width - 1, width - 2), (west_ref, 0, 1)):
        for place, field, column in (
            (0, t_ref, near),
            (1, t_ref, far),
            (2, s_ref, near),
            (3, s_ref, far),
            (4, u_ref, near),
            (5, v_ref, near),
        ):
            message[pl.ds(place * levels, levels), :] = field[:, column, :]
        depth = depth_ref[...].astype(jnp.float32)
        message[pl.ds(6 * levels, 8), :] = jnp.concatenate(
            [depth[near : near + 1], depth[far : far + 1]] * 4, axis=0
        )

    tops, bottoms = [], []
    for first, second, count in ((t_ref, s_ref, depth_ref), (u_ref, v_ref, None)):
        top = jnp.zeros((SUB, lanes), jnp.float32)
        bottom = jnp.zeros((SUB, lanes), jnp.float32)
        places = [(3 * k, first, k) for k in range(levels)]
        places += [(3 * (levels + k), second, k) for k in range(levels)]
        if count is not None:
            places.append((6 * levels, count, None))
        for start, ref, k in places:
            value = depth_ref[...].astype(jnp.float32) if k is None else ref[k]
            value = tall(value)
            here = jnp.logical_and(lane >= start, lane < start + 3)
            top = jnp.where(here, pltpu.roll(value, start + 3, 1), top)
            bottom = jnp.where(here, pltpu.roll(value, start, 1), bottom)
        bottom = jnp.where(lax.rem(lane, 3) == 2, pltpu.roll(bottom, 2, 1), bottom)
        tops.append(top[:width])
        bottoms.append(bottom[:width])
    for index in range(2):
        rows = pl.ds(index * width, width)
        top_ref[rows, :] = tops[index]
        bottom_ref[rows, :] = bottoms[index]
        first_ref[rows, :] = jnp.where(even, tops[index], bottoms[index])
        second_ref[rows, :] = jnp.where(even, bottoms[index], tops[index])


def corners_kernel(top_ref, base_ref, seam_ref, *refs):
    north_ref, south_ref, west_ref, fold_ref, rest_ref = refs[-5:]
    received = refs[:-5]
    lanes = top_ref.shape[1]
    width = top_ref.shape[0] // 2
    lat = lax.axis_index("lat")
    even = lax.rem(lat, 2) == 0
    first = received[0][...]
    second = received[1][...] if len(received) > 1 else jnp.zeros_like(first)
    north = jnp.where(even, first, second)
    south = jnp.where(even, second, first)
    north_ref[...] = north
    south_ref[...] = south
    base = base_ref.shape[0] - 8
    west_ref[pl.ds(0, base), :] = base_ref[pl.ds(0, base), :]
    west_ref[pl.ds(base, 8), :] = jnp.concatenate(
        [
            base_ref[pl.ds(base, 2), :],
            north[0:1],
            north[width : width + 1],
            south[0:1],
            south[width : width + 1],
            jnp.zeros((2, lanes), jnp.float32),
        ],
        axis=0,
    )
    is_top = lat == lax.axis_size("lat") - 1
    code = seam_ref[0]
    corner = lax.rem(code, 2) == 1
    for index in range(2):
        rows = pl.ds(index * width, width)
        top = tall(top_ref[rows, :])
        mirrored = jnp.where(corner, top, pltpu.roll(top, 1, 1))
        fold_ref[rows, :] = jnp.where(
            is_top, mirrored[:width], north[index * width : (index + 1) * width]
        )
    rest_ref[...] = jnp.full((SUB, lanes), lax.rem(code, width), jnp.int32)


def mixing_constants(levels):
    gain = TIME_STEP * VERTICAL_VISC
    inner, last, ratio = [], [], 0.0
    for k in range(levels):
        above = gain if k > 0 else 0.0
        last.append(1.0 / (1.0 + above + above * ratio))
        pivot = 1.0 + above + gain + above * ratio
        inner.append(1.0 / pivot)
        ratio = -gain / pivot
    return inner, last


def keep_kernel(message_ref, kept_ref):
    kept_ref[...] = message_ref[...]


def mirror_kernel(second_ref, first_ref, rest_ref, mirror_ref, tiles_ref):
    width = tiles_ref.shape[1] // 3
    rest = rest_ref[0, 0]
    for index in range(2):
        for place, ref in enumerate((first_ref, second_ref, first_ref)):
            tiles_ref[index, pl.ds(place * width, width), :] = ref[pl.ds(index * width, width), :]
        for i in range(-1, width + 1):
            mirror_ref[index, pl.ds(i + 1, 1), :] = tiles_ref[
                index, pl.ds(width + rest - i, 1), :
            ]
        mirror_ref[index, pl.ds(CORNER, 1), :] = second_ref[pl.ds((index + 1) * width - 1, 1), :]


def step_kernel(
    t_ref,
    s_ref,
    u_ref,
    v_ref,
    depth_ref,
    mix_ref,
    wind_ref,
    bottom_ref,
    north_ref,
    south_ref,
    west_ref,
    east_ref,
    mirror_ref,
    t_out,
    s_out,
    u_out,
    v_out,
    gx_t_ref,
    gx_s_ref,
    u2_ref,
    v2_ref,
    val_ref,
    near_north_ref,
    near_south_ref,
    face_south_ref,
):
    levels, width, lanes = t_ref.shape
    lat = lax.axis_index("lat")
    lat_count = lax.axis_size("lat")
    is_top = lat == lat_count - 1
    lane = lane_of(lanes)
    row = row_of(lanes)
    depth_at = 6 * levels
    count_at = 6 * levels + 2

    def half(ref, index):
        return tall(ref[pl.ds(index * width, width), :])

    north, north_uv = (
        jnp.where(
            is_top, sign * tall(mirror_ref[index, pl.ds(1, width), :]), half(north_ref, index)
        )
        for index, sign in ((0, 1.0), (1, -1.0))
    )
    south, south_uv = half(south_ref, 0), half(south_ref, 1)
    bottom = half(bottom_ref, 0)

    def line(ref, index):
        return jnp.broadcast_to(ref[pl.ds(index, 1), :], (SUB, lanes))

    def mirror_line(index, i):
        return jnp.broadcast_to(mirror_ref[index, pl.ds(i + 1, 1), :], (SUB, lanes))

    nw = jnp.where(is_top, mirror_line(0, -1), mirror_line(0, CORNER - 1))
    nw_uv = jnp.where(is_top, -mirror_line(1, -1), mirror_line(1, CORNER - 1))
    ne = jnp.where(is_top, mirror_line(0, width), line(east_ref, depth_at + 2))
    se = line(east_ref, depth_at + 4)
    se_uv = line(east_ref, depth_at + 5)

    def to_east(value, halo):
        return jnp.where(row == width - 1, halo, pltpu.roll(value, SUB - 1, 0))

    def to_west(value, halo):
        return jnp.where(row == 0, halo, pltpu.roll(value, 1, 0))

    def to_north(value, halo):
        return jnp.where(lane == lanes - 1, halo, pltpu.roll(value, lanes - 1, 1))

    def to_south(value, halo):
        return jnp.where(lane == 0, halo, pltpu.roll(value, 1, 1))

    def at_north(message, index):
        return pltpu.roll(message, lanes - 1 - index, 1)

    def at_south(message, index):
        return pltpu.roll(message, (lanes - index) % lanes, 1)

    depth = tall(depth_ref[...])
    d_n = to_north(depth, at_north(north, count_at))
    d_nn = to_north(d_n, at_north(north, count_at - 1))
    d_s = to_south(depth, at_south(south, count_at))
    d_e = to_east(depth, line(east_ref, depth_at))
    d_ee = to_east(d_e, line(east_ref, depth_at + 1))
    d_w = to_west(depth, line(west_ref, depth_at))
    east_line = line(east_ref, depth_at)
    west_line = line(west_ref, depth_at)
    d_ne = to_east(d_n, to_north(east_line, at_north(ne, count_at)))
    d_se = to_east(d_s, to_south(east_line, at_south(se, count_at)))
    d_nw = to_west(d_n, to_north(west_line, at_north(nw, count_at)))
    d_u = jnp.minimum(depth, d_e)
    d_v = jnp.minimum(depth, d_n)
    u_neighbours = [
        jnp.minimum(d_u, d)
        for d in (
            jnp.minimum(d_e, d_ee),
            d_w,
            jnp.minimum(d_n, d_ne),
            jnp.minimum(d_s, d_se),
        )
    ]
    v_neighbours = [
        jnp.minimum(d_v, d)
        for d in (
            jnp.minimum(d_e, d_ne),
            jnp.minimum(d_w, d_nw),
            jnp.minimum(d_n, d_nn),
            d_s,
        )
    ]

    level_row = lax.broadcasted_iota(jnp.int32, (levels, lanes), 0)
    level_lane = lax.broadcasted_iota(jnp.int32, (levels, lanes), 1)
    wet_row = jnp.minimum(
        west_ref[pl.ds(depth_at, 1), :], depth_ref[pl.ds(0, 1), :]
    )
    wet_face = level_row.astype(jnp.float32) < wet_row
    u_west = west_ref[pl.ds(4 * levels, levels), :]
    for place, field, target in ((0, t_ref, gx_t_ref), (2, s_ref, gx_s_ref)):
        near = west_ref[pl.ds(place * levels, levels), :]
        far = west_ref[pl.ds((place + 1) * levels, levels), :]
        own = field[:, 0, :]
        face = u_west * (1.0 / 12.0) * (7.0 * (near + own) - (far + field[:, 1, :]))
        target[...] = jnp.where(wet_face, face - TRACER_DIFF * (own - near), 0.0)

    def column(corner, place):
        picked = jnp.where(level_lane == 3 * (place * levels + level_row) + 2, corner[0:1], 0.0)
        return jnp.sum(picked, axis=1, keepdims=True)

    u_corner = column(nw_uv, 0)
    v_corner = column(se_uv, 1)
    u2_ref[...] = u_west + jnp.where(
        level_lane == lanes - 1, u_corner, pltpu.roll(u_west, lanes - 1, 1)
    )
    v_east = east_ref[pl.ds(5 * levels, levels), :]
    v2_ref[...] = v_east + jnp.where(level_lane == 0, v_corner, pltpu.roll(v_east, 1, 1))

    in_block = jnp.where(lane < 3 * levels, lane, lane - 3 * levels).astype(jnp.float32)
    v_south = jnp.where(lane < 3 * levels, at_south(south_uv, 3 * levels), south_uv)
    both = south + bottom
    face = v_south * (1.0 / 12.0) * (7.0 * both - pltpu.roll(both, 1, 1))
    face = face - TRACER_DIFF * (bottom - south)
    wet_south = jnp.minimum(
        south[:, count_at : count_at + 1], bottom[:, count_at : count_at + 1]
    )
    face_south = jnp.where(in_block < 3.0 * wet_south, face, 0.0)

    for k in range(levels):
        for place, message in ((0, north), (2, north), (4, north_uv), (5, north_uv)):
            spot = 3 * k + 2 + (3 * levels if place in (2, 5) else 0)
            near_north_ref[place * levels + k] = at_north(message, spot)
            if place < 4:
                near_north_ref[(place + 1) * levels + k] = at_north(message, spot - 1)
    for k in range(levels):
        for place, message in ((0, south), (1, south), (2, south_uv), (3, south_uv)):
            spot = 3 * (place % 2 * levels + k) + 2
            near_south_ref[place * levels + k] = at_south(message, spot)
        for place in range(2):
            face_south_ref[place * levels + k] = at_south(
                face_south, 3 * (place * levels + k) + 2
            )

    row_id = (lat * lanes + lane).astype(jnp.float32)
    total = float(lat_count * lanes)
    cor_u = 2.0 * (row_id + 0.5) / total - 1.0
    cor_v = 2.0 * (row_id + 1.0) / total - 1.0
    inner, last = mixing_constants(levels)
    gain = TIME_STEP * VERTICAL_VISC

    def masked(k, count, value):
        return jnp.where(float(k) < count, value, 0.0)

    px = jnp.zeros((SUB, lanes), jnp.float32)
    py = jnp.zeros((SUB, lanes), jnp.float32)
    above = None
    ratio = None
    values = None
    for k in range(levels):
        u = tall(u_ref[k])
        v = tall(v_ref[k])
        u_face = masked(k, d_u, u * (1.0 / 12.0))
        u_diff = masked(k, d_u, TRACER_DIFF)
        v_face = masked(k, d_v, v * (1.0 / 12.0))
        v_diff = masked(k, d_v, TRACER_DIFF)
        stars = []
        seen = []
        for place, field, gx_ref in ((0, t_ref, gx_t_ref), (2, s_ref, gx_s_ref)):
            near, far = place * levels + k, (place + 1) * levels + k
            c = tall(field[k])
            c_e = to_east(c, line(east_ref, near))
            c_ee = to_east(c_e, line(east_ref, far))
            c_w = to_west(c, line(west_ref, near))
            c_n = to_north(c, near_north_ref[near])
            c_nn = to_north(c_n, near_north_ref[far])
            c_s = to_south(c, near_south_ref[place // 2 * levels + k])
            gx = u_face * (7.0 * (c + c_e) - (c_w + c_ee)) - u_diff * (c_e - c)
            gy = v_face * (7.0 * (c + c_n) - (c_s + c_nn)) - v_diff * (c_n - c)
            gx_w = to_west(gx, line(gx_ref, k))
            gy_s = to_south(gy, face_south_ref[place // 2 * levels + k])
            stars.append(c - TIME_STEP * masked(k, depth, (gx - gx_w) + (gy - gy_s)))
            seen.append((c, c_e, c_n))
        weights = THERMAL_EXPANSION, HALINE_CONTRACTION
        b, b_e, b_n = (
            masked(k, d, weights[0] * warm - weights[1] * salt)
            for d, warm, salt in zip((depth, d_e, d_n), seen[0], seen[1])
        )
        bx = b_e - b
        by = b_n - b
        px = px + bx
        py = py + by

        u_e = to_east(u, line(east_ref, 4 * levels + k))
        u_w = to_west(u, line(west_ref, 4 * levels + k))
        u_n = to_north(u, near_north_ref[4 * levels + k])
        u_s = to_south(u, near_south_ref[2 * levels + k])
        v_e = to_east(v, line(east_ref, 5 * levels + k))
        v_w = to_west(v, line(west_ref, 5 * levels + k))
        v_n = to_north(v, near_north_ref[5 * levels + k])
        v_s = to_south(v, near_south_ref[3 * levels + k])
        v2 = v + v_s
        u2 = u + u_n
        v_bar = 0.25 * (v2 + to_east(v2, line(v2_ref, k)))
        u_bar = 0.25 * (u2 + to_west(u2, line(u2_ref, k)))
        u_visc = sum(masked(k, d, n - u) for d, n in zip(u_neighbours, (u_e, u_w, u_n, u_s)))
        v_visc = sum(masked(k, d, n - v) for d, n in zip(v_neighbours, (v_e, v_w, v_n, v_s)))
        u_star = u + TIME_STEP * (cor_u * v_bar - (px - 0.5 * bx) + MOMENTUM_VISC * u_visc)
        v_star = v + TIME_STEP * (-cor_v * u_bar - (py - 0.5 * by) + MOMENTUM_VISC * v_visc)
        if k == 0:
            u_star = u_star + TIME_STEP * WIND_GAIN * tall(wind_ref[0])
            v_star = v_star + TIME_STEP * WIND_GAIN * tall(wind_ref[1])

        if k < levels - 1:
            below = masked(k + 1, depth, TIME_STEP * tall(mix_ref[k]))
        else:
            below = None
        pivot = 1.0
        if above is not None:
            pivot = pivot + above * (1.0 - ratio)
        if below is not None:
            pivot = pivot + below
        inverse = 1.0 / pivot

        def momentum_weight(count):
            weight = jnp.where(float(k) < count, last[k], 0.0)
            if k < levels - 1:
                weight = jnp.where(float(k + 1) < count, inner[k], weight)
            return weight

        rights = stars + [u_star, v_star]
        scales = [inverse, inverse, momentum_weight(d_u), momentum_weight(d_v)]
        if k > 0:
            gains = [above, above, gain, gain]
            rights = [right + g * value for right, g, value in zip(rights, gains, values)]
        values = [right * scale for right, scale in zip(rights, scales)]
        for index, value in enumerate(values):
            val_ref[index, k] = value
        if below is not None:
            ratio = below * inverse
            val_ref[4, k] = ratio
        above = below

    outs = (t_out, s_out, u_out, v_out)
    for k in range(levels - 1, -1, -1):
        if k < levels - 1:
            ratios = [val_ref[4, k], val_ref[4, k], gain * inner[k], gain * inner[k]]
            values = [val_ref[i, k] + ratios[i] * values[i] for i in range(4)]
        for out, value in zip(outs, values):
            out[k] = value[:width]


def shards(
    thermal_anomaly,
    saltiness_anomaly,
    zonal_current,
    meridional_current,
    bottom_ocean_layer,
    seam_axis_meridian,
    interface_diffusivity,
    atmospheric_forcing,
):
    levels, width, lanes = thermal_anomaly.shape
    lon_count = lax.axis_size("lon")
    lat_count = lax.axis_size("lat")
    fields = (thermal_anomaly, saltiness_anomaly, zonal_current, meridional_current)
    wind = atmospheric_forcing
    f32 = jnp.float32
    row_message = jax.ShapeDtypeStruct((2 * width, lanes), f32)
    column_message = jax.ShapeDtypeStruct((6 * levels + 8, lanes), f32)

    fold_message = jax.ShapeDtypeStruct((6 * levels + 16, lanes), f32)
    top, bottom, eastward, westward, first, second, counts, stress = pl.pallas_call(
        edges_kernel,
        out_shape=[row_message] * 2
        + [column_message] * 2
        + [row_message] * 2
        + [jax.ShapeDtypeStruct((width, lanes), f32), jax.ShapeDtypeStruct(wind.shape, f32)],
        in_specs=[VMEM] * 6,
        out_specs=[VMEM] * 8,
        compiler_params=FIRST,
    )(*[pltpu.with_memory_space_constraint(x, pltpu.HBM) for x in (*fields, bottom_ocean_layer, wind)])

    from_west = lax.ppermute(eastward, "lon", [(i, (i + 1) % lon_count) for i in range(lon_count)])

    received = []
    for start, message in ((0, first), (1, second)):
        pairs = [
            (a, b) for i in range(start, lat_count - 1, 2) for a, b in ((i, i + 1), (i + 1, i))
        ]
        if pairs:
            received.append(lax.ppermute(message, "lat", pairs))

    north, south, westward, fold, rest = pl.pallas_call(
        corners_kernel,
        out_shape=[row_message] * 2
        + [column_message, fold_message, jax.ShapeDtypeStruct((SUB, lanes), jnp.int32)],
        in_specs=[VMEM] * 2 + [SMEM] + [VMEM] * len(received),
        out_specs=[VMEM] * 5,
        compiler_params=SMALL,
    )(top, westward, seam_axis_meridian, *received)

    code = seam_axis_meridian[0]
    tile = lax.rem(lax.div(code, width), lon_count)
    three = (lax.rem(code, width) == width - 1).astype(jnp.int32)
    stay = [(i, i) for i in range(lon_count)]
    ring = [(i, (i + 1) % lon_count) for i in range(lon_count)]
    last_row = lat_count - 1

    def over_both(mirror, others):
        return [
            (a * lat_count + row, b * lat_count + row)
            for row in range(lat_count)
            for a, b in (mirror if row == last_row else others)
        ]

    def exchange(first, count):
        mirrors = [
            [(i, (first - 1 + d - i) % lon_count) for i in range(lon_count)] for d in range(3)
        ]

        def branch(westward, fold, rest):
            both = ("lon", "lat")
            mirrored = [
                lax.ppermute(fold, both, over_both(mirrors[d], ring if d == 1 else stay))
                for d in range(count)
            ]
            if count == 3:
                last = lax.broadcasted_iota(jnp.int32, fold.shape, 0) % width == width - 1
                mirrored[0] = jnp.where(last, mirrored[0], mirrored[2])
            return (
                keep(lax.ppermute(westward, "lon", [(b, a) for a, b in ring])),
                mirror(mirrored[1], mirrored[0], rest),
            )

        return branch

    mirror = pl.pallas_call(
        mirror_kernel,
        out_shape=jax.ShapeDtypeStruct((2, 16, lanes), f32),
        in_specs=[VMEM] * 3,
        out_specs=VMEM,
        scratch_shapes=[pltpu.VMEM((2, 3 * width, lanes), f32)],
        compiler_params=SMALL,
        cost_estimate=pl.CostEstimate(flops=0, bytes_accessed=2**28, transcendentals=0),
    )

    keep = pl.pallas_call(
        keep_kernel,
        out_shape=column_message,
        in_specs=[VMEM],
        out_specs=VMEM,
        compiler_params=SMALL,
    )

    branches = [exchange(first, count) for first in range(lon_count) for count in (2, 3)]
    from_east, mirrored = lax.switch(
        tile * 2 + three, branches, westward, fold, rest
    )

    whole = jax.ShapeDtypeStruct((levels, width, lanes), f32)
    return pl.pallas_call(
        step_kernel,
        out_shape=[whole] * 4,
        in_specs=[VMEM] * 13,
        out_specs=[VMEM] * 4,
        compiler_params=LARGE,
        scratch_shapes=[pltpu.VMEM((levels, lanes), f32)] * 4
        + [pltpu.VMEM((5, levels, SUB, lanes), f32)]
        + [pltpu.VMEM((count * levels, SUB, lanes), f32) for count in (6, 4, 2)],
    )(
        *fields,
        counts,
        interface_diffusivity,
        stress,
        bottom,
        north,
        south,
        from_west,
        from_east,
        mirrored,
    )


def solution(mesh):
    split = P(None, "lon", "lat")
    return jax.shard_map(
        shards,
        mesh=mesh,
        in_specs=(split, split, split, split, P("lon", "lat"), P(), split, split),
        out_specs=(split, split, split, split),
        check_vma=False,
    )
```

```python
import functools

import jax
import jax.numpy as jnp
from jax import lax
from jax.experimental import pallas as pl
from jax.experimental.pallas import tpu as pltpu
from jax.sharding import PartitionSpec as P

TIME_STEP = 0.2
TRACER_DIFF = 0.2
MOMENTUM_VISC = 0.2
THERMAL_EXPANSION = 0.5
HALINE_CONTRACTION = 0.4
WIND_GAIN = 2.0
VERTICAL_VISC = 1.0

VMEM = pl.BlockSpec(memory_space=pltpu.VMEM)
SMEM = pl.BlockSpec(memory_space=pltpu.SMEM)
SUB = 8
SMALL = pltpu.CompilerParams(vmem_limit_bytes=4 * 2**20)
FIRST = pltpu.CompilerParams(vmem_limit_bytes=4 * 2**20)
LARGE = pltpu.CompilerParams(vmem_limit_bytes=8 * 2**20)


def lane_of(lanes):
    return lax.broadcasted_iota(jnp.int32, (SUB, lanes), 1)


def row_of(lanes):
    return lax.broadcasted_iota(jnp.int32, (SUB, lanes), 0)


def tall(value):
    missing = SUB - value.shape[0]
    if missing == 0:
        return value
    return jnp.concatenate([value, jnp.zeros((missing, value.shape[1]), value.dtype)], axis=0)


def edges_kernel(t_ref, s_ref, u_ref, v_ref, depth_ref, stress_ref, *outs):
    top_ref, bottom_ref, east_ref, west_ref, first_ref, second_ref, count_ref, wind_ref = outs
    levels, width, lanes = t_ref.shape
    count_ref[...] = depth_ref[...].astype(jnp.float32)
    wind_ref[...] = stress_ref[...]
    even = lax.rem(lax.axis_index("lat"), 2) == 0
    lane = lane_of(lanes)
    for message, near, far in ((east_ref, width - 1, width - 2), (west_ref, 0, 1)):
        for place, field, column in (
            (0, t_ref, near),
            (1, t_ref, far),
            (2, s_ref, near),
            (3, s_ref, far),
            (4, u_ref, near),
            (5, v_ref, near),
        ):
            message[pl.ds(place * levels, levels), :] = field[:, column, :]
        depth = depth_ref[...].astype(jnp.float32)
        message[pl.ds(6 * levels, 8), :] = jnp.concatenate(
            [depth[near : near + 1], depth[far : far + 1]] * 4, axis=0
        )

    tops, bottoms = [], []
    for first, second, count in ((t_ref, s_ref, depth_ref), (u_ref, v_ref, None)):
        top = jnp.zeros((SUB, lanes), jnp.float32)
        bottom = jnp.zeros((SUB, lanes), jnp.float32)
        places = [(3 * k, first, k) for k in range(levels)]
        places += [(3 * (levels + k), second, k) for k in range(levels)]
        if count is not None:
            places.append((6 * levels, count, None))
        for start, ref, k in places:
            value = depth_ref[...].astype(jnp.float32) if k is None else ref[k]
            value = tall(value)
            here = jnp.logical_and(lane >= start, lane < start + 3)
            top = jnp.where(here, pltpu.roll(value, start + 3, 1), top)
            bottom = jnp.where(here, pltpu.roll(value, start, 1), bottom)
        bottom = jnp.where(lax.rem(lane, 3) == 2, pltpu.roll(bottom, 2, 1), bottom)
        tops.append(top[:width])
        bottoms.append(bottom[:width])
    for index in range(2):
        rows = pl.ds(index * width, width)
        top_ref[rows, :] = tops[index]
        bottom_ref[rows, :] = bottoms[index]
        first_ref[rows, :] = jnp.where(even, tops[index], bottoms[index])
        second_ref[rows, :] = jnp.where(even, bottoms[index], tops[index])


def corners_kernel(top_ref, east_base_ref, west_base_ref, seam_ref, *refs):
    north_ref, south_ref, east_ref, fold_ref, west_ref, rest_ref = refs[-6:]
    received = refs[:-6]
    lanes = top_ref.shape[1]
    width = top_ref.shape[0] // 2
    lat = lax.axis_index("lat")
    even = lax.rem(lat, 2) == 0
    from_first = received[0][...]
    from_second = received[1][...] if len(received) > 1 else jnp.zeros_like(from_first)
    north = jnp.where(even, from_first, from_second)
    south = jnp.where(even, from_second, from_first)
    north_ref[...] = north
    south_ref[...] = south
    base = west_base_ref.shape[0] - 8
    near = width - 1
    east_ref[pl.ds(0, base), :] = east_base_ref[pl.ds(0, base), :]
    east_ref[pl.ds(base, 8), :] = jnp.concatenate(
        [
            east_base_ref[pl.ds(base, 2), :],
            north[near : near + 1],
            north[width + near : width + near + 1],
            jnp.zeros((4, lanes), jnp.float32),
        ],
        axis=0,
    )
    west_ref[pl.ds(0, base), :] = west_base_ref[pl.ds(0, base), :]
    west_ref[pl.ds(base, 8), :] = jnp.concatenate(
        [
            west_base_ref[pl.ds(base, 2), :],
            north[0:1],
            north[width : width + 1],
            south[0:1],
            south[width : width + 1],
            jnp.zeros((2, lanes), jnp.float32),
        ],
        axis=0,
    )
    code = seam_ref[0]
    corner = lax.rem(code, 2) == 1
    for index in range(2):
        rows = pl.ds(index * width, width)
        top = tall(top_ref[rows, :])
        fold_ref[rows, :] = jnp.where(corner, top, pltpu.roll(top, 1, 1))[:width]
    unused = fold_ref.shape[0] - 2 * width
    fold_ref[pl.ds(2 * width, unused), :] = jnp.zeros((unused, lanes), jnp.float32)
    rest_ref[...] = jnp.full((SUB, lanes), lax.rem(code, width), jnp.int32)


def mixing_constants(levels):
    gain = TIME_STEP * VERTICAL_VISC
    inner, last, ratio = [], [], 0.0
    for k in range(levels):
        above = gain if k > 0 else 0.0
        last.append(1.0 / (1.0 + above + above * ratio))
        pivot = 1.0 + above + gain + above * ratio
        inner.append(1.0 / pivot)
        ratio = -gain / pivot
    return inner, last


def keep_kernel(message_ref, kept_ref):
    kept_ref[...] = message_ref[...]


def mirror_kernel(own_tiles, own_ref, rest_ref, *refs):
    tiles, (mirror_ref, tiles_ref) = refs[:-2], refs[-2:]
    width = tiles_ref.shape[1] // 3
    rest = rest_ref[0, 0]
    lon = lax.axis_index("lon")
    for index in range(2):
        half = pl.ds(index * width, width)
        for place, ref in zip((1, 0, 2), tiles):
            tile = ref[half, :]
            for device in own_tiles[place]:
                tile = jnp.where(lon == device, own_ref[half, :], tile)
            tiles_ref[index, pl.ds(place * width, width), :] = tile
        for i in range(-1, width + 1):
            mirror_ref[index, pl.ds(i + 1, 1), :] = tiles_ref[
                index, pl.ds(width + rest - i, 1), :
            ]


def step_kernel(
    t_ref,
    s_ref,
    u_ref,
    v_ref,
    depth_ref,
    mix_ref,
    wind_ref,
    bottom_ref,
    north_ref,
    south_ref,
    west_ref,
    east_ref,
    mirror_ref,
    t_out,
    s_out,
    u_out,
    v_out,
    gx_t_ref,
    gx_s_ref,
    u2_ref,
    v2_ref,
    val_ref,
    near_north_ref,
    near_south_ref,
    face_south_ref,
):
    levels, width, lanes = t_ref.shape
    lat = lax.axis_index("lat")
    lat_count = lax.axis_size("lat")
    is_top = lat == lat_count - 1
    lane = lane_of(lanes)
    row = row_of(lanes)
    depth_at = 6 * levels
    count_at = 6 * levels + 2

    def half(ref, index):
        return tall(ref[pl.ds(index * width, width), :])

    north, north_uv = (
        jnp.where(
            is_top, sign * tall(mirror_ref[index, pl.ds(1, width), :]), half(north_ref, index)
        )
        for index, sign in ((0, 1.0), (1, -1.0))
    )
    south, south_uv = half(south_ref, 0), half(south_ref, 1)
    bottom = half(bottom_ref, 0)

    def line(ref, index):
        return jnp.broadcast_to(ref[pl.ds(index, 1), :], (SUB, lanes))

    def mirror_line(index, i):
        return jnp.broadcast_to(mirror_ref[index, pl.ds(i + 1, 1), :], (SUB, lanes))

    nw = jnp.where(is_top, mirror_line(0, -1), line(west_ref, depth_at + 2))
    nw_uv = jnp.where(is_top, -mirror_line(1, -1), line(west_ref, depth_at + 3))
    ne = jnp.where(is_top, mirror_line(0, width), line(east_ref, depth_at + 2))
    se = line(east_ref, depth_at + 4)
    se_uv = line(east_ref, depth_at + 5)

    def to_east(value, halo):
        return jnp.where(row == width - 1, halo, pltpu.roll(value, SUB - 1, 0))

    def to_west(value, halo):
        return jnp.where(row == 0, halo, pltpu.roll(value, 1, 0))

    def to_north(value, halo):
        return jnp.where(lane == lanes - 1, halo, pltpu.roll(value, lanes - 1, 1))

    def to_south(value, halo):
        return jnp.where(lane == 0, halo, pltpu.roll(value, 1, 1))

    def at_north(message, index):
        return pltpu.roll(message, lanes - 1 - index, 1)

    def at_south(message, index):
        return pltpu.roll(message, (lanes - index) % lanes, 1)

    depth = tall(depth_ref[...])
    d_n = to_north(depth, at_north(north, count_at))
    d_nn = to_north(d_n, at_north(north, count_at - 1))
    d_s = to_south(depth, at_south(south, count_at))
    d_e = to_east(depth, line(east_ref, depth_at))
    d_ee = to_east(d_e, line(east_ref, depth_at + 1))
    d_w = to_west(depth, line(west_ref, depth_at))
    east_line = line(east_ref, depth_at)
    west_line = line(west_ref, depth_at)
    d_ne = to_east(d_n, to_north(east_line, at_north(ne, count_at)))
    d_se = to_east(d_s, to_south(east_line, at_south(se, count_at)))
    d_nw = to_west(d_n, to_north(west_line, at_north(nw, count_at)))
    d_u = jnp.minimum(depth, d_e)
    d_v = jnp.minimum(depth, d_n)
    u_neighbours = [
        jnp.minimum(d_u, d)
        for d in (
            jnp.minimum(d_e, d_ee),
            d_w,
            jnp.minimum(d_n, d_ne),
            jnp.minimum(d_s, d_se),
        )
    ]
    v_neighbours = [
        jnp.minimum(d_v, d)
        for d in (
            jnp.minimum(d_e, d_ne),
            jnp.minimum(d_w, d_nw),
            jnp.minimum(d_n, d_nn),
            d_s,
        )
    ]

    level_row = lax.broadcasted_iota(jnp.int32, (levels, lanes), 0)
    level_lane = lax.broadcasted_iota(jnp.int32, (levels, lanes), 1)
    wet_row = jnp.minimum(
        west_ref[pl.ds(depth_at, 1), :], depth_ref[pl.ds(0, 1), :]
    )
    wet_face = level_row.astype(jnp.float32) < wet_row
    u_west = west_ref[pl.ds(4 * levels, levels), :]
    for place, field, target in ((0, t_ref, gx_t_ref), (2, s_ref, gx_s_ref)):
        near = west_ref[pl.ds(place * levels, levels), :]
        far = west_ref[pl.ds((place + 1) * levels, levels), :]
        own = field[:, 0, :]
        face = u_west * (1.0 / 12.0) * (7.0 * (near + own) - (far + field[:, 1, :]))
        target[...] = jnp.where(wet_face, face - TRACER_DIFF * (own - near), 0.0)

    def column(corner, place):
        picked = jnp.where(level_lane == 3 * (place * levels + level_row) + 2, corner[0:1], 0.0)
        return jnp.sum(picked, axis=1, keepdims=True)

    u_corner = column(nw_uv, 0)
    v_corner = column(se_uv, 1)
    u2_ref[...] = u_west + jnp.where(
        level_lane == lanes - 1, u_corner, pltpu.roll(u_west, lanes - 1, 1)
    )
    v_east = east_ref[pl.ds(5 * levels, levels), :]
    v2_ref[...] = v_east + jnp.where(level_lane == 0, v_corner, pltpu.roll(v_east, 1, 1))

    in_block = jnp.where(lane < 3 * levels, lane, lane - 3 * levels).astype(jnp.float32)
    v_south = jnp.where(lane < 3 * levels, at_south(south_uv, 3 * levels), south_uv)
    both = south + bottom
    face = v_south * (1.0 / 12.0) * (7.0 * both - pltpu.roll(both, 1, 1))
    face = face - TRACER_DIFF * (bottom - south)
    wet_south = jnp.minimum(
        south[:, count_at : count_at + 1], bottom[:, count_at : count_at + 1]
    )
    face_south = jnp.where(in_block < 3.0 * wet_south, face, 0.0)

    for k in range(levels):
        for place, message in ((0, north), (2, north), (4, north_uv), (5, north_uv)):
            spot = 3 * k + 2 + (3 * levels if place in (2, 5) else 0)
            near_north_ref[place * levels + k] = at_north(message, spot)
            if place < 4:
                near_north_ref[(place + 1) * levels + k] = at_north(message, spot - 1)
    for k in range(levels):
        for place, message in ((0, south), (1, south), (2, south_uv), (3, south_uv)):
            spot = 3 * (place % 2 * levels + k) + 2
            near_south_ref[place * levels + k] = at_south(message, spot)
        for place in range(2):
            face_south_ref[place * levels + k] = at_south(
                face_south, 3 * (place * levels + k) + 2
            )

    row_id = (lat * lanes + lane).astype(jnp.float32)
    total = float(lat_count * lanes)
    cor_u = 2.0 * (row_id + 0.5) / total - 1.0
    cor_v = 2.0 * (row_id + 1.0) / total - 1.0
    inner, last = mixing_constants(levels)
    gain = TIME_STEP * VERTICAL_VISC

    def masked(k, count, value):
        return jnp.where(float(k) < count, value, 0.0)

    px = jnp.zeros((SUB, lanes), jnp.float32)
    py = jnp.zeros((SUB, lanes), jnp.float32)
    above = None
    ratio = None
    values = None
    for k in range(levels):
        u = tall(u_ref[k])
        v = tall(v_ref[k])
        u_face = masked(k, d_u, u * (1.0 / 12.0))
        u_diff = masked(k, d_u, TRACER_DIFF)
        v_face = masked(k, d_v, v * (1.0 / 12.0))
        v_diff = masked(k, d_v, TRACER_DIFF)
        stars = []
        seen = []
        for place, field, gx_ref in ((0, t_ref, gx_t_ref), (2, s_ref, gx_s_ref)):
            near, far = place * levels + k, (place + 1) * levels + k
            c = tall(field[k])
            c_e = to_east(c, line(east_ref, near))
            c_ee = to_east(c_e, line(east_ref, far))
            c_w = to_west(c, line(west_ref, near))
            c_n = to_north(c, near_north_ref[near])
            c_nn = to_north(c_n, near_north_ref[far])
            c_s = to_south(c, near_south_ref[place // 2 * levels + k])
            gx = u_face * (7.0 * (c + c_e) - (c_w + c_ee)) - u_diff * (c_e - c)
            gy = v_face * (7.0 * (c + c_n) - (c_s + c_nn)) - v_diff * (c_n - c)
            gx_w = to_west(gx, line(gx_ref, k))
            gy_s = to_south(gy, face_south_ref[place // 2 * levels + k])
            stars.append(c - TIME_STEP * masked(k, depth, (gx - gx_w) + (gy - gy_s)))
            seen.append((c, c_e, c_n))
        weights = THERMAL_EXPANSION, HALINE_CONTRACTION
        b, b_e, b_n = (
            masked(k, d, weights[0] * warm - weights[1] * salt)
            for d, warm, salt in zip((depth, d_e, d_n), seen[0], seen[1])
        )
        bx = b_e - b
        by = b_n - b
        px = px + bx
        py = py + by

        u_e = to_east(u, line(east_ref, 4 * levels + k))
        u_w = to_west(u, line(west_ref, 4 * levels + k))
        u_n = to_north(u, near_north_ref[4 * levels + k])
        u_s = to_south(u, near_south_ref[2 * levels + k])
        v_e = to_east(v, line(east_ref, 5 * levels + k))
        v_w = to_west(v, line(west_ref, 5 * levels + k))
        v_n = to_north(v, near_north_ref[5 * levels + k])
        v_s = to_south(v, near_south_ref[3 * levels + k])
        v2 = v + v_s
        u2 = u + u_n
        v_bar = 0.25 * (v2 + to_east(v2, line(v2_ref, k)))
        u_bar = 0.25 * (u2 + to_west(u2, line(u2_ref, k)))
        u_visc = sum(masked(k, d, n - u) for d, n in zip(u_neighbours, (u_e, u_w, u_n, u_s)))
        v_visc = sum(masked(k, d, n - v) for d, n in zip(v_neighbours, (v_e, v_w, v_n, v_s)))
        u_star = u + TIME_STEP * (cor_u * v_bar - (px - 0.5 * bx) + MOMENTUM_VISC * u_visc)
        v_star = v + TIME_STEP * (-cor_v * u_bar - (py - 0.5 * by) + MOMENTUM_VISC * v_visc)
        if k == 0:
            u_star = u_star + TIME_STEP * WIND_GAIN * tall(wind_ref[0])
            v_star = v_star + TIME_STEP * WIND_GAIN * tall(wind_ref[1])

        if k < levels - 1:
            below = masked(k + 1, depth, TIME_STEP * tall(mix_ref[k]))
        else:
            below = None
        pivot = 1.0
        if above is not None:
            pivot = pivot + above * (1.0 - ratio)
        if below is not None:
            pivot = pivot + below
        inverse = 1.0 / pivot

        def momentum_weight(count):
            weight = jnp.where(float(k) < count, last[k], 0.0)
            if k < levels - 1:
                weight = jnp.where(float(k + 1) < count, inner[k], weight)
            return weight

        rights = stars + [u_star, v_star]
        scales = [inverse, inverse, momentum_weight(d_u), momentum_weight(d_v)]
        if k > 0:
            gains = [above, above, gain, gain]
            rights = [right + g * value for right, g, value in zip(rights, gains, values)]
        values = [right * scale for right, scale in zip(rights, scales)]
        for index, value in enumerate(values):
            val_ref[index, k] = value
        if below is not None:
            ratio = below * inverse
            val_ref[4, k] = ratio
        above = below

    outs = (t_out, s_out, u_out, v_out)
    for k in range(levels - 1, -1, -1):
        if k < levels - 1:
            ratios = [val_ref[4, k], val_ref[4, k], gain * inner[k], gain * inner[k]]
            values = [val_ref[i, k] + ratios[i] * values[i] for i in range(4)]
        for out, value in zip(outs, values):
            out[k] = value[:width]


def shards(
    thermal_anomaly,
    saltiness_anomaly,
    zonal_current,
    meridional_current,
    bottom_ocean_layer,
    seam_axis_meridian,
    interface_diffusivity,
    atmospheric_forcing,
):
    levels, width, lanes = thermal_anomaly.shape
    lon_count = lax.axis_size("lon")
    lat_count = lax.axis_size("lat")
    fields = (thermal_anomaly, saltiness_anomaly, zonal_current, meridional_current)
    wind = atmospheric_forcing
    f32 = jnp.float32
    row_message = jax.ShapeDtypeStruct((2 * width, lanes), f32)
    column_message = jax.ShapeDtypeStruct((6 * levels + 8, lanes), f32)

    fold_message = jax.ShapeDtypeStruct((6 * levels + 16, lanes), f32)
    top, bottom, eastward, westward, first, second, counts, stress = pl.pallas_call(
        edges_kernel,
        out_shape=[row_message] * 2
        + [column_message] * 2
        + [row_message] * 2
        + [jax.ShapeDtypeStruct((width, lanes), f32), jax.ShapeDtypeStruct(wind.shape, f32)],
        in_specs=[VMEM] * 6,
        out_specs=[VMEM] * 8,
        compiler_params=FIRST,
    )(*[pltpu.with_memory_space_constraint(x, pltpu.HBM) for x in (*fields, bottom_ocean_layer, wind)])

    received = []
    for start, message in ((0, first), (1, second)):
        pairs = [
            (a, b) for i in range(start, lat_count - 1, 2) for a, b in ((i, i + 1), (i + 1, i))
        ]
        if pairs:
            received.append(lax.ppermute(message, "lat", pairs))

    north, south, eastward, fold, westward, rest = pl.pallas_call(
        corners_kernel,
        out_shape=[row_message] * 2
        + [column_message, fold_message, column_message]
        + [jax.ShapeDtypeStruct((SUB, lanes), jnp.int32)],
        in_specs=[VMEM] * 3 + [SMEM] + [VMEM] * len(received),
        out_specs=[VMEM] * 6,
        compiler_params=SMALL,
    )(top, eastward, westward, seam_axis_meridian, *received)

    code = seam_axis_meridian[0]
    tile = lax.rem(lax.div(code, width), lon_count)
    three = (lax.rem(code, width) == width - 1).astype(jnp.int32)
    ring = [(i, (i + 1) % lon_count) for i in range(lon_count)]
    trade = [(i, i ^ 1) for i in range(lon_count)]
    last_row = lat_count - 1

    def fold_pairs(mirror):
        return [
            (a * lat_count + row, b * lat_count + row)
            for row in range(lat_count)
            for a, b in (mirror if row == last_row else trade)
        ]

    from_west = lax.ppermute(eastward, "lon", ring)
    keep = pl.pallas_call(
        keep_kernel,
        out_shape=column_message,
        in_specs=[VMEM],
        out_specs=VMEM,
        compiler_params=SMALL,
    )

    def reflect(code):
        own = [i for i in range(lon_count) if (code - i) % lon_count == i]
        if len(own) != 2:
            return [(i, (code - i) % lon_count) for i in range(lon_count)], []
        trade = {own[0]: own[1], own[1]: own[0]}
        return [(i, trade.get(i, (code - i) % lon_count)) for i in range(lon_count)], own

    def exchange(first, count):
        mirrors, own_tiles = zip(*(reflect(first - 1 + d) for d in range(3)))
        mirror = pl.pallas_call(
            functools.partial(mirror_kernel, own_tiles),
            out_shape=jax.ShapeDtypeStruct((2, 16, lanes), f32),
            in_specs=[VMEM] * (2 + count),
            out_specs=VMEM,
            scratch_shapes=[pltpu.VMEM((2, 3 * width, lanes), f32)],
            compiler_params=SMALL,
        )

        def branch(fold, westward, rest):
            tiles = [lax.ppermute(fold, ("lon", "lat"), fold_pairs(mirrors[d])) for d in (1, 0, 2)[:count]]
            return (
                keep(lax.ppermute(westward, "lon", [(b, a) for a, b in ring])),
                mirror(fold, rest, *tiles),
            )

        return branch

    branches = [exchange(first, count) for first in range(lon_count) for count in (2, 3)]
    from_east, mirrored = lax.switch(
        tile * 2 + three, branches, fold, westward, rest
    )

    whole = jax.ShapeDtypeStruct((levels, width, lanes), f32)
    return pl.pallas_call(
        step_kernel,
        out_shape=[whole] * 4,
        in_specs=[VMEM] * 13,
        out_specs=[VMEM] * 4,
        compiler_params=LARGE,
        scratch_shapes=[pltpu.VMEM((levels, lanes), f32)] * 4
        + [pltpu.VMEM((5, levels, SUB, lanes), f32)]
        + [pltpu.VMEM((count * levels, SUB, lanes), f32) for count in (6, 4, 2)],
    )(
        *fields,
        counts,
        interface_diffusivity,
        stress,
        bottom,
        north,
        south,
        from_west,
        from_east,
        mirrored,
    )


def solution(mesh):
    split = P(None, "lon", "lat")
    return jax.shard_map(
        shards,
        mesh=mesh,
        in_specs=(split, split, split, split, P("lon", "lat"), P(), split, split),
        out_specs=(split, split, split, split),
        check_vma=False,
    )
```

```python
import functools

import jax
import jax.numpy as jnp
from jax import lax
from jax.experimental import pallas as pl
from jax.experimental.pallas import tpu as pltpu
from jax.sharding import PartitionSpec as P

TIME_STEP = 0.2
TRACER_DIFF = 0.2
MOMENTUM_VISC = 0.2
THERMAL_EXPANSION = 0.5
HALINE_CONTRACTION = 0.4
WIND_GAIN = 2.0
VERTICAL_VISC = 1.0

VMEM = pl.BlockSpec(memory_space=pltpu.VMEM)
SMEM = pl.BlockSpec(memory_space=pltpu.SMEM)
SUB = 8
SMALL = pltpu.CompilerParams(vmem_limit_bytes=4 * 2**20)
FIRST = pltpu.CompilerParams(vmem_limit_bytes=4 * 2**20)
LARGE = pltpu.CompilerParams(vmem_limit_bytes=8 * 2**20)


def lane_of(lanes):
    return lax.broadcasted_iota(jnp.int32, (SUB, lanes), 1)


def row_of(lanes):
    return lax.broadcasted_iota(jnp.int32, (SUB, lanes), 0)


def tall(value):
    missing = SUB - value.shape[0]
    if missing == 0:
        return value
    return jnp.concatenate([value, jnp.zeros((missing, value.shape[1]), value.dtype)], axis=0)


def edges_kernel(t_ref, s_ref, u_ref, v_ref, depth_ref, stress_ref, *outs):
    top_ref, bottom_ref, east_ref, west_ref, count_ref, wind_ref, first_ref = outs[:7]
    levels, width, lanes = t_ref.shape
    count_ref[...] = depth_ref[...].astype(jnp.float32)
    wind_ref[...] = stress_ref[...]
    even = lax.rem(lax.axis_index("lat"), 2) == 0
    lane = lane_of(lanes)
    for message, near, far in ((east_ref, width - 1, width - 2), (west_ref, 0, 1)):
        for place, field, column in (
            (0, t_ref, near),
            (1, t_ref, far),
            (2, s_ref, near),
            (3, s_ref, far),
            (4, u_ref, near),
            (5, v_ref, near),
        ):
            message[pl.ds(place * levels, levels), :] = field.reshape(levels * width, lanes)[pl.ds(column, levels, stride=width), :]
        depth = depth_ref[...].astype(jnp.float32)
        message[pl.ds(6 * levels, 8), :] = jnp.concatenate(
            [depth[near : near + 1], depth[far : far + 1]] * 4, axis=0
        )

    tops, bottoms = [], []
    for first, second, count in ((t_ref, s_ref, depth_ref), (u_ref, v_ref, None)):
        top = jnp.zeros((SUB, lanes), jnp.float32)
        bottom = jnp.zeros((SUB, lanes), jnp.float32)
        places = [(3 * k, first, k) for k in range(levels)]
        places += [(3 * (levels + k), second, k) for k in range(levels)]
        if count is not None:
            places.append((6 * levels, count, None))
        for start, ref, k in places:
            value = depth_ref[...].astype(jnp.float32) if k is None else ref[k]
            value = tall(value)
            here = jnp.logical_and(lane >= start, lane < start + 3)
            top = jnp.where(here, pltpu.roll(value, start + 3, 1), top)
            bottom = jnp.where(here, pltpu.roll(value, start, 1), bottom)
        bottom = jnp.where(lax.rem(lane, 3) == 2, pltpu.roll(bottom, 2, 1), bottom)
        tops.append(top[:width])
        bottoms.append(bottom[:width])
    for index in range(2):
        rows = pl.ds(index * width, width)
        top_ref[rows, :] = tops[index]
        bottom_ref[rows, :] = bottoms[index]
        first_ref[rows, :] = jnp.where(even, tops[index], bottoms[index])
        first_ref[pl.ds((2 + index) * width, width), :] = tops[index]
        for second_ref in outs[7:]:
            second_ref[rows, :] = jnp.where(even, bottoms[index], tops[index])


def corners_kernel(top_ref, east_base_ref, west_base_ref, seam_ref, *refs):
    north_ref, south_ref, east_ref, fold_ref, west_ref, rest_ref = refs[-6:]
    received = refs[:-6]
    lanes = top_ref.shape[1]
    width = top_ref.shape[0] // 2
    lat = lax.axis_index("lat")
    even = lax.rem(lat, 2) == 0
    halo = pl.ds(0, 2 * width)
    from_first = received[0][halo, :]
    from_second = received[1][...] if len(received) > 1 else jnp.zeros_like(from_first)
    north = jnp.where(even, from_first, from_second)
    south = jnp.where(even, from_second, from_first)
    north_ref[...] = north
    south_ref[...] = south
    base = west_base_ref.shape[0] - 8
    near = width - 1
    east_ref[pl.ds(0, base), :] = east_base_ref[pl.ds(0, base), :]
    east_ref[pl.ds(base, 8), :] = jnp.concatenate(
        [
            east_base_ref[pl.ds(base, 2), :],
            north[near : near + 1],
            north[width + near : width + near + 1],
            jnp.zeros((4, lanes), jnp.float32),
        ],
        axis=0,
    )
    west_ref[pl.ds(0, base), :] = west_base_ref[pl.ds(0, base), :]
    west_ref[pl.ds(base, 8), :] = jnp.concatenate(
        [
            west_base_ref[pl.ds(base, 2), :],
            north[0:1],
            north[width : width + 1],
            south[0:1],
            south[width : width + 1],
            jnp.zeros((2, lanes), jnp.float32),
        ],
        axis=0,
    )
    is_top = lat == lax.axis_size("lat") - 1
    code = seam_ref[0]
    corner = lax.rem(code, 2) == 1
    for index in range(2):
        rows = pl.ds(index * width, width)
        theirs = received[0][pl.ds((2 + index) * width, width), :]
        top = tall(jnp.where(is_top, top_ref[rows, :], theirs))
        fold_ref[rows, :] = jnp.where(corner, top, pltpu.roll(top, 1, 1))[:width]
    unused = fold_ref.shape[0] - 2 * width
    fold_ref[pl.ds(2 * width, unused), :] = jnp.zeros((unused, lanes), jnp.float32)
    rest_ref[...] = jnp.full((SUB, lanes), lax.rem(code, width), jnp.int32)


def mixing_constants(levels):
    gain = TIME_STEP * VERTICAL_VISC
    inner, last, ratio = [], [], 0.0
    for k in range(levels):
        above = gain if k > 0 else 0.0
        last.append(1.0 / (1.0 + above + above * ratio))
        pivot = 1.0 + above + gain + above * ratio
        inner.append(1.0 / pivot)
        ratio = -gain / pivot
    return inner, last


def keep_kernel(message_ref, kept_ref):
    kept_ref[...] = message_ref[...]


def mirror_kernel(own_tiles, own_ref, rest_ref, *refs):
    tiles, (mirror_ref, tiles_ref) = refs[:-2], refs[-2:]
    width = tiles_ref.shape[1] // 3
    rest = rest_ref[0, 0]
    lon = lax.axis_index("lon")
    for index in range(2):
        half = pl.ds(index * width, width)
        for place, ref in enumerate(tiles):
            tile = ref[half, :]
            for device in own_tiles[place]:
                tile = jnp.where(lon == device, own_ref[half, :], tile)
            tiles_ref[index, pl.ds(place * width, width), :] = tile
        for i in range(-1, width + 1):
            mirror_ref[index, pl.ds(i + 1, 1), :] = tiles_ref[
                index, pl.ds(width + rest - i, 1), :
            ]


def step_kernel(
    t_ref,
    s_ref,
    u_ref,
    v_ref,
    depth_ref,
    mix_ref,
    wind_ref,
    bottom_ref,
    north_ref,
    south_ref,
    west_ref,
    east_ref,
    mirror_ref,
    t_out,
    s_out,
    u_out,
    v_out,
    gx_t_ref,
    gx_s_ref,
    u2_ref,
    v2_ref,
    val_ref,
    near_north_ref,
    near_south_ref,
    face_south_ref,
):
    levels, width, lanes = t_ref.shape
    lat = lax.axis_index("lat")
    lat_count = lax.axis_size("lat")
    is_top = lat == lat_count - 1
    lane = lane_of(lanes)
    row = row_of(lanes)
    depth_at = 6 * levels
    count_at = 6 * levels + 2

    def half(ref, index):
        return tall(ref[pl.ds(index * width, width), :])

    north, north_uv = (
        jnp.where(
            is_top, sign * tall(mirror_ref[index, pl.ds(1, width), :]), half(north_ref, index)
        )
        for index, sign in ((0, 1.0), (1, -1.0))
    )
    south, south_uv = half(south_ref, 0), half(south_ref, 1)
    bottom = half(bottom_ref, 0)

    def line(ref, index):
        return jnp.broadcast_to(ref[pl.ds(index, 1), :], (SUB, lanes))

    def mirror_line(index, i):
        return jnp.broadcast_to(mirror_ref[index, pl.ds(i + 1, 1), :], (SUB, lanes))

    nw = jnp.where(is_top, mirror_line(0, -1), line(west_ref, depth_at + 2))
    nw_uv = jnp.where(is_top, -mirror_line(1, -1), line(west_ref, depth_at + 3))
    ne = jnp.where(is_top, mirror_line(0, width), line(east_ref, depth_at + 2))
    se = line(east_ref, depth_at + 4)
    se_uv = line(east_ref, depth_at + 5)

    def to_east(value, halo):
        return jnp.where(row == width - 1, halo, pltpu.roll(value, SUB - 1, 0))

    def to_west(value, halo):
        return jnp.where(row == 0, halo, pltpu.roll(value, 1, 0))

    def to_north(value, halo):
        return jnp.where(lane == lanes - 1, halo, pltpu.roll(value, lanes - 1, 1))

    def to_south(value, halo):
        return jnp.where(lane == 0, halo, pltpu.roll(value, 1, 1))

    def at_north(message, index):
        return pltpu.roll(message, lanes - 1 - index, 1)

    def at_south(message, index):
        return pltpu.roll(message, (lanes - index) % lanes, 1)

    depth = tall(depth_ref[...])
    d_n = to_north(depth, at_north(north, count_at))
    d_nn = to_north(d_n, at_north(north, count_at - 1))
    d_s = to_south(depth, at_south(south, count_at))
    d_e = to_east(depth, line(east_ref, depth_at))
    d_ee = to_east(d_e, line(east_ref, depth_at + 1))
    d_w = to_west(depth, line(west_ref, depth_at))
    east_line = line(east_ref, depth_at)
    west_line = line(west_ref, depth_at)
    d_ne = to_east(d_n, to_north(east_line, at_north(ne, count_at)))
    d_se = to_east(d_s, to_south(east_line, at_south(se, count_at)))
    d_nw = to_west(d_n, to_north(west_line, at_north(nw, count_at)))
    d_u = jnp.minimum(depth, d_e)
    d_v = jnp.minimum(depth, d_n)
    u_neighbours = [
        jnp.minimum(d_u, d)
        for d in (
            jnp.minimum(d_e, d_ee),
            d_w,
            jnp.minimum(d_n, d_ne),
            jnp.minimum(d_s, d_se),
        )
    ]
    v_neighbours = [
        jnp.minimum(d_v, d)
        for d in (
            jnp.minimum(d_e, d_ne),
            jnp.minimum(d_w, d_nw),
            jnp.minimum(d_n, d_nn),
            d_s,
        )
    ]

    level_row = lax.broadcasted_iota(jnp.int32, (levels, lanes), 0)
    level_lane = lax.broadcasted_iota(jnp.int32, (levels, lanes), 1)
    wet_row = jnp.minimum(
        west_ref[pl.ds(depth_at, 1), :], depth_ref[pl.ds(0, 1), :]
    )
    wet_face = level_row.astype(jnp.float32) < wet_row
    u_west = west_ref[pl.ds(4 * levels, levels), :]
    for place, field, target in ((0, t_ref, gx_t_ref), (2, s_ref, gx_s_ref)):
        near = west_ref[pl.ds(place * levels, levels), :]
        far = west_ref[pl.ds((place + 1) * levels, levels), :]
        own = field[:, 0, :]
        face = u_west * (1.0 / 12.0) * (7.0 * (near + own) - (far + field[:, 1, :]))
        target[...] = jnp.where(wet_face, face - TRACER_DIFF * (own - near), 0.0)

    def column(corner, place):
        picked = jnp.where(level_lane == 3 * (place * levels + level_row) + 2, corner[0:1], 0.0)
        return jnp.sum(picked, axis=1, keepdims=True)

    u_corner = column(nw_uv, 0)
    v_corner = column(se_uv, 1)
    u2_ref[...] = u_west + jnp.where(
        level_lane == lanes - 1, u_corner, pltpu.roll(u_west, lanes - 1, 1)
    )
    v_east = east_ref[pl.ds(5 * levels, levels), :]
    v2_ref[...] = v_east + jnp.where(level_lane == 0, v_corner, pltpu.roll(v_east, 1, 1))

    in_block = jnp.where(lane < 3 * levels, lane, lane - 3 * levels).astype(jnp.float32)
    v_south = jnp.where(lane < 3 * levels, at_south(south_uv, 3 * levels), south_uv)
    both = south + bottom
    face = v_south * (1.0 / 12.0) * (7.0 * both - pltpu.roll(both, 1, 1))
    face = face - TRACER_DIFF * (bottom - south)
    wet_south = jnp.minimum(
        south[:, count_at : count_at + 1], bottom[:, count_at : count_at + 1]
    )
    face_south = jnp.where(in_block < 3.0 * wet_south, face, 0.0)

    for k in range(levels):
        for place, message in ((0, north), (2, north), (4, north_uv), (5, north_uv)):
            spot = 3 * k + 2 + (3 * levels if place in (2, 5) else 0)
            near_north_ref[place * levels + k] = at_north(message, spot)
            if place < 4:
                near_north_ref[(place + 1) * levels + k] = at_north(message, spot - 1)
    for k in range(levels):
        for place, message in ((0, south), (1, south), (2, south_uv), (3, south_uv)):
            spot = 3 * (place % 2 * levels + k) + 2
            near_south_ref[place * levels + k] = at_south(message, spot)
        for place in range(2):
            face_south_ref[place * levels + k] = at_south(
                face_south, 3 * (place * levels + k) + 2
            )

    row_id = (lat * lanes + lane).astype(jnp.float32)
    total = float(lat_count * lanes)
    cor_u = 2.0 * (row_id + 0.5) / total - 1.0
    cor_v = 2.0 * (row_id + 1.0) / total - 1.0
    inner, last = mixing_constants(levels)
    gain = TIME_STEP * VERTICAL_VISC

    def masked(k, count, value):
        return jnp.where(float(k) < count, value, 0.0)

    px = jnp.zeros((SUB, lanes), jnp.float32)
    py = jnp.zeros((SUB, lanes), jnp.float32)
    above = None
    ratio = None
    values = None
    for k in range(levels):
        u = tall(u_ref[k])
        v = tall(v_ref[k])
        u_face = masked(k, d_u, u * (1.0 / 12.0))
        u_diff = masked(k, d_u, TRACER_DIFF)
        v_face = masked(k, d_v, v * (1.0 / 12.0))
        v_diff = masked(k, d_v, TRACER_DIFF)
        stars = []
        seen = []
        for place, field, gx_ref in ((0, t_ref, gx_t_ref), (2, s_ref, gx_s_ref)):
            near, far = place * levels + k, (place + 1) * levels + k
            c = tall(field[k])
            c_e = to_east(c, line(east_ref, near))
            c_ee = to_east(c_e, line(east_ref, far))
            c_w = to_west(c, line(west_ref, near))
            c_n = to_north(c, near_north_ref[near])
            c_nn = to_north(c_n, near_north_ref[far])
            c_s = to_south(c, near_south_ref[place // 2 * levels + k])
            gx = u_face * (7.0 * (c + c_e) - (c_w + c_ee)) - u_diff * (c_e - c)
            gy = v_face * (7.0 * (c + c_n) - (c_s + c_nn)) - v_diff * (c_n - c)
            gx_w = to_west(gx, line(gx_ref, k))
            gy_s = to_south(gy, face_south_ref[place // 2 * levels + k])
            stars.append(c - TIME_STEP * masked(k, depth, (gx - gx_w) + (gy - gy_s)))
            seen.append((c, c_e, c_n))
        weights = THERMAL_EXPANSION, HALINE_CONTRACTION
        b, b_e, b_n = (
            masked(k, d, weights[0] * warm - weights[1] * salt)
            for d, warm, salt in zip((depth, d_e, d_n), seen[0], seen[1])
        )
        bx = b_e - b
        by = b_n - b
        px = px + bx
        py = py + by

        u_e = to_east(u, line(east_ref, 4 * levels + k))
        u_w = to_west(u, line(west_ref, 4 * levels + k))
        u_n = to_north(u, near_north_ref[4 * levels + k])
        u_s = to_south(u, near_south_ref[2 * levels + k])
        v_e = to_east(v, line(east_ref, 5 * levels + k))
        v_w = to_west(v, line(west_ref, 5 * levels + k))
        v_n = to_north(v, near_north_ref[5 * levels + k])
        v_s = to_south(v, near_south_ref[3 * levels + k])
        v2 = v + v_s
        u2 = u + u_n
        v_bar = 0.25 * (v2 + to_east(v2, line(v2_ref, k)))
        u_bar = 0.25 * (u2 + to_west(u2, line(u2_ref, k)))
        u_visc = sum(masked(k, d, n - u) for d, n in zip(u_neighbours, (u_e, u_w, u_n, u_s)))
        v_visc = sum(masked(k, d, n - v) for d, n in zip(v_neighbours, (v_e, v_w, v_n, v_s)))
        u_star = u + TIME_STEP * (cor_u * v_bar - (px - 0.5 * bx) + MOMENTUM_VISC * u_visc)
        v_star = v + TIME_STEP * (-cor_v * u_bar - (py - 0.5 * by) + MOMENTUM_VISC * v_visc)
        if k == 0:
            u_star = u_star + TIME_STEP * WIND_GAIN * tall(wind_ref[0])
            v_star = v_star + TIME_STEP * WIND_GAIN * tall(wind_ref[1])

        if k < levels - 1:
            below = masked(k + 1, depth, TIME_STEP * tall(mix_ref[k]))
        else:
            below = None
        pivot = 1.0
        if above is not None:
            pivot = pivot + above * (1.0 - ratio)
        if below is not None:
            pivot = pivot + below
        inverse = 1.0 / pivot

        def momentum_weight(count):
            weight = jnp.where(float(k) < count, last[k], 0.0)
            if k < levels - 1:
                weight = jnp.where(float(k + 1) < count, inner[k], weight)
            return weight

        rights = stars + [u_star, v_star]
        scales = [inverse, inverse, momentum_weight(d_u), momentum_weight(d_v)]
        if k > 0:
            gains = [above, above, gain, gain]
            rights = [right + g * value for right, g, value in zip(rights, gains, values)]
        values = [right * scale for right, scale in zip(rights, scales)]
        for index, value in enumerate(values):
            val_ref[index, k] = value
        if below is not None:
            ratio = below * inverse
            val_ref[4, k] = ratio
        above = below

    outs = (t_out, s_out, u_out, v_out)
    for k in range(levels - 1, -1, -1):
        if k < levels - 1:
            ratios = [val_ref[4, k], val_ref[4, k], gain * inner[k], gain * inner[k]]
            values = [val_ref[i, k] + ratios[i] * values[i] for i in range(4)]
        for out, value in zip(outs, values):
            out[k] = value[:width]


def shards(
    thermal_anomaly,
    saltiness_anomaly,
    zonal_current,
    meridional_current,
    bottom_ocean_layer,
    seam_axis_meridian,
    interface_diffusivity,
    atmospheric_forcing,
):
    levels, width, lanes = thermal_anomaly.shape
    lon_count = lax.axis_size("lon")
    lat_count = lax.axis_size("lat")
    fields = (thermal_anomaly, saltiness_anomaly, zonal_current, meridional_current)
    wind = atmospheric_forcing
    f32 = jnp.float32
    row_message = jax.ShapeDtypeStruct((2 * width, lanes), f32)
    column_message = jax.ShapeDtypeStruct((6 * levels + 8, lanes), f32)

    fold_message = jax.ShapeDtypeStruct((6 * levels + 16, lanes), f32)
    lat_pairs = [
        [(a, b) for i in range(start, lat_count - 1, 2) for a, b in ((i, i + 1), (i + 1, i))]
        for start in (0, 1)
    ]
    lat_pairs = [pairs for pairs in lat_pairs if pairs]
    top, bottom, eastward, westward, counts, stress, *messages = pl.pallas_call(
        edges_kernel,
        out_shape=[row_message] * 2
        + [column_message] * 2
        + [jax.ShapeDtypeStruct((width, lanes), f32), jax.ShapeDtypeStruct(wind.shape, f32)]
        + [jax.ShapeDtypeStruct((4 * width, lanes), f32), row_message][: len(lat_pairs)],
        in_specs=[VMEM] * 6,
        out_specs=[VMEM] * (6 + len(lat_pairs)),
        compiler_params=FIRST,
    )(*[pltpu.with_memory_space_constraint(x, pltpu.HBM) for x in (*fields, bottom_ocean_layer, wind)])
    received = [
        lax.ppermute(message, "lat", pairs) for message, pairs in zip(messages, lat_pairs)
    ]

    north, south, eastward, fold, westward, rest = pl.pallas_call(
        corners_kernel,
        out_shape=[row_message] * 2
        + [column_message, fold_message, column_message]
        + [jax.ShapeDtypeStruct((SUB, lanes), jnp.int32)],
        in_specs=[VMEM] * 3 + [SMEM] + [VMEM] * len(received),
        out_specs=[VMEM] * 6,
        compiler_params=SMALL,
    )(top, eastward, westward, seam_axis_meridian, *received)

    code = seam_axis_meridian[0]
    tile = lax.rem(lax.div(code, width), lon_count)
    three = (lax.rem(code, width) == width - 1).astype(jnp.int32)
    ring = [(i, (i + 1) % lon_count) for i in range(lon_count)]
    trade = [(i, i ^ 1) for i in range(lon_count)]
    pairs = [(i, i ^ 1) for i in range(lat_count)]

    def fold_pairs(*mirrors):
        rows = [*mirrors] + [trade] * (lat_count - len(mirrors))
        return [
            (a * lat_count + lat_count - 1 - row, b * lat_count + lat_count - 1 - row)
            for row, mirror in enumerate(rows)
            for a, b in mirror
        ]

    from_west = lax.ppermute(eastward, "lon", ring)
    keep = pl.pallas_call(
        keep_kernel,
        out_shape=column_message,
        in_specs=[VMEM],
        out_specs=VMEM,
        compiler_params=SMALL,
    )

    def reflect(code):
        own = [i for i in range(lon_count) if (code - i) % lon_count == i]
        if len(own) != 2:
            return [(i, (code - i) % lon_count) for i in range(lon_count)], []
        trade = {own[0]: own[1], own[1]: own[0]}
        return [(i, trade.get(i, (code - i) % lon_count)) for i in range(lon_count)], own

    def exchange(first, count):
        mirrors, own_tiles = zip(*(reflect(first - 1 + d) for d in range(3)))
        mirror = pl.pallas_call(
            functools.partial(mirror_kernel, own_tiles),
            out_shape=jax.ShapeDtypeStruct((2, 16, lanes), f32),
            in_specs=[VMEM] * (2 + count),
            out_specs=VMEM,
            scratch_shapes=[pltpu.VMEM((2, 3 * width, lanes), f32)],
            compiler_params=SMALL,
        )

        def branch(fold, westward, rest):
            both = ("lon", "lat")
            tile = lax.ppermute(fold, both, fold_pairs(mirrors[0], mirrors[1]))
            tiles = [tile, lax.ppermute(tile[: 2 * width], "lat", pairs)]
            if count == 3:
                tiles.append(lax.ppermute(fold, both, fold_pairs(mirrors[2])))
            return (
                keep(lax.ppermute(westward, "lon", [(b, a) for a, b in ring])),
                mirror(fold, rest, *tiles),
            )

        return branch

    branches = [exchange(first, count) for first in range(lon_count) for count in (2, 3)]
    from_east, mirrored = lax.switch(
        tile * 2 + three, branches, fold, westward, rest
    )

    whole = jax.ShapeDtypeStruct((levels, width, lanes), f32)
    return pl.pallas_call(
        step_kernel,
        out_shape=[whole] * 4,
        in_specs=[VMEM] * 13,
        out_specs=[VMEM] * 4,
        compiler_params=LARGE,
        scratch_shapes=[pltpu.VMEM((levels, lanes), f32)] * 4
        + [pltpu.VMEM((5, levels, SUB, lanes), f32)]
        + [pltpu.VMEM((count * levels, SUB, lanes), f32) for count in (6, 4, 2)],
    )(
        *fields,
        counts,
        interface_diffusivity,
        stress,
        bottom,
        north,
        south,
        from_west,
        from_east,
        mirrored,
    )


def solution(mesh):
    split = P(None, "lon", "lat")
    return jax.shard_map(
        shards,
        mesh=mesh,
        in_specs=(split, split, split, split, P("lon", "lat"), P(), split, split),
        out_specs=(split, split, split, split),
        check_vma=False,
    )
```

```python
import functools

import jax
import jax.numpy as jnp
from jax import lax
from jax.experimental import pallas as pl
from jax.experimental.pallas import tpu as pltpu
from jax.sharding import PartitionSpec as P

TIME_STEP = 0.2
TRACER_DIFF = 0.2
MOMENTUM_VISC = 0.2
THERMAL_EXPANSION = 0.5
HALINE_CONTRACTION = 0.4
WIND_GAIN = 2.0
VERTICAL_VISC = 1.0

VMEM = pl.BlockSpec(memory_space=pltpu.VMEM)
SMEM = pl.BlockSpec(memory_space=pltpu.SMEM)
SUB = 8
SMALL = pltpu.CompilerParams(vmem_limit_bytes=4 * 2**20)
FIRST = pltpu.CompilerParams(vmem_limit_bytes=4 * 2**20)
LARGE = pltpu.CompilerParams(vmem_limit_bytes=8 * 2**20)


def lane_of(lanes):
    return lax.broadcasted_iota(jnp.int32, (SUB, lanes), 1)


def row_of(lanes):
    return lax.broadcasted_iota(jnp.int32, (SUB, lanes), 0)


def tall(value):
    missing = SUB - value.shape[0]
    if missing == 0:
        return value
    return jnp.concatenate([value, jnp.zeros((missing, value.shape[1]), value.dtype)], axis=0)


def edges_kernel(t_ref, s_ref, u_ref, v_ref, depth_ref, stress_ref, *outs):
    top_ref, bottom_ref, east_ref, west_ref, count_ref, wind_ref, first_ref = outs[:7]
    levels, width, lanes = t_ref.shape
    count_ref[...] = depth_ref[...].astype(jnp.float32)
    wind_ref[...] = stress_ref[...]
    even = lax.rem(lax.axis_index("lat"), 2) == 0
    lane = lane_of(lanes)
    for message, near, far in ((east_ref, width - 1, width - 2), (west_ref, 0, 1)):
        for place, field, column in (
            (0, t_ref, near),
            (1, t_ref, far),
            (2, s_ref, near),
            (3, s_ref, far),
            (4, u_ref, near),
            (5, v_ref, near),
        ):
            message[pl.ds(place * levels, levels), :] = field.reshape(levels * width, lanes)[pl.ds(column, levels, stride=width), :]
        depth = depth_ref[...].astype(jnp.float32)
        message[pl.ds(6 * levels, 8), :] = jnp.concatenate(
            [depth[near : near + 1], depth[far : far + 1]] * 4, axis=0
        )

    tops, bottoms = [], []
    for first, second, count in ((t_ref, s_ref, depth_ref), (u_ref, v_ref, None)):
        top = jnp.zeros((SUB, lanes), jnp.float32)
        bottom = jnp.zeros((SUB, lanes), jnp.float32)
        places = [(3 * k, first, k) for k in range(levels)]
        places += [(3 * (levels + k), second, k) for k in range(levels)]
        if count is not None:
            places.append((6 * levels, count, None))
        for start, ref, k in places:
            value = depth_ref[...].astype(jnp.float32) if k is None else ref[k]
            value = tall(value)
            here = jnp.logical_and(lane >= start, lane < start + 3)
            top = jnp.where(here, pltpu.roll(value, start + 3, 1), top)
            bottom = jnp.where(here, pltpu.roll(value, start, 1), bottom)
        bottom = jnp.where(lax.rem(lane, 3) == 2, pltpu.roll(bottom, 2, 1), bottom)
        tops.append(top[:width])
        bottoms.append(bottom[:width])
    for index in range(2):
        rows = pl.ds(index * width, width)
        top_ref[rows, :] = tops[index]
        bottom_ref[rows, :] = bottoms[index]
        first_ref[rows, :] = jnp.where(even, tops[index], bottoms[index])
        first_ref[pl.ds((2 + index) * width, width), :] = tops[index]
        for second_ref in outs[7:]:
            second_ref[rows, :] = jnp.where(even, bottoms[index], tops[index])


def corners_kernel(top_ref, east_base_ref, west_base_ref, seam_ref, *refs):
    north_ref, south_ref, east_ref, fold_ref, west_ref, rest_ref = refs[-6:]
    received = refs[:-6]
    lanes = top_ref.shape[1]
    width = top_ref.shape[0] // 2
    lat = lax.axis_index("lat")
    even = lax.rem(lat, 2) == 0
    halo = pl.ds(0, 2 * width)
    from_first = received[0][halo, :]
    from_second = received[1][...] if len(received) > 1 else jnp.zeros_like(from_first)
    north = jnp.where(even, from_first, from_second)
    south = jnp.where(even, from_second, from_first)
    north_ref[...] = north
    south_ref[...] = south
    base = west_base_ref.shape[0] - 8
    near = width - 1
    east_ref[pl.ds(0, base), :] = east_base_ref[pl.ds(0, base), :]
    east_ref[pl.ds(base, 8), :] = jnp.concatenate(
        [
            east_base_ref[pl.ds(base, 2), :],
            north[near : near + 1],
            north[width + near : width + near + 1],
            jnp.zeros((4, lanes), jnp.float32),
        ],
        axis=0,
    )
    west_ref[pl.ds(0, base), :] = west_base_ref[pl.ds(0, base), :]
    west_ref[pl.ds(base, 8), :] = jnp.concatenate(
        [
            west_base_ref[pl.ds(base, 2), :],
            north[0:1],
            north[width : width + 1],
            south[0:1],
            south[width : width + 1],
            jnp.zeros((2, lanes), jnp.float32),
        ],
        axis=0,
    )
    is_top = lat == lax.axis_size("lat") - 1
    code = seam_ref[0]
    corner = lax.rem(code, 2) == 1
    for index in range(2):
        rows = pl.ds(index * width, width)
        theirs = received[0][pl.ds((2 + index) * width, width), :]
        top = tall(jnp.where(is_top, top_ref[rows, :], theirs))
        fold_ref[rows, :] = jnp.where(corner, top, pltpu.roll(top, 1, 1))[:width]
    unused = fold_ref.shape[0] - 2 * width
    fold_ref[pl.ds(2 * width, unused), :] = jnp.zeros((unused, lanes), jnp.float32)
    rest_ref[...] = jnp.full((SUB, lanes), lax.rem(code, width), jnp.int32)


def mixing_constants(levels):
    gain = TIME_STEP * VERTICAL_VISC
    inner, last, ratio = [], [], 0.0
    for k in range(levels):
        above = gain if k > 0 else 0.0
        last.append(1.0 / (1.0 + above + above * ratio))
        pivot = 1.0 + above + gain + above * ratio
        inner.append(1.0 / pivot)
        ratio = -gain / pivot
    return inner, last


def keep_kernel(message_ref, kept_ref):
    kept_ref[...] = message_ref[...]


def mirror_kernel(own_tiles, own_ref, rest_ref, *refs):
    tiles, (mirror_ref, tiles_ref) = refs[:-2], refs[-2:]
    width = tiles_ref.shape[1] // 3
    rest = rest_ref[0, 0]
    lon = lax.axis_index("lon")
    for index in range(2):
        half = pl.ds(index * width, width)
        for place, ref in enumerate(tiles):
            tile = ref[half, :]
            for device in own_tiles[place]:
                tile = jnp.where(lon == device, own_ref[half, :], tile)
            tiles_ref[index, pl.ds(place * width, width), :] = tile
        for i in range(-1, width + 1):
            mirror_ref[index, pl.ds(i + 1, 1), :] = tiles_ref[
                index, pl.ds(width + rest - i, 1), :
            ]


def step_kernel(
    t_ref,
    s_ref,
    u_ref,
    v_ref,
    depth_ref,
    mix_ref,
    wind_ref,
    bottom_ref,
    north_ref,
    south_ref,
    west_ref,
    east_ref,
    mirror_ref,
    t_out,
    s_out,
    u_out,
    v_out,
    gx_t_ref,
    gx_s_ref,
    u2_ref,
    v2_ref,
    val_ref,
    near_ref,
    far_ref,
):
    levels, width, lanes = t_ref.shape
    lat = lax.axis_index("lat")
    lat_count = lax.axis_size("lat")
    is_top = lat == lat_count - 1
    lane = lane_of(lanes)
    row = row_of(lanes)
    depth_at = 6 * levels
    count_at = 6 * levels + 2

    def half(ref, index):
        return tall(ref[pl.ds(index * width, width), :])

    north, north_uv = (
        jnp.where(
            is_top, sign * tall(mirror_ref[index, pl.ds(1, width), :]), half(north_ref, index)
        )
        for index, sign in ((0, 1.0), (1, -1.0))
    )
    south, south_uv = half(south_ref, 0), half(south_ref, 1)
    bottom = half(bottom_ref, 0)

    def line(ref, index):
        return jnp.broadcast_to(ref[pl.ds(index, 1), :], (SUB, lanes))

    def mirror_line(index, i):
        return jnp.broadcast_to(mirror_ref[index, pl.ds(i + 1, 1), :], (SUB, lanes))

    nw = jnp.where(is_top, mirror_line(0, -1), line(west_ref, depth_at + 2))
    nw_uv = jnp.where(is_top, -mirror_line(1, -1), line(west_ref, depth_at + 3))
    ne = jnp.where(is_top, mirror_line(0, width), line(east_ref, depth_at + 2))
    se = line(east_ref, depth_at + 4)
    se_uv = line(east_ref, depth_at + 5)

    def to_east(value, halo):
        return jnp.where(row == width - 1, halo, pltpu.roll(value, SUB - 1, 0))

    def to_west(value, halo):
        return jnp.where(row == 0, halo, pltpu.roll(value, 1, 0))

    def to_north(value, halo):
        return jnp.where(lane == lanes - 1, halo, pltpu.roll(value, lanes - 1, 1))

    def to_south(value, halo):
        return jnp.where(lane == 0, halo, pltpu.roll(value, 1, 1))

    def at_north(message, index):
        return pltpu.roll(message, lanes - 1 - index, 1)

    def at_south(message, index):
        return pltpu.roll(message, (lanes - index) % lanes, 1)

    depth = tall(depth_ref[...])
    d_n = to_north(depth, at_north(north, count_at))
    d_nn = to_north(d_n, at_north(north, count_at - 1))
    d_s = to_south(depth, at_south(south, count_at))
    d_e = to_east(depth, line(east_ref, depth_at))
    d_ee = to_east(d_e, line(east_ref, depth_at + 1))
    d_w = to_west(depth, line(west_ref, depth_at))
    east_line = line(east_ref, depth_at)
    west_line = line(west_ref, depth_at)
    d_ne = to_east(d_n, to_north(east_line, at_north(ne, count_at)))
    d_se = to_east(d_s, to_south(east_line, at_south(se, count_at)))
    d_nw = to_west(d_n, to_north(west_line, at_north(nw, count_at)))
    d_u = jnp.minimum(depth, d_e)
    d_v = jnp.minimum(depth, d_n)
    u_neighbours = [
        jnp.minimum(d_u, d)
        for d in (
            jnp.minimum(d_e, d_ee),
            d_w,
            jnp.minimum(d_n, d_ne),
            jnp.minimum(d_s, d_se),
        )
    ]
    v_neighbours = [
        jnp.minimum(d_v, d)
        for d in (
            jnp.minimum(d_e, d_ne),
            jnp.minimum(d_w, d_nw),
            jnp.minimum(d_n, d_nn),
            d_s,
        )
    ]

    level_row = lax.broadcasted_iota(jnp.int32, (levels, lanes), 0)
    level_lane = lax.broadcasted_iota(jnp.int32, (levels, lanes), 1)
    wet_row = jnp.minimum(
        west_ref[pl.ds(depth_at, 1), :], depth_ref[pl.ds(0, 1), :]
    )
    wet_face = level_row.astype(jnp.float32) < wet_row
    u_west = west_ref[pl.ds(4 * levels, levels), :]
    for place, field, target in ((0, t_ref, gx_t_ref), (2, s_ref, gx_s_ref)):
        near = west_ref[pl.ds(place * levels, levels), :]
        far = west_ref[pl.ds((place + 1) * levels, levels), :]
        own = field[:, 0, :]
        face = u_west * (1.0 / 12.0) * (7.0 * (near + own) - (far + field[:, 1, :]))
        target[...] = jnp.where(wet_face, face - TRACER_DIFF * (own - near), 0.0)

    def column(corner, place):
        picked = jnp.where(level_lane == 3 * (place * levels + level_row) + 2, corner[0:1], 0.0)
        return jnp.sum(picked, axis=1, keepdims=True)

    u_corner = column(nw_uv, 0)
    v_corner = column(se_uv, 1)
    u2_ref[...] = u_west + jnp.where(
        level_lane == lanes - 1, u_corner, pltpu.roll(u_west, lanes - 1, 1)
    )
    v_east = east_ref[pl.ds(5 * levels, levels), :]
    v2_ref[...] = v_east + jnp.where(level_lane == 0, v_corner, pltpu.roll(v_east, 1, 1))

    in_block = jnp.where(lane < 3 * levels, lane, lane - 3 * levels).astype(jnp.float32)
    v_south = jnp.where(lane < 3 * levels, at_south(south_uv, 3 * levels), south_uv)
    both = south + bottom
    face = v_south * (1.0 / 12.0) * (7.0 * both - pltpu.roll(both, 1, 1))
    face = face - TRACER_DIFF * (bottom - south)
    wet_south = jnp.minimum(
        south[:, count_at : count_at + 1], bottom[:, count_at : count_at + 1]
    )
    face_south = jnp.where(in_block < 3.0 * wet_south, face, 0.0)

    third = lax.rem(lane, 3)
    near, near_uv = (
        jnp.where(third == 0, pltpu.roll(s, 1, 1), n)
        for n, s in ((north, south), (north_uv, south_uv))
    )
    far = jnp.where(third == 2, face_south, north)
    for place in range(2):
        for k in range(levels):
            spot = 3 * (place * levels + k) + 2
            near_ref[place * levels + k] = at_north(near, spot)
            near_ref[(place + 2) * levels + k] = at_north(near_uv, spot)
            far_ref[place * levels + k] = at_north(far, spot - 1)

    row_id = (lat * lanes + lane).astype(jnp.float32)
    total = float(lat_count * lanes)
    cor_u = 2.0 * (row_id + 0.5) / total - 1.0
    cor_v = 2.0 * (row_id + 1.0) / total - 1.0
    inner, last = mixing_constants(levels)
    gain = TIME_STEP * VERTICAL_VISC

    def masked(k, count, value):
        return jnp.where(float(k) < count, value, 0.0)

    px = jnp.zeros((SUB, lanes), jnp.float32)
    py = jnp.zeros((SUB, lanes), jnp.float32)
    above = None
    ratio = None
    values = None
    for k in range(levels):
        u = tall(u_ref[k])
        v = tall(v_ref[k])
        u_face = masked(k, d_u, u * (1.0 / 12.0))
        u_diff = masked(k, d_u, TRACER_DIFF)
        v_face = masked(k, d_v, v * (1.0 / 12.0))
        v_diff = masked(k, d_v, TRACER_DIFF)
        stars = []
        seen = []
        for place, field, gx_ref in ((0, t_ref, gx_t_ref), (2, s_ref, gx_s_ref)):
            near, far = place * levels + k, (place + 1) * levels + k
            c = tall(field[k])
            c_e = to_east(c, line(east_ref, near))
            c_ee = to_east(c_e, line(east_ref, far))
            c_w = to_west(c, line(west_ref, near))
            beyond = near_ref[place // 2 * levels + k]
            c_n = to_north(c, beyond)
            beyond_2 = far_ref[place // 2 * levels + k]
            c_nn = to_north(c_n, beyond_2)
            c_s = to_south(c, beyond)
            gx = u_face * (7.0 * (c + c_e) - (c_w + c_ee)) - u_diff * (c_e - c)
            gy = v_face * (7.0 * (c + c_n) - (c_s + c_nn)) - v_diff * (c_n - c)
            gx_w = to_west(gx, line(gx_ref, k))
            gy_s = to_south(gy, beyond_2)
            stars.append(c - TIME_STEP * masked(k, depth, (gx - gx_w) + (gy - gy_s)))
            seen.append((c, c_e, c_n))
        weights = THERMAL_EXPANSION, HALINE_CONTRACTION
        b, b_e, b_n = (
            masked(k, d, weights[0] * warm - weights[1] * salt)
            for d, warm, salt in zip((depth, d_e, d_n), seen[0], seen[1])
        )
        bx = b_e - b
        by = b_n - b
        px = px + bx
        py = py + by

        u_e = to_east(u, line(east_ref, 4 * levels + k))
        u_w = to_west(u, line(west_ref, 4 * levels + k))
        u_n = to_north(u, near_ref[2 * levels + k])
        u_s = to_south(u, near_ref[2 * levels + k])
        v_e = to_east(v, line(east_ref, 5 * levels + k))
        v_w = to_west(v, line(west_ref, 5 * levels + k))
        v_n = to_north(v, near_ref[3 * levels + k])
        v_s = to_south(v, near_ref[3 * levels + k])
        v2 = v + v_s
        u2 = u + u_n
        v_bar = 0.25 * (v2 + to_east(v2, line(v2_ref, k)))
        u_bar = 0.25 * (u2 + to_west(u2, line(u2_ref, k)))
        u_visc = sum(masked(k, d, n - u) for d, n in zip(u_neighbours, (u_e, u_w, u_n, u_s)))
        v_visc = sum(masked(k, d, n - v) for d, n in zip(v_neighbours, (v_e, v_w, v_n, v_s)))
        u_star = u + TIME_STEP * (cor_u * v_bar - (px - 0.5 * bx) + MOMENTUM_VISC * u_visc)
        v_star = v + TIME_STEP * (-cor_v * u_bar - (py - 0.5 * by) + MOMENTUM_VISC * v_visc)
        if k == 0:
            u_star = u_star + TIME_STEP * WIND_GAIN * tall(wind_ref[0])
            v_star = v_star + TIME_STEP * WIND_GAIN * tall(wind_ref[1])

        if k < levels - 1:
            below = masked(k + 1, depth, TIME_STEP * tall(mix_ref[k]))
        else:
            below = None
        pivot = 1.0
        if above is not None:
            pivot = pivot + above * (1.0 - ratio)
        if below is not None:
            pivot = pivot + below
        inverse = 1.0 / pivot

        def momentum_weight(count):
            weight = jnp.where(float(k) < count, last[k], 0.0)
            if k < levels - 1:
                weight = jnp.where(float(k + 1) < count, inner[k], weight)
            return weight

        rights = stars + [u_star, v_star]
        scales = [inverse, inverse, momentum_weight(d_u), momentum_weight(d_v)]
        if k > 0:
            gains = [above, above, gain, gain]
            rights = [right + g * value for right, g, value in zip(rights, gains, values)]
        values = [right * scale for right, scale in zip(rights, scales)]
        for index, value in enumerate(values):
            val_ref[index, k] = value
        if below is not None:
            ratio = below * inverse
            val_ref[4, k] = ratio
        above = below

    outs = (t_out, s_out, u_out, v_out)
    for k in range(levels - 1, -1, -1):
        if k < levels - 1:
            ratios = [val_ref[4, k], val_ref[4, k], gain * inner[k], gain * inner[k]]
            values = [val_ref[i, k] + ratios[i] * values[i] for i in range(4)]
        for out, value in zip(outs, values):
            out[k] = value[:width]


def shards(
    thermal_anomaly,
    saltiness_anomaly,
    zonal_current,
    meridional_current,
    bottom_ocean_layer,
    seam_axis_meridian,
    interface_diffusivity,
    atmospheric_forcing,
):
    levels, width, lanes = thermal_anomaly.shape
    lon_count = lax.axis_size("lon")
    lat_count = lax.axis_size("lat")
    fields = (thermal_anomaly, saltiness_anomaly, zonal_current, meridional_current)
    wind = atmospheric_forcing
    f32 = jnp.float32
    row_message = jax.ShapeDtypeStruct((2 * width, lanes), f32)
    column_message = jax.ShapeDtypeStruct((6 * levels + 8, lanes), f32)

    fold_message = jax.ShapeDtypeStruct((6 * levels + 16, lanes), f32)
    lat_pairs = [
        [(a, b) for i in range(start, lat_count - 1, 2) for a, b in ((i, i + 1), (i + 1, i))]
        for start in (0, 1)
    ]
    lat_pairs = [pairs for pairs in lat_pairs if pairs]
    top, bottom, eastward, westward, counts, stress, *messages = pl.pallas_call(
        edges_kernel,
        out_shape=[row_message] * 2
        + [column_message] * 2
        + [jax.ShapeDtypeStruct((width, lanes), f32), jax.ShapeDtypeStruct(wind.shape, f32)]
        + [jax.ShapeDtypeStruct((4 * width, lanes), f32), row_message][: len(lat_pairs)],
        in_specs=[VMEM] * 6,
        out_specs=[VMEM] * (6 + len(lat_pairs)),
        compiler_params=FIRST,
    )(*[pltpu.with_memory_space_constraint(x, pltpu.HBM) for x in (*fields, bottom_ocean_layer, wind)])
    received = [
        lax.ppermute(message, "lat", pairs) for message, pairs in zip(messages, lat_pairs)
    ]

    north, south, eastward, fold, westward, rest = pl.pallas_call(
        corners_kernel,
        out_shape=[row_message] * 2
        + [column_message, fold_message, column_message]
        + [jax.ShapeDtypeStruct((SUB, lanes), jnp.int32)],
        in_specs=[VMEM] * 3 + [SMEM] + [VMEM] * len(received),
        out_specs=[VMEM] * 6,
        compiler_params=SMALL,
    )(top, eastward, westward, seam_axis_meridian, *received)

    code = seam_axis_meridian[0]
    tile = lax.rem(lax.div(code, width), lon_count)
    three = (lax.rem(code, width) == width - 1).astype(jnp.int32)
    ring = [(i, (i + 1) % lon_count) for i in range(lon_count)]
    trade = [(i, i ^ 1) for i in range(lon_count)]
    pairs = [(i, i ^ 1) for i in range(lat_count)]

    def fold_pairs(*mirrors):
        rows = [*mirrors] + [trade] * (lat_count - len(mirrors))
        return [
            (a * lat_count + lat_count - 1 - row, b * lat_count + lat_count - 1 - row)
            for row, mirror in enumerate(rows)
            for a, b in mirror
        ]

    from_west = lax.ppermute(eastward, "lon", ring)
    keep = pl.pallas_call(
        keep_kernel,
        out_shape=column_message,
        in_specs=[VMEM],
        out_specs=VMEM,
        compiler_params=SMALL,
    )

    def reflect(code):
        own = [i for i in range(lon_count) if (code - i) % lon_count == i]
        if len(own) != 2:
            return [(i, (code - i) % lon_count) for i in range(lon_count)], []
        trade = {own[0]: own[1], own[1]: own[0]}
        return [(i, trade.get(i, (code - i) % lon_count)) for i in range(lon_count)], own

    def exchange(first, count):
        direct = first % 2
        mirrors, own_tiles = zip(*(reflect(first - 1 + d) for d in range(3)))
        mirror = pl.pallas_call(
            functools.partial(mirror_kernel, own_tiles),
            out_shape=jax.ShapeDtypeStruct((2, 16, lanes), f32),
            in_specs=[VMEM] * (2 + count),
            out_specs=VMEM,
            scratch_shapes=[pltpu.VMEM((2, 3 * width, lanes), f32)],
            compiler_params=SMALL,
        )

        def branch(fold, westward, rest):
            both = ("lon", "lat")
            tile = lax.ppermute(fold, both, fold_pairs(mirrors[direct], mirrors[1 - direct]))
            tiles = [tile, lax.ppermute(tile[: 2 * width], "lat", pairs)]
            if direct == 1:
                tiles = tiles[::-1]
            if count == 3:
                tiles.append(lax.ppermute(fold, both, fold_pairs(mirrors[2])))
            return (
                keep(lax.ppermute(westward, "lon", [(b, a) for a, b in ring])),
                mirror(fold, rest, *tiles),
            )

        return branch

    branches = [exchange(first, count) for first in range(lon_count) for count in (2, 3)]
    from_east, mirrored = lax.switch(
        tile * 2 + three, branches, fold, westward, rest
    )

    whole = jax.ShapeDtypeStruct((levels, width, lanes), f32)
    return pl.pallas_call(
        step_kernel,
        out_shape=[whole] * 4,
        in_specs=[VMEM] * 13,
        out_specs=[VMEM] * 4,
        compiler_params=LARGE,
        scratch_shapes=[pltpu.VMEM((levels, lanes), f32)] * 4
        + [pltpu.VMEM((5, levels, SUB, lanes), f32)]
        + [pltpu.VMEM((count * levels, SUB, lanes), f32) for count in (4, 2)],
    )(
        *fields,
        counts,
        interface_diffusivity,
        stress,
        bottom,
        north,
        south,
        from_west,
        from_east,
        mirrored,
    )


def solution(mesh):
    split = P(None, "lon", "lat")
    return jax.shard_map(
        shards,
        mesh=mesh,
        in_specs=(split, split, split, split, P("lon", "lat"), P(), split, split),
        out_specs=(split, split, split, split),
        check_vma=False,
    )
```

```python
import functools

import jax
import jax.numpy as jnp
from jax import lax
from jax.experimental import pallas as pl
from jax.experimental.pallas import tpu as pltpu
from jax.sharding import PartitionSpec as P

TIME_STEP = 0.2
TRACER_DIFF = 0.2
MOMENTUM_VISC = 0.2
THERMAL_EXPANSION = 0.5
HALINE_CONTRACTION = 0.4
WIND_GAIN = 2.0
VERTICAL_VISC = 1.0

VMEM = pl.BlockSpec(memory_space=pltpu.VMEM)
SMEM = pl.BlockSpec(memory_space=pltpu.SMEM)
SUB = 8
SMALL = pltpu.CompilerParams(vmem_limit_bytes=4 * 2**20)
FIRST = pltpu.CompilerParams(vmem_limit_bytes=4 * 2**20)
LARGE = pltpu.CompilerParams(vmem_limit_bytes=8 * 2**20)


def lane_of(lanes):
    return lax.broadcasted_iota(jnp.int32, (SUB, lanes), 1)


def row_of(lanes):
    return lax.broadcasted_iota(jnp.int32, (SUB, lanes), 0)


def tall(value):
    missing = SUB - value.shape[0]
    if missing == 0:
        return value
    return jnp.concatenate([value, jnp.zeros((missing, value.shape[1]), value.dtype)], axis=0)


def edges_kernel(t_ref, s_ref, u_ref, v_ref, depth_ref, stress_ref, *outs):
    top_ref, bottom_ref, east_ref, west_ref, count_ref, wind_ref, first_ref = outs[:7]
    levels, width, lanes = t_ref.shape
    count_ref[...] = depth_ref[...].astype(jnp.float32)
    wind_ref[...] = stress_ref[...]
    even = lax.rem(lax.axis_index("lat"), 2) == 0
    lane = lane_of(lanes)
    for message, near, far in ((east_ref, width - 1, width - 2), (west_ref, 0, 1)):
        for place, field, column in (
            (0, t_ref, near),
            (1, t_ref, far),
            (2, s_ref, near),
            (3, s_ref, far),
            (4, u_ref, near),
            (5, v_ref, near),
        ):
            message[pl.ds(place * levels, levels), :] = field[:, column, :]
        depth = depth_ref[...].astype(jnp.float32)
        message[pl.ds(6 * levels, 8), :] = jnp.concatenate(
            [depth[near : near + 1], depth[far : far + 1]] * 4, axis=0
        )

    tops, bottoms = [], []
    for first, second, count in ((t_ref, s_ref, depth_ref), (u_ref, v_ref, None)):
        top = jnp.zeros((SUB, lanes), jnp.float32)
        bottom = jnp.zeros((SUB, lanes), jnp.float32)
        places = [(3 * k, first, k) for k in range(levels)]
        places += [(3 * (levels + k), second, k) for k in range(levels)]
        if count is not None:
            places.append((6 * levels, count, None))
        for start, ref, k in places:
            value = depth_ref[...].astype(jnp.float32) if k is None else ref[k]
            value = tall(value)
            here = jnp.logical_and(lane >= start, lane < start + 3)
            top = jnp.where(here, pltpu.roll(value, start + 3, 1), top)
            bottom = jnp.where(here, pltpu.roll(value, start, 1), bottom)
        bottom = jnp.where(lax.rem(lane, 3) == 2, pltpu.roll(bottom, 2, 1), bottom)
        tops.append(top[:width])
        bottoms.append(bottom[:width])
    for index in range(2):
        rows = pl.ds(index * width, width)
        top_ref[rows, :] = tops[index]
        bottom_ref[rows, :] = bottoms[index]
        first_ref[rows, :] = jnp.where(even, tops[index], bottoms[index])
        first_ref[pl.ds((2 + index) * width, width), :] = tops[index]
        for second_ref in outs[7:]:
            second_ref[rows, :] = jnp.where(even, bottoms[index], tops[index])


def corners_kernel(top_ref, east_base_ref, west_base_ref, seam_ref, *refs):
    north_ref, south_ref, east_ref, fold_ref, west_ref, rest_ref = refs[-6:]
    received = refs[:-6]
    lanes = top_ref.shape[1]
    width = top_ref.shape[0] // 2
    lat = lax.axis_index("lat")
    even = lax.rem(lat, 2) == 0
    halo = pl.ds(0, 2 * width)
    from_first = received[0][halo, :]
    from_second = received[1][...] if len(received) > 1 else jnp.zeros_like(from_first)
    north = jnp.where(even, from_first, from_second)
    south = jnp.where(even, from_second, from_first)
    north_ref[...] = north
    south_ref[...] = south
    base = west_base_ref.shape[0] - 8
    near = width - 1
    east_ref[pl.ds(0, base), :] = east_base_ref[pl.ds(0, base), :]
    east_ref[pl.ds(base, 8), :] = jnp.concatenate(
        [
            east_base_ref[pl.ds(base, 2), :],
            north[near : near + 1],
            north[width + near : width + near + 1],
            jnp.zeros((4, lanes), jnp.float32),
        ],
        axis=0,
    )
    west_ref[pl.ds(0, base), :] = west_base_ref[pl.ds(0, base), :]
    west_ref[pl.ds(base, 8), :] = jnp.concatenate(
        [
            west_base_ref[pl.ds(base, 2), :],
            north[0:1],
            north[width : width + 1],
            south[0:1],
            south[width : width + 1],
            jnp.zeros((2, lanes), jnp.float32),
        ],
        axis=0,
    )
    is_top = lat == lax.axis_size("lat") - 1
    code = seam_ref[0]
    corner = lax.rem(code, 2) == 1
    for index in range(2):
        rows = pl.ds(index * width, width)
        theirs = received[0][pl.ds((2 + index) * width, width), :]
        top = tall(jnp.where(is_top, top_ref[rows, :], theirs))
        fold_ref[rows, :] = jnp.where(corner, top, pltpu.roll(top, 1, 1))[:width]
    unused = fold_ref.shape[0] - 2 * width
    fold_ref[pl.ds(2 * width, unused), :] = jnp.zeros((unused, lanes), jnp.float32)
    rest_ref[...] = jnp.full((SUB, lanes), lax.rem(code, width), jnp.int32)


def mixing_constants(levels):
    gain = TIME_STEP * VERTICAL_VISC
    inner, last, ratio = [], [], 0.0
    for k in range(levels):
        above = gain if k > 0 else 0.0
        last.append(1.0 / (1.0 + above + above * ratio))
        pivot = 1.0 + above + gain + above * ratio
        inner.append(1.0 / pivot)
        ratio = -gain / pivot
    return inner, last


def keep_kernel(message_ref, kept_ref):
    kept_ref[...] = message_ref[...]


def mirror_kernel(own_tiles, own_ref, rest_ref, *refs):
    tiles, (mirror_ref, tiles_ref) = refs[:-2], refs[-2:]
    width = tiles_ref.shape[1] // 3
    rest = rest_ref[0, 0]
    lon = lax.axis_index("lon")
    for index in range(2):
        half = pl.ds(index * width, width)
        for place, ref in enumerate(tiles):
            tile = ref[half, :]
            for device in own_tiles[place]:
                tile = jnp.where(lon == device, own_ref[half, :], tile)
            tiles_ref[index, pl.ds(place * width, width), :] = tile
        for i in range(-1, width + 1):
            mirror_ref[index, pl.ds(i + 1, 1), :] = tiles_ref[
                index, pl.ds(width + rest - i, 1), :
            ]


def step_kernel(
    t_ref,
    s_ref,
    u_ref,
    v_ref,
    depth_ref,
    mix_ref,
    wind_ref,
    bottom_ref,
    north_ref,
    south_ref,
    west_ref,
    east_ref,
    mirror_ref,
    t_out,
    s_out,
    u_out,
    v_out,
    gx_t_ref,
    gx_s_ref,
    u2_ref,
    v2_ref,
    val_ref,
    near_ref,
    far_ref,
):
    levels, width, lanes = t_ref.shape
    lat = lax.axis_index("lat")
    lat_count = lax.axis_size("lat")
    is_top = lat == lat_count - 1
    lane = lane_of(lanes)
    row = row_of(lanes)
    depth_at = 6 * levels
    count_at = 6 * levels + 2

    def half(ref, index):
        return tall(ref[pl.ds(index * width, width), :])

    north, north_uv = (
        jnp.where(
            is_top, sign * tall(mirror_ref[index, pl.ds(1, width), :]), half(north_ref, index)
        )
        for index, sign in ((0, 1.0), (1, -1.0))
    )
    south, south_uv = half(south_ref, 0), half(south_ref, 1)
    bottom = half(bottom_ref, 0)

    def line(ref, index):
        return jnp.broadcast_to(ref[pl.ds(index, 1), :], (SUB, lanes))

    def mirror_line(index, i):
        return jnp.broadcast_to(mirror_ref[index, pl.ds(i + 1, 1), :], (SUB, lanes))

    nw = jnp.where(is_top, mirror_line(0, -1), line(west_ref, depth_at + 2))
    nw_uv = jnp.where(is_top, -mirror_line(1, -1), line(west_ref, depth_at + 3))
    ne = jnp.where(is_top, mirror_line(0, width), line(east_ref, depth_at + 2))
    se = line(east_ref, depth_at + 4)
    se_uv = line(east_ref, depth_at + 5)

    def to_east(value, halo):
        return jnp.where(row == width - 1, halo, pltpu.roll(value, SUB - 1, 0))

    def to_west(value, halo):
        return jnp.where(row == 0, halo, pltpu.roll(value, 1, 0))

    def to_north(value, halo):
        return jnp.where(lane == lanes - 1, halo, pltpu.roll(value, lanes - 1, 1))

    def to_south(value, halo):
        return jnp.where(lane == 0, halo, pltpu.roll(value, 1, 1))

    def at_north(message, index):
        return pltpu.roll(message, lanes - 1 - index, 1)

    def at_south(message, index):
        return pltpu.roll(message, (lanes - index) % lanes, 1)

    depth = tall(depth_ref[...])
    d_n = to_north(depth, at_north(north, count_at))
    d_nn = to_north(d_n, at_north(north, count_at - 1))
    d_s = to_south(depth, at_south(south, count_at))
    d_e = to_east(depth, line(east_ref, depth_at))
    d_ee = to_east(d_e, line(east_ref, depth_at + 1))
    d_w = to_west(depth, line(west_ref, depth_at))
    east_line = line(east_ref, depth_at)
    west_line = line(west_ref, depth_at)
    d_ne = to_east(d_n, to_north(east_line, at_north(ne, count_at)))
    d_se = to_east(d_s, to_south(east_line, at_south(se, count_at)))
    d_nw = to_west(d_n, to_north(west_line, at_north(nw, count_at)))
    d_u = jnp.minimum(depth, d_e)
    d_v = jnp.minimum(depth, d_n)
    u_neighbours = [
        jnp.minimum(d_u, d)
        for d in (
            jnp.minimum(d_e, d_ee),
            d_w,
            jnp.minimum(d_n, d_ne),
            jnp.minimum(d_s, d_se),
        )
    ]
    v_neighbours = [
        jnp.minimum(d_v, d)
        for d in (
            jnp.minimum(d_e, d_ne),
            jnp.minimum(d_w, d_nw),
            jnp.minimum(d_n, d_nn),
            d_s,
        )
    ]

    level_row = lax.broadcasted_iota(jnp.int32, (levels, lanes), 0)
    level_lane = lax.broadcasted_iota(jnp.int32, (levels, lanes), 1)
    wet_row = jnp.minimum(
        west_ref[pl.ds(depth_at, 1), :], depth_ref[pl.ds(0, 1), :]
    )
    wet_face = level_row.astype(jnp.float32) < wet_row
    u_west = west_ref[pl.ds(4 * levels, levels), :]
    for place, field, target in ((0, t_ref, gx_t_ref), (2, s_ref, gx_s_ref)):
        near = west_ref[pl.ds(place * levels, levels), :]
        far = west_ref[pl.ds((place + 1) * levels, levels), :]
        own = field[:, 0, :]
        face = u_west * (1.0 / 12.0) * (7.0 * (near + own) - (far + field[:, 1, :]))
        target[...] = jnp.where(wet_face, face - TRACER_DIFF * (own - near), 0.0)

    def column(corner, place):
        picked = jnp.where(level_lane == 3 * (place * levels + level_row) + 2, corner[0:1], 0.0)
        return jnp.sum(picked, axis=1, keepdims=True)

    u_corner = column(nw_uv, 0)
    v_corner = column(se_uv, 1)
    u2_ref[...] = u_west + jnp.where(
        level_lane == lanes - 1, u_corner, pltpu.roll(u_west, lanes - 1, 1)
    )
    v_east = east_ref[pl.ds(5 * levels, levels), :]
    v2_ref[...] = v_east + jnp.where(level_lane == 0, v_corner, pltpu.roll(v_east, 1, 1))

    in_block = jnp.where(lane < 3 * levels, lane, lane - 3 * levels).astype(jnp.float32)
    v_south = jnp.where(lane < 3 * levels, at_south(south_uv, 3 * levels), south_uv)
    both = south + bottom
    face = v_south * (1.0 / 12.0) * (7.0 * both - pltpu.roll(both, 1, 1))
    face = face - TRACER_DIFF * (bottom - south)
    wet_south = jnp.minimum(
        south[:, count_at : count_at + 1], bottom[:, count_at : count_at + 1]
    )
    face_south = jnp.where(in_block < 3.0 * wet_south, face, 0.0)

    third = lax.rem(lane, 3)
    near, near_uv = (
        jnp.where(third == 0, pltpu.roll(s, 1, 1), n)
        for n, s in ((north, south), (north_uv, south_uv))
    )
    far = jnp.where(third == 2, face_south, north)
    for place in range(2):
        for k in range(levels):
            spot = 3 * (place * levels + k) + 2
            near_ref[place * levels + k] = at_north(near, spot)
            near_ref[(place + 2) * levels + k] = at_north(near_uv, spot)
            far_ref[place * levels + k] = at_north(far, spot - 1)

    row_id = (lat * lanes + lane).astype(jnp.float32)
    total = float(lat_count * lanes)
    cor_u = 2.0 * (row_id + 0.5) / total - 1.0
    cor_v = 2.0 * (row_id + 1.0) / total - 1.0
    inner, last = mixing_constants(levels)
    gain = TIME_STEP * VERTICAL_VISC

    def masked(k, count, value):
        return jnp.where(float(k) < count, value, 0.0)

    px = jnp.zeros((SUB, lanes), jnp.float32)
    py = jnp.zeros((SUB, lanes), jnp.float32)
    above = None
    ratio = None
    values = None
    for k in range(levels):
        u = tall(u_ref[k])
        v = tall(v_ref[k])
        u_face = masked(k, d_u, u * (1.0 / 12.0))
        u_diff = masked(k, d_u, TRACER_DIFF)
        v_face = masked(k, d_v, v * (1.0 / 12.0))
        v_diff = masked(k, d_v, TRACER_DIFF)
        stars = []
        seen = []
        for place, field, gx_ref in ((0, t_ref, gx_t_ref), (2, s_ref, gx_s_ref)):
            near, far = place * levels + k, (place + 1) * levels + k
            c = tall(field[k])
            c_e = to_east(c, line(east_ref, near))
            c_ee = to_east(c_e, line(east_ref, far))
            c_w = to_west(c, line(west_ref, near))
            beyond = near_ref[place // 2 * levels + k]
            c_n = to_north(c, beyond)
            beyond_2 = far_ref[place // 2 * levels + k]
            c_nn = to_north(c_n, beyond_2)
            c_s = to_south(c, beyond)
            gx = u_face * (7.0 * (c + c_e) - (c_w + c_ee)) - u_diff * (c_e - c)
            gy = v_face * (7.0 * (c + c_n) - (c_s + c_nn)) - v_diff * (c_n - c)
            gx_w = to_west(gx, line(gx_ref, k))
            gy_s = to_south(gy, beyond_2)
            stars.append(c - TIME_STEP * masked(k, depth, (gx - gx_w) + (gy - gy_s)))
            seen.append((c, c_e, c_n))
        weights = THERMAL_EXPANSION, HALINE_CONTRACTION
        b, b_e, b_n = (
            masked(k, d, weights[0] * warm - weights[1] * salt)
            for d, warm, salt in zip((depth, d_e, d_n), seen[0], seen[1])
        )
        bx = b_e - b
        by = b_n - b
        px = px + bx
        py = py + by

        u_e = to_east(u, line(east_ref, 4 * levels + k))
        u_w = to_west(u, line(west_ref, 4 * levels + k))
        u_n = to_north(u, near_ref[2 * levels + k])
        u_s = to_south(u, near_ref[2 * levels + k])
        v_e = to_east(v, line(east_ref, 5 * levels + k))
        v_w = to_west(v, line(west_ref, 5 * levels + k))
        v_n = to_north(v, near_ref[3 * levels + k])
        v_s = to_south(v, near_ref[3 * levels + k])
        v2 = v + v_s
        u2 = u + u_n
        v_bar = 0.25 * (v2 + to_east(v2, line(v2_ref, k)))
        u_bar = 0.25 * (u2 + to_west(u2, line(u2_ref, k)))
        u_visc = sum(masked(k, d, n - u) for d, n in zip(u_neighbours, (u_e, u_w, u_n, u_s)))
        v_visc = sum(masked(k, d, n - v) for d, n in zip(v_neighbours, (v_e, v_w, v_n, v_s)))
        u_star = u + TIME_STEP * (cor_u * v_bar - (px - 0.5 * bx) + MOMENTUM_VISC * u_visc)
        v_star = v + TIME_STEP * (-cor_v * u_bar - (py - 0.5 * by) + MOMENTUM_VISC * v_visc)
        if k == 0:
            u_star = u_star + TIME_STEP * WIND_GAIN * tall(wind_ref[0])
            v_star = v_star + TIME_STEP * WIND_GAIN * tall(wind_ref[1])

        if k < levels - 1:
            below = masked(k + 1, depth, TIME_STEP * tall(mix_ref[k]))
        else:
            below = None
        pivot = 1.0
        if above is not None:
            pivot = pivot + above * (1.0 - ratio)
        if below is not None:
            pivot = pivot + below
        inverse = 1.0 / pivot

        def momentum_weight(count):
            weight = jnp.where(float(k) < count, last[k], 0.0)
            if k < levels - 1:
                weight = jnp.where(float(k + 1) < count, inner[k], weight)
            return weight

        rights = stars + [u_star, v_star]
        scales = [inverse, inverse, momentum_weight(d_u), momentum_weight(d_v)]
        if k > 0:
            gains = [above, above, gain, gain]
            rights = [right + g * value for right, g, value in zip(rights, gains, values)]
        values = [right * scale for right, scale in zip(rights, scales)]
        for index, value in enumerate(values):
            val_ref[index, k] = value
        if below is not None:
            ratio = below * inverse
            val_ref[4, k] = ratio
        above = below

    outs = (t_out, s_out, u_out, v_out)
    for k in range(levels - 1, -1, -1):
        if k < levels - 1:
            ratios = [val_ref[4, k], val_ref[4, k], gain * inner[k], gain * inner[k]]
            values = [val_ref[i, k] + ratios[i] * values[i] for i in range(4)]
        for out, value in zip(outs, values):
            out[k] = value[:width]


def shards(
    thermal_anomaly,
    saltiness_anomaly,
    zonal_current,
    meridional_current,
    bottom_ocean_layer,
    seam_axis_meridian,
    interface_diffusivity,
    atmospheric_forcing,
):
    levels, width, lanes = thermal_anomaly.shape
    lon_count = lax.axis_size("lon")
    lat_count = lax.axis_size("lat")
    fields = (thermal_anomaly, saltiness_anomaly, zonal_current, meridional_current)
    wind = atmospheric_forcing
    f32 = jnp.float32
    row_message = jax.ShapeDtypeStruct((2 * width, lanes), f32)
    column_message = jax.ShapeDtypeStruct((6 * levels + 8, lanes), f32)

    fold_message = jax.ShapeDtypeStruct((6 * levels + 16, lanes), f32)
    lat_pairs = [
        [(a, b) for i in range(start, lat_count - 1, 2) for a, b in ((i, i + 1), (i + 1, i))]
        for start in (0, 1)
    ]
    lat_pairs = [pairs for pairs in lat_pairs if pairs]
    top, bottom, eastward, westward, counts, stress, *messages = pl.pallas_call(
        edges_kernel,
        out_shape=[row_message] * 2
        + [column_message] * 2
        + [jax.ShapeDtypeStruct((width, lanes), f32), jax.ShapeDtypeStruct(wind.shape, f32)]
        + [jax.ShapeDtypeStruct((4 * width, lanes), f32), row_message][: len(lat_pairs)],
        in_specs=[VMEM] * 6,
        out_specs=[VMEM] * (6 + len(lat_pairs)),
        compiler_params=FIRST,
    )(*[pltpu.with_memory_space_constraint(x, pltpu.HBM) for x in (*fields, bottom_ocean_layer, wind)])
    received = [
        lax.ppermute(message, "lat", pairs) for message, pairs in zip(messages, lat_pairs)
    ]

    north, south, eastward, fold, westward, rest = pl.pallas_call(
        corners_kernel,
        out_shape=[row_message] * 2
        + [column_message, fold_message, column_message]
        + [jax.ShapeDtypeStruct((SUB, lanes), jnp.int32)],
        in_specs=[VMEM] * 3 + [SMEM] + [VMEM] * len(received),
        out_specs=[VMEM] * 6,
        compiler_params=SMALL,
    )(top, eastward, westward, seam_axis_meridian, *received)

    code = seam_axis_meridian[0]
    tile = lax.rem(lax.div(code, width), lon_count)
    three = (lax.rem(code, width) == width - 1).astype(jnp.int32)
    ring = [(i, (i + 1) % lon_count) for i in range(lon_count)]
    trade = [(i, i ^ 1) for i in range(lon_count)]
    pairs = [(i, i ^ 1) for i in range(lat_count)]

    def fold_pairs(*mirrors):
        rows = [*mirrors] + [trade] * (lat_count - len(mirrors))
        return [
            (a * lat_count + lat_count - 1 - row, b * lat_count + lat_count - 1 - row)
            for row, mirror in enumerate(rows)
            for a, b in mirror
        ]

    from_west = lax.ppermute(eastward, "lon", ring)
    keep = pl.pallas_call(
        keep_kernel,
        out_shape=column_message,
        in_specs=[VMEM],
        out_specs=VMEM,
        compiler_params=SMALL,
    )

    def reflect(code):
        own = [i for i in range(lon_count) if (code - i) % lon_count == i]
        if len(own) != 2:
            return [(i, (code - i) % lon_count) for i in range(lon_count)], []
        trade = {own[0]: own[1], own[1]: own[0]}
        return [(i, trade.get(i, (code - i) % lon_count)) for i in range(lon_count)], own

    def exchange(first, count):
        direct = first % 2
        mirrors, own_tiles = zip(*(reflect(first - 1 + d) for d in range(3)))
        mirror = pl.pallas_call(
            functools.partial(mirror_kernel, own_tiles),
            out_shape=jax.ShapeDtypeStruct((2, 16, lanes), f32),
            in_specs=[VMEM] * (2 + count),
            out_specs=VMEM,
            scratch_shapes=[pltpu.VMEM((2, 3 * width, lanes), f32)],
            compiler_params=SMALL,
        )

        def branch(fold, westward, rest):
            both = ("lon", "lat")
            tile = lax.ppermute(fold, both, fold_pairs(mirrors[direct], mirrors[1 - direct]))
            tiles = [tile, lax.ppermute(tile[: 2 * width], "lat", pairs)]
            if direct == 1:
                tiles = tiles[::-1]
            if count == 3:
                tiles.append(lax.ppermute(fold, both, fold_pairs(mirrors[2])))
            return (
                keep(lax.ppermute(westward, "lon", [(b, a) for a, b in ring])),
                mirror(fold, rest, *tiles),
            )

        return branch

    branches = [exchange(first, count) for first in range(lon_count) for count in (2, 3)]
    from_east, mirrored = lax.switch(
        tile * 2 + three, branches, fold, westward, rest
    )

    whole = jax.ShapeDtypeStruct((levels, width, lanes), f32)
    return pl.pallas_call(
        step_kernel,
        out_shape=[whole] * 4,
        in_specs=[VMEM] * 13,
        out_specs=[VMEM] * 4,
        compiler_params=LARGE,
        scratch_shapes=[pltpu.VMEM((levels, lanes), f32)] * 4
        + [pltpu.VMEM((5, levels, SUB, lanes), f32)]
        + [pltpu.VMEM((count * levels, SUB, lanes), f32) for count in (4, 2)],
    )(
        *fields,
        counts,
        interface_diffusivity,
        stress,
        bottom,
        north,
        south,
        from_west,
        from_east,
        mirrored,
    )


def solution(mesh):
    split = P(None, "lon", "lat")
    return jax.shard_map(
        shards,
        mesh=mesh,
        in_specs=(split, split, split, split, P("lon", "lat"), P(), split, split),
        out_specs=(split, split, split, split),
        check_vma=False,
    )
```

```python
import functools

import jax
import jax.numpy as jnp
from jax import lax
from jax.experimental import pallas as pl
from jax.experimental.pallas import tpu as pltpu
from jax.sharding import PartitionSpec as P

TIME_STEP = 0.2
TRACER_DIFF = 0.2
MOMENTUM_VISC = 0.2
THERMAL_EXPANSION = 0.5
HALINE_CONTRACTION = 0.4
WIND_GAIN = 2.0
VERTICAL_VISC = 1.0

VMEM = pl.BlockSpec(memory_space=pltpu.VMEM)
SMEM = pl.BlockSpec(memory_space=pltpu.SMEM)
SUB = 8
SMALL = pltpu.CompilerParams(vmem_limit_bytes=4 * 2**20)
FIRST = pltpu.CompilerParams(vmem_limit_bytes=4 * 2**20)
LARGE = pltpu.CompilerParams(vmem_limit_bytes=8 * 2**20)


def lane_of(lanes):
    return lax.broadcasted_iota(jnp.int32, (SUB, lanes), 1)


def row_of(lanes):
    return lax.broadcasted_iota(jnp.int32, (SUB, lanes), 0)


def tall(value):
    missing = SUB - value.shape[0]
    if missing == 0:
        return value
    return jnp.concatenate([value, jnp.zeros((missing, value.shape[1]), value.dtype)], axis=0)


def edges_kernel(t_ref, s_ref, u_ref, v_ref, depth_ref, stress_ref, *outs):
    top_ref, bottom_ref, east_ref, west_ref, count_ref, wind_ref, first_ref = outs[:7]
    levels, width, lanes = t_ref.shape
    count_ref[...] = depth_ref[...].astype(jnp.float32)
    wind_ref[...] = stress_ref[...]
    even = lax.rem(lax.axis_index("lat"), 2) == 0
    lane = lane_of(lanes)
    for message, near, far in ((east_ref, width - 1, width - 2), (west_ref, 0, 1)):
        for place, field, column in (
            (0, t_ref, near),
            (1, t_ref, far),
            (2, s_ref, near),
            (3, s_ref, far),
            (4, u_ref, near),
            (5, v_ref, near),
        ):
            message[pl.ds(place * levels, levels), :] = field[:, column, :]
        depth = depth_ref[...].astype(jnp.float32)
        message[pl.ds(6 * levels, 8), :] = jnp.concatenate(
            [depth[near : near + 1], depth[far : far + 1]] * 4, axis=0
        )

    tops, bottoms = [], []
    for first, second, count in ((t_ref, s_ref, depth_ref), (u_ref, v_ref, None)):
        top = jnp.zeros((SUB, lanes), jnp.float32)
        bottom = jnp.zeros((SUB, lanes), jnp.float32)
        places = [(3 * (levels - 1 - k), first, k) for k in range(levels)]
        places += [(3 * (2 * levels - 1 - k), second, k) for k in range(levels)]
        if count is not None:
            places.append((6 * levels, count, None))
        for start, ref, k in places:
            value = depth_ref[...].astype(jnp.float32) if k is None else ref[k]
            value = tall(value)
            here = jnp.logical_and(lane >= start, lane < start + 3)
            top = jnp.where(here, pltpu.roll(value, start + 3, 1), top)
            bottom = jnp.where(here, pltpu.roll(value, start, 1), bottom)
        bottom = jnp.where(lax.rem(lane, 3) == 2, pltpu.roll(bottom, 2, 1), bottom)
        tops.append(top[:width])
        bottoms.append(bottom[:width])
    for index in range(2):
        rows = pl.ds(index * width, width)
        top_ref[rows, :] = tops[index]
        bottom_ref[rows, :] = bottoms[index]
        first_ref[rows, :] = jnp.where(even, tops[index], bottoms[index])
        first_ref[pl.ds((2 + index) * width, width), :] = tops[index]
        for second_ref in outs[7:]:
            second_ref[rows, :] = jnp.where(even, bottoms[index], tops[index])


def corners_kernel(top_ref, east_base_ref, west_base_ref, seam_ref, *refs):
    north_ref, south_ref, east_ref, fold_ref, west_ref, rest_ref = refs[-6:]
    received = refs[:-6]
    lanes = top_ref.shape[1]
    width = top_ref.shape[0] // 2
    lat = lax.axis_index("lat")
    even = lax.rem(lat, 2) == 0
    halo = pl.ds(0, 2 * width)
    from_first = received[0][halo, :]
    from_second = received[1][...] if len(received) > 1 else jnp.zeros_like(from_first)
    north = jnp.where(even, from_first, from_second)
    south = jnp.where(even, from_second, from_first)
    north_ref[...] = north
    south_ref[...] = south
    base = west_base_ref.shape[0] - 8
    near = width - 1
    east_ref[pl.ds(0, base), :] = east_base_ref[pl.ds(0, base), :]
    east_ref[pl.ds(base, 8), :] = jnp.concatenate(
        [
            east_base_ref[pl.ds(base, 2), :],
            north[near : near + 1],
            north[width + near : width + near + 1],
            jnp.zeros((4, lanes), jnp.float32),
        ],
        axis=0,
    )
    west_ref[pl.ds(0, base), :] = west_base_ref[pl.ds(0, base), :]
    west_ref[pl.ds(base, 8), :] = jnp.concatenate(
        [
            west_base_ref[pl.ds(base, 2), :],
            north[0:1],
            north[width : width + 1],
            south[0:1],
            south[width : width + 1],
            jnp.zeros((2, lanes), jnp.float32),
        ],
        axis=0,
    )
    is_top = lat == lax.axis_size("lat") - 1
    code = seam_ref[0]
    corner = lax.rem(code, 2) == 1
    for index in range(2):
        rows = pl.ds(index * width, width)
        theirs = received[0][pl.ds((2 + index) * width, width), :]
        top = tall(jnp.where(is_top, top_ref[rows, :], theirs))
        fold_ref[rows, :] = jnp.where(corner, top, pltpu.roll(top, 1, 1))[:width]
    unused = fold_ref.shape[0] - 2 * width
    fold_ref[pl.ds(2 * width, unused), :] = jnp.zeros((unused, lanes), jnp.float32)
    rest_ref[...] = jnp.full((SUB, lanes), lax.rem(code, width), jnp.int32)


def mixing_constants(levels):
    gain = TIME_STEP * VERTICAL_VISC
    inner, last, ratio = [], [], 0.0
    for k in range(levels):
        above = gain if k > 0 else 0.0
        last.append(1.0 / (1.0 + above + above * ratio))
        pivot = 1.0 + above + gain + above * ratio
        inner.append(1.0 / pivot)
        ratio = -gain / pivot
    return inner, last


def keep_kernel(message_ref, kept_ref):
    kept_ref[...] = message_ref[...]


def mirror_kernel(own_tiles, own_ref, rest_ref, *refs):
    tiles, (mirror_ref, tiles_ref) = refs[:-2], refs[-2:]
    width = tiles_ref.shape[1] // 3
    rest = rest_ref[0, 0]
    lon = lax.axis_index("lon")
    for index in range(2):
        half = pl.ds(index * width, width)
        for place, ref in enumerate(tiles):
            tile = ref[half, :]
            for device in own_tiles[place]:
                tile = jnp.where(lon == device, own_ref[half, :], tile)
            tiles_ref[index, pl.ds(place * width, width), :] = tile
        for i in range(-1, width + 1):
            mirror_ref[index, pl.ds(i + 1, 1), :] = tiles_ref[
                index, pl.ds(width + rest - i, 1), :
            ]


def step_kernel(
    t_ref,
    s_ref,
    u_ref,
    v_ref,
    depth_ref,
    mix_ref,
    wind_ref,
    bottom_ref,
    north_ref,
    south_ref,
    west_ref,
    east_ref,
    mirror_ref,
    t_out,
    s_out,
    u_out,
    v_out,
    gx_t_ref,
    gx_s_ref,
    u2_ref,
    v2_ref,
    val_ref,
    near_ref,
    far_ref,
):
    levels, width, lanes = t_ref.shape
    lat = lax.axis_index("lat")
    lat_count = lax.axis_size("lat")
    is_top = lat == lat_count - 1
    lane = lane_of(lanes)
    row = row_of(lanes)
    depth_at = 6 * levels
    count_at = 6 * levels + 2

    def half(ref, index):
        return tall(ref[pl.ds(index * width, width), :])

    north, north_uv = (
        jnp.where(
            is_top, sign * tall(mirror_ref[index, pl.ds(1, width), :]), half(north_ref, index)
        )
        for index, sign in ((0, 1.0), (1, -1.0))
    )
    south, south_uv = half(south_ref, 0), half(south_ref, 1)
    bottom = half(bottom_ref, 0)

    def line(ref, index):
        return jnp.broadcast_to(ref[pl.ds(index, 1), :], (SUB, lanes))

    def mirror_line(index, i):
        return jnp.broadcast_to(mirror_ref[index, pl.ds(i + 1, 1), :], (SUB, lanes))

    nw = jnp.where(is_top, mirror_line(0, -1), line(west_ref, depth_at + 2))
    nw_uv = jnp.where(is_top, -mirror_line(1, -1), line(west_ref, depth_at + 3))
    ne = jnp.where(is_top, mirror_line(0, width), line(east_ref, depth_at + 2))
    se = line(east_ref, depth_at + 4)
    se_uv = line(east_ref, depth_at + 5)

    def to_east(value, halo):
        return jnp.where(row == width - 1, halo, pltpu.roll(value, SUB - 1, 0))

    def to_west(value, halo):
        return jnp.where(row == 0, halo, pltpu.roll(value, 1, 0))

    def to_north(value, halo):
        return jnp.where(lane == lanes - 1, halo, pltpu.roll(value, lanes - 1, 1))

    def to_south(value, halo):
        return jnp.where(lane == 0, halo, pltpu.roll(value, 1, 1))

    def at_north(message, index):
        return pltpu.roll(message, lanes - 1 - index, 1)

    def at_south(message, index):
        return pltpu.roll(message, (lanes - index) % lanes, 1)

    depth = tall(depth_ref[...])
    d_n = to_north(depth, at_north(north, count_at))
    d_nn = to_north(d_n, at_north(north, count_at - 1))
    d_s = to_south(depth, at_south(south, count_at))
    d_e = to_east(depth, line(east_ref, depth_at))
    d_ee = to_east(d_e, line(east_ref, depth_at + 1))
    d_w = to_west(depth, line(west_ref, depth_at))
    east_line = line(east_ref, depth_at)
    west_line = line(west_ref, depth_at)
    d_ne = to_east(d_n, to_north(east_line, at_north(ne, count_at)))
    d_se = to_east(d_s, to_south(east_line, at_south(se, count_at)))
    d_nw = to_west(d_n, to_north(west_line, at_north(nw, count_at)))
    d_u = jnp.minimum(depth, d_e)
    d_v = jnp.minimum(depth, d_n)
    u_neighbours = [
        jnp.minimum(d_u, d)
        for d in (
            jnp.minimum(d_e, d_ee),
            d_w,
            jnp.minimum(d_n, d_ne),
            jnp.minimum(d_s, d_se),
        )
    ]
    v_neighbours = [
        jnp.minimum(d_v, d)
        for d in (
            jnp.minimum(d_e, d_ne),
            jnp.minimum(d_w, d_nw),
            jnp.minimum(d_n, d_nn),
            d_s,
        )
    ]

    level_row = lax.broadcasted_iota(jnp.int32, (levels, lanes), 0)
    level_lane = lax.broadcasted_iota(jnp.int32, (levels, lanes), 1)
    wet_row = jnp.minimum(
        west_ref[pl.ds(depth_at, 1), :], depth_ref[pl.ds(0, 1), :]
    )
    wet_face = level_row.astype(jnp.float32) < wet_row
    u_west = west_ref[pl.ds(4 * levels, levels), :]
    for place, field, target in ((0, t_ref, gx_t_ref), (2, s_ref, gx_s_ref)):
        near = west_ref[pl.ds(place * levels, levels), :]
        far = west_ref[pl.ds((place + 1) * levels, levels), :]
        own = field[:, 0, :]
        face = u_west * (1.0 / 12.0) * (7.0 * (near + own) - (far + field[:, 1, :]))
        target[...] = jnp.where(wet_face, face - TRACER_DIFF * (own - near), 0.0)

    def spread(corner, place, target):
        lines = jnp.broadcast_to(corner[0:1], (levels, lanes))
        shift = target - (3 * ((place + 1) * levels - 1) + 2)
        return pltpu.roll(lines, shift % lanes, 1, stride=3, stride_axis=0)

    u_corner = spread(nw_uv, 0, lanes - 1)
    v_corner = spread(se_uv, 1, 0)
    u2_ref[...] = u_west + jnp.where(
        level_lane == lanes - 1, u_corner, pltpu.roll(u_west, lanes - 1, 1)
    )
    v_east = east_ref[pl.ds(5 * levels, levels), :]
    v2_ref[...] = v_east + jnp.where(level_lane == 0, v_corner, pltpu.roll(v_east, 1, 1))

    in_block = jnp.where(lane < 3 * levels, lane, lane - 3 * levels).astype(jnp.float32)
    v_south = jnp.where(lane < 3 * levels, at_south(south_uv, 3 * levels), south_uv)
    both = south + bottom
    face = v_south * (1.0 / 12.0) * (7.0 * both - pltpu.roll(both, 1, 1))
    face = face - TRACER_DIFF * (bottom - south)
    wet_south = jnp.minimum(
        south[:, count_at : count_at + 1], bottom[:, count_at : count_at + 1]
    )
    face_south = jnp.where(in_block > 3.0 * (levels - wet_south), face, 0.0)

    third = lax.rem(lane, 3)
    near, near_uv = (
        jnp.where(third == 0, pltpu.roll(s, 1, 1), n)
        for n, s in ((north, south), (north_uv, south_uv))
    )
    far = jnp.where(third == 2, face_south, north)
    for place in range(2):
        for k in range(levels):
            spot = 3 * ((place + 1) * levels - 1 - k) + 2
            near_ref[place * levels + k] = at_north(near, spot)
            near_ref[(place + 2) * levels + k] = at_north(near_uv, spot)
            far_ref[place * levels + k] = at_north(far, spot - 1)

    row_id = (lat * lanes + lane).astype(jnp.float32)
    total = float(lat_count * lanes)
    cor_u = 2.0 * (row_id + 0.5) / total - 1.0
    cor_v = 2.0 * (row_id + 1.0) / total - 1.0
    inner, last = mixing_constants(levels)
    gain = TIME_STEP * VERTICAL_VISC

    def masked(k, count, value):
        return jnp.where(float(k) < count, value, 0.0)

    px = jnp.zeros((SUB, lanes), jnp.float32)
    py = jnp.zeros((SUB, lanes), jnp.float32)
    above = None
    ratio = None
    values = None
    for k in range(levels):
        u = tall(u_ref[k])
        v = tall(v_ref[k])
        u_face = masked(k, d_u, u * (1.0 / 12.0))
        u_diff = masked(k, d_u, TRACER_DIFF)
        v_face = masked(k, d_v, v * (1.0 / 12.0))
        v_diff = masked(k, d_v, TRACER_DIFF)
        stars = []
        seen = []
        for place, field, gx_ref in ((0, t_ref, gx_t_ref), (2, s_ref, gx_s_ref)):
            near, far = place * levels + k, (place + 1) * levels + k
            c = tall(field[k])
            c_e = to_east(c, line(east_ref, near))
            c_ee = to_east(c_e, line(east_ref, far))
            c_w = to_west(c, line(west_ref, near))
            beyond = near_ref[place // 2 * levels + k]
            c_n = to_north(c, beyond)
            beyond_2 = far_ref[place // 2 * levels + k]
            c_nn = to_north(c_n, beyond_2)
            c_s = to_south(c, beyond)
            gx = u_face * (7.0 * (c + c_e) - (c_w + c_ee)) - u_diff * (c_e - c)
            gy = v_face * (7.0 * (c + c_n) - (c_s + c_nn)) - v_diff * (c_n - c)
            gx_w = to_west(gx, line(gx_ref, k))
            gy_s = to_south(gy, beyond_2)
            stars.append(c - TIME_STEP * masked(k, depth, (gx - gx_w) + (gy - gy_s)))
            seen.append((c, c_e, c_n))
        weights = THERMAL_EXPANSION, HALINE_CONTRACTION
        b, b_e, b_n = (
            masked(k, d, weights[0] * warm - weights[1] * salt)
            for d, warm, salt in zip((depth, d_e, d_n), seen[0], seen[1])
        )
        bx = b_e - b
        by = b_n - b
        px = px + bx
        py = py + by

        u_e = to_east(u, line(east_ref, 4 * levels + k))
        u_w = to_west(u, line(west_ref, 4 * levels + k))
        u_n = to_north(u, near_ref[2 * levels + k])
        u_s = to_south(u, near_ref[2 * levels + k])
        v_e = to_east(v, line(east_ref, 5 * levels + k))
        v_w = to_west(v, line(west_ref, 5 * levels + k))
        v_n = to_north(v, near_ref[3 * levels + k])
        v_s = to_south(v, near_ref[3 * levels + k])
        v2 = v + v_s
        u2 = u + u_n
        v_bar = 0.25 * (v2 + to_east(v2, line(v2_ref, k)))
        u_bar = 0.25 * (u2 + to_west(u2, line(u2_ref, k)))
        u_visc = sum(masked(k, d, n - u) for d, n in zip(u_neighbours, (u_e, u_w, u_n, u_s)))
        v_visc = sum(masked(k, d, n - v) for d, n in zip(v_neighbours, (v_e, v_w, v_n, v_s)))
        u_star = u + TIME_STEP * (cor_u * v_bar - (px - 0.5 * bx) + MOMENTUM_VISC * u_visc)
        v_star = v + TIME_STEP * (-cor_v * u_bar - (py - 0.5 * by) + MOMENTUM_VISC * v_visc)
        if k == 0:
            u_star = u_star + TIME_STEP * WIND_GAIN * tall(wind_ref[0])
            v_star = v_star + TIME_STEP * WIND_GAIN * tall(wind_ref[1])

        if k < levels - 1:
            below = masked(k + 1, depth, TIME_STEP * tall(mix_ref[k]))
        else:
            below = None
        pivot = 1.0
        if above is not None:
            pivot = pivot + above * (1.0 - ratio)
        if below is not None:
            pivot = pivot + below
        inverse = 1.0 / pivot

        def momentum_weight(count):
            weight = jnp.where(float(k) < count, last[k], 0.0)
            if k < levels - 1:
                weight = jnp.where(float(k + 1) < count, inner[k], weight)
            return weight

        rights = stars + [u_star, v_star]
        scales = [inverse, inverse, momentum_weight(d_u), momentum_weight(d_v)]
        if k > 0:
            gains = [above, above, gain, gain]
            rights = [right + g * value for right, g, value in zip(rights, gains, values)]
        values = [right * scale for right, scale in zip(rights, scales)]
        for index, value in enumerate(values):
            val_ref[index, k] = value
        if below is not None:
            ratio = below * inverse
            val_ref[4, k] = ratio
        above = below

    outs = (t_out, s_out, u_out, v_out)
    for k in range(levels - 1, -1, -1):
        if k < levels - 1:
            ratios = [val_ref[4, k], val_ref[4, k], gain * inner[k], gain * inner[k]]
            values = [val_ref[i, k] + ratios[i] * values[i] for i in range(4)]
        for out, value in zip(outs, values):
            out[k] = value[:width]


def shards(
    thermal_anomaly,
    saltiness_anomaly,
    zonal_current,
    meridional_current,
    bottom_ocean_layer,
    seam_axis_meridian,
    interface_diffusivity,
    atmospheric_forcing,
):
    levels, width, lanes = thermal_anomaly.shape
    lon_count = lax.axis_size("lon")
    lat_count = lax.axis_size("lat")
    fields = (thermal_anomaly, saltiness_anomaly, zonal_current, meridional_current)
    wind = atmospheric_forcing
    f32 = jnp.float32
    row_message = jax.ShapeDtypeStruct((2 * width, lanes), f32)
    column_message = jax.ShapeDtypeStruct((6 * levels + 8, lanes), f32)

    fold_message = jax.ShapeDtypeStruct((6 * levels + 16, lanes), f32)
    lat_pairs = [
        [(a, b) for i in range(start, lat_count - 1, 2) for a, b in ((i, i + 1), (i + 1, i))]
        for start in (0, 1)
    ]
    lat_pairs = [pairs for pairs in lat_pairs if pairs]
    top, bottom, eastward, westward, counts, stress, *messages = pl.pallas_call(
        edges_kernel,
        out_shape=[row_message] * 2
        + [column_message] * 2
        + [jax.ShapeDtypeStruct((width, lanes), f32), jax.ShapeDtypeStruct(wind.shape, f32)]
        + [jax.ShapeDtypeStruct((4 * width, lanes), f32), row_message][: len(lat_pairs)],
        in_specs=[VMEM] * 6,
        out_specs=[VMEM] * (6 + len(lat_pairs)),
        compiler_params=FIRST,
    )(*[pltpu.with_memory_space_constraint(x, pltpu.HBM) for x in (*fields, bottom_ocean_layer, wind)])
    received = [
        lax.ppermute(message, "lat", pairs) for message, pairs in zip(messages, lat_pairs)
    ]

    north, south, eastward, fold, westward, rest = pl.pallas_call(
        corners_kernel,
        out_shape=[row_message] * 2
        + [column_message, fold_message, column_message]
        + [jax.ShapeDtypeStruct((SUB, lanes), jnp.int32)],
        in_specs=[VMEM] * 3 + [SMEM] + [VMEM] * len(received),
        out_specs=[VMEM] * 6,
        compiler_params=SMALL,
    )(top, eastward, westward, seam_axis_meridian, *received)

    code = seam_axis_meridian[0]
    tile = lax.rem(lax.div(code, width), lon_count)
    three = (lax.rem(code, width) == width - 1).astype(jnp.int32)
    ring = [(i, (i + 1) % lon_count) for i in range(lon_count)]
    trade = [(i, i ^ 1) for i in range(lon_count)]
    pairs = [(i, i ^ 1) for i in range(lat_count)]

    def fold_pairs(*mirrors):
        rows = [*mirrors] + [trade] * (lat_count - len(mirrors))
        return [
            (a * lat_count + lat_count - 1 - row, b * lat_count + lat_count - 1 - row)
            for row, mirror in enumerate(rows)
            for a, b in mirror
        ]

    from_west = lax.ppermute(eastward, "lon", ring)
    keep = pl.pallas_call(
        keep_kernel,
        out_shape=column_message,
        in_specs=[VMEM],
        out_specs=VMEM,
        compiler_params=SMALL,
    )

    def reflect(code):
        own = [i for i in range(lon_count) if (code - i) % lon_count == i]
        if len(own) != 2:
            return [(i, (code - i) % lon_count) for i in range(lon_count)], []
        trade = {own[0]: own[1], own[1]: own[0]}
        return [(i, trade.get(i, (code - i) % lon_count)) for i in range(lon_count)], own

    def exchange(first, count):
        direct = first % 2
        mirrors, own_tiles = zip(*(reflect(first - 1 + d) for d in range(3)))
        mirror = pl.pallas_call(
            functools.partial(mirror_kernel, own_tiles),
            out_shape=jax.ShapeDtypeStruct((2, 16, lanes), f32),
            in_specs=[VMEM] * (2 + count),
            out_specs=VMEM,
            scratch_shapes=[pltpu.VMEM((2, 3 * width, lanes), f32)],
            compiler_params=SMALL,
        )

        def branch(fold, westward, rest):
            both = ("lon", "lat")
            tile = lax.ppermute(fold, both, fold_pairs(mirrors[direct], mirrors[1 - direct]))
            tiles = [tile, lax.ppermute(tile[: 2 * width], "lat", pairs)]
            if direct == 1:
                tiles = tiles[::-1]
            if count == 3:
                tiles.append(lax.ppermute(fold, both, fold_pairs(mirrors[2])))
            return (
                keep(lax.ppermute(westward, "lon", [(b, a) for a, b in ring])),
                mirror(fold, rest, *tiles),
            )

        return branch

    branches = [exchange(first, count) for first in range(lon_count) for count in (2, 3)]
    from_east, mirrored = lax.switch(
        tile * 2 + three, branches, fold, westward, rest
    )

    whole = jax.ShapeDtypeStruct((levels, width, lanes), f32)
    return pl.pallas_call(
        step_kernel,
        out_shape=[whole] * 4,
        in_specs=[VMEM] * 13,
        out_specs=[VMEM] * 4,
        compiler_params=LARGE,
        scratch_shapes=[pltpu.VMEM((levels, lanes), f32)] * 4
        + [pltpu.VMEM((5, levels, SUB, lanes), f32)]
        + [pltpu.VMEM((count * levels, SUB, lanes), f32) for count in (4, 2)],
    )(
        *fields,
        counts,
        interface_diffusivity,
        stress,
        bottom,
        north,
        south,
        from_west,
        from_east,
        mirrored,
    )


def solution(mesh):
    split = P(None, "lon", "lat")
    return jax.shard_map(
        shards,
        mesh=mesh,
        in_specs=(split, split, split, split, P("lon", "lat"), P(), split, split),
        out_specs=(split, split, split, split),
        check_vma=False,
    )
```

```python
import functools

import jax
import jax.numpy as jnp
from jax import lax
from jax.experimental import pallas as pl
from jax.experimental.pallas import tpu as pltpu
from jax.sharding import PartitionSpec as P

TIME_STEP = 0.2
TRACER_DIFF = 0.2
MOMENTUM_VISC = 0.2
THERMAL_EXPANSION = 0.5
HALINE_CONTRACTION = 0.4
WIND_GAIN = 2.0
VERTICAL_VISC = 1.0

VMEM = pl.BlockSpec(memory_space=pltpu.VMEM)
SMEM = pl.BlockSpec(memory_space=pltpu.SMEM)
SUB = 8
SMALL = pltpu.CompilerParams(vmem_limit_bytes=4 * 2**20)
FIRST = pltpu.CompilerParams(vmem_limit_bytes=4 * 2**20)
LARGE = pltpu.CompilerParams(vmem_limit_bytes=8 * 2**20)


def lane_of(lanes):
    return lax.broadcasted_iota(jnp.int32, (SUB, lanes), 1)


def row_of(lanes):
    return lax.broadcasted_iota(jnp.int32, (SUB, lanes), 0)


def tall(value):
    missing = SUB - value.shape[0]
    if missing == 0:
        return value
    return jnp.concatenate([value, jnp.zeros((missing, value.shape[1]), value.dtype)], axis=0)


def edges_kernel(t_ref, s_ref, u_ref, v_ref, depth_ref, stress_ref, *outs):
    top_ref, bottom_ref, east_ref, west_ref, count_ref, wind_ref, first_ref = outs[:7]
    levels, width, lanes = t_ref.shape
    count_ref[...] = depth_ref[...].astype(jnp.float32)
    wind_ref[...] = stress_ref[...]
    even = lax.rem(lax.axis_index("lat"), 2) == 0
    lane = lane_of(lanes)
    for message, near, far in ((east_ref, width - 1, width - 2), (west_ref, 0, 1)):
        for place, field, column in (
            (0, t_ref, near),
            (1, t_ref, far),
            (2, s_ref, near),
            (3, s_ref, far),
            (4, u_ref, near),
            (5, v_ref, near),
        ):
            message[pl.ds(place * levels, levels), :] = field[:, column, :]
        depth = depth_ref[...].astype(jnp.float32)
        message[pl.ds(6 * levels, 8), :] = jnp.concatenate(
            [depth[near : near + 1], depth[far : far + 1]] * 4, axis=0
        )

    tops, bottoms = [], []
    for first, second, count in ((t_ref, s_ref, depth_ref), (u_ref, v_ref, None)):
        top = jnp.zeros((SUB, lanes), jnp.float32)
        bottom = jnp.zeros((SUB, lanes), jnp.float32)
        places = [(3 * (levels - 1 - k), first, k) for k in range(levels)]
        places += [(3 * (2 * levels - 1 - k), second, k) for k in range(levels)]
        if count is not None:
            places.append((6 * levels, count, None))
        for start, ref, k in places:
            value = depth_ref[...].astype(jnp.float32) if k is None else ref[k]
            value = tall(value)
            value = pltpu.roll(value, start + 3, 1)
            top = jnp.where(jnp.logical_and(lane >= start, lane < start + 3), value, top)
            bottom = jnp.where(jnp.logical_and(lane >= start + 3, lane < start + 6), value, bottom)
        bottom = jnp.where(
            lax.rem(lane, 3) == 2,
            pltpu.roll(bottom, lanes - 1, 1),
            pltpu.roll(bottom, lanes - 3, 1),
        )
        tops.append(top[:width])
        bottoms.append(bottom[:width])
    for index in range(2):
        rows = pl.ds(index * width, width)
        top_ref[rows, :] = tops[index]
        bottom_ref[rows, :] = bottoms[index]
        first_ref[rows, :] = jnp.where(even, tops[index], bottoms[index])
        first_ref[pl.ds((2 + index) * width, width), :] = tops[index]
        for second_ref in outs[7:]:
            second_ref[rows, :] = jnp.where(even, bottoms[index], tops[index])


def corners_kernel(top_ref, east_base_ref, west_base_ref, seam_ref, *refs):
    north_ref, south_ref, east_ref, fold_ref, west_ref, rest_ref = refs[-6:]
    received = refs[:-6]
    lanes = top_ref.shape[1]
    width = top_ref.shape[0] // 2
    lat = lax.axis_index("lat")
    even = lax.rem(lat, 2) == 0
    halo = pl.ds(0, 2 * width)
    from_first = received[0][halo, :]
    from_second = received[1][...] if len(received) > 1 else jnp.zeros_like(from_first)
    north = jnp.where(even, from_first, from_second)
    south = jnp.where(even, from_second, from_first)
    north_ref[...] = north
    south_ref[...] = south
    base = west_base_ref.shape[0] - 8
    near = width - 1
    east_ref[pl.ds(0, base), :] = east_base_ref[pl.ds(0, base), :]
    east_ref[pl.ds(base, 8), :] = jnp.concatenate(
        [
            east_base_ref[pl.ds(base, 2), :],
            north[near : near + 1],
            north[width + near : width + near + 1],
            jnp.zeros((4, lanes), jnp.float32),
        ],
        axis=0,
    )
    west_ref[pl.ds(0, base), :] = west_base_ref[pl.ds(0, base), :]
    west_ref[pl.ds(base, 8), :] = jnp.concatenate(
        [
            west_base_ref[pl.ds(base, 2), :],
            north[0:1],
            north[width : width + 1],
            south[0:1],
            south[width : width + 1],
            jnp.zeros((2, lanes), jnp.float32),
        ],
        axis=0,
    )
    is_top = lat == lax.axis_size("lat") - 1
    code = seam_ref[0]
    corner = lax.rem(code, 2) == 1
    for index in range(2):
        rows = pl.ds(index * width, width)
        theirs = received[0][pl.ds((2 + index) * width, width), :]
        top = tall(jnp.where(is_top, top_ref[rows, :], theirs))
        fold_ref[rows, :] = jnp.where(corner, top, pltpu.roll(top, 1, 1))[:width]
    unused = fold_ref.shape[0] - 2 * width
    fold_ref[pl.ds(2 * width, unused), :] = jnp.zeros((unused, lanes), jnp.float32)
    rest_ref[...] = jnp.full((SUB, lanes), lax.rem(code, width), jnp.int32)


def mixing_constants(levels):
    gain = TIME_STEP * VERTICAL_VISC
    inner, last, ratio = [], [], 0.0
    for k in range(levels):
        above = gain if k > 0 else 0.0
        last.append(1.0 / (1.0 + above + above * ratio))
        pivot = 1.0 + above + gain + above * ratio
        inner.append(1.0 / pivot)
        ratio = -gain / pivot
    return inner, last


def keep_kernel(message_ref, kept_ref):
    kept_ref[...] = message_ref[...]


def mirror_kernel(own_tiles, own_ref, rest_ref, *refs):
    tiles, (mirror_ref, tiles_ref) = refs[:-2], refs[-2:]
    width = tiles_ref.shape[1] // 3
    rest = rest_ref[0, 0]
    lon = lax.axis_index("lon")
    for index in range(2):
        half = pl.ds(index * width, width)
        for place, ref in enumerate(tiles):
            tile = ref[half, :]
            for device in own_tiles[place]:
                tile = jnp.where(lon == device, own_ref[half, :], tile)
            tiles_ref[index, pl.ds(place * width, width), :] = tile
        for i in range(-1, width + 1):
            mirror_ref[index, pl.ds(i + 1, 1), :] = tiles_ref[
                index, pl.ds(width + rest - i, 1), :
            ]


def step_kernel(
    t_ref,
    s_ref,
    u_ref,
    v_ref,
    depth_ref,
    mix_ref,
    wind_ref,
    bottom_ref,
    north_ref,
    south_ref,
    west_ref,
    east_ref,
    mirror_ref,
    t_out,
    s_out,
    u_out,
    v_out,
    gx_t_ref,
    gx_s_ref,
    u2_ref,
    v2_ref,
    val_ref,
    near_ref,
    far_ref,
):
    levels, width, lanes = t_ref.shape
    lat = lax.axis_index("lat")
    lat_count = lax.axis_size("lat")
    is_top = lat == lat_count - 1
    lane = lane_of(lanes)
    row = row_of(lanes)
    depth_at = 6 * levels
    count_at = 6 * levels + 2

    def half(ref, index):
        return tall(ref[pl.ds(index * width, width), :])

    north, north_uv = (
        jnp.where(
            is_top, sign * tall(mirror_ref[index, pl.ds(1, width), :]), half(north_ref, index)
        )
        for index, sign in ((0, 1.0), (1, -1.0))
    )
    south, south_uv = half(south_ref, 0), half(south_ref, 1)
    bottom = half(bottom_ref, 0)

    def line(ref, index):
        return jnp.broadcast_to(ref[pl.ds(index, 1), :], (SUB, lanes))

    def mirror_line(index, i):
        return jnp.broadcast_to(mirror_ref[index, pl.ds(i + 1, 1), :], (SUB, lanes))

    nw = jnp.where(is_top, mirror_line(0, -1), line(west_ref, depth_at + 2))
    nw_uv = jnp.where(is_top, -mirror_line(1, -1), line(west_ref, depth_at + 3))
    ne = jnp.where(is_top, mirror_line(0, width), line(east_ref, depth_at + 2))
    se = line(east_ref, depth_at + 4)
    se_uv = line(east_ref, depth_at + 5)

    def to_east(value, halo):
        return jnp.where(row == width - 1, halo, pltpu.roll(value, SUB - 1, 0))

    def to_west(value, halo):
        return jnp.where(row == 0, halo, pltpu.roll(value, 1, 0))

    def to_north(value, halo):
        return jnp.where(lane == lanes - 1, halo, pltpu.roll(value, lanes - 1, 1))

    def to_south(value, halo):
        return jnp.where(lane == 0, halo, pltpu.roll(value, 1, 1))

    def at_north(message, index):
        return pltpu.roll(message, lanes - 1 - index, 1)

    def at_south(message, index):
        return pltpu.roll(message, (lanes - index) % lanes, 1)

    depth = tall(depth_ref[...])
    d_n = to_north(depth, at_north(north, count_at))
    d_nn = to_north(d_n, at_north(north, count_at - 1))
    d_s = to_south(depth, at_south(south, count_at))
    d_e = to_east(depth, line(east_ref, depth_at))
    d_ee = to_east(d_e, line(east_ref, depth_at + 1))
    d_w = to_west(depth, line(west_ref, depth_at))
    east_line = line(east_ref, depth_at)
    west_line = line(west_ref, depth_at)
    d_ne = to_east(d_n, to_north(east_line, at_north(ne, count_at)))
    d_se = to_east(d_s, to_south(east_line, at_south(se, count_at)))
    d_nw = to_west(d_n, to_north(west_line, at_north(nw, count_at)))
    d_u = jnp.minimum(depth, d_e)
    d_v = jnp.minimum(depth, d_n)
    u_neighbours = [
        jnp.minimum(d_u, d)
        for d in (
            jnp.minimum(d_e, d_ee),
            d_w,
            jnp.minimum(d_n, d_ne),
            jnp.minimum(d_s, d_se),
        )
    ]
    v_neighbours = [
        jnp.minimum(d_v, d)
        for d in (
            jnp.minimum(d_e, d_ne),
            jnp.minimum(d_w, d_nw),
            jnp.minimum(d_n, d_nn),
            d_s,
        )
    ]

    level_row = lax.broadcasted_iota(jnp.int32, (levels, lanes), 0)
    level_lane = lax.broadcasted_iota(jnp.int32, (levels, lanes), 1)
    wet_row = jnp.minimum(
        west_ref[pl.ds(depth_at, 1), :], depth_ref[pl.ds(0, 1), :]
    )
    wet_face = level_row.astype(jnp.float32) < wet_row
    u_west = west_ref[pl.ds(4 * levels, levels), :]
    for place, field, target in ((0, t_ref, gx_t_ref), (2, s_ref, gx_s_ref)):
        near = west_ref[pl.ds(place * levels, levels), :]
        far = west_ref[pl.ds((place + 1) * levels, levels), :]
        own = field[:, 0, :]
        face = u_west * (1.0 / 12.0) * (7.0 * (near + own) - (far + field[:, 1, :]))
        target[...] = jnp.where(wet_face, face - TRACER_DIFF * (own - near), 0.0)

    def spread(corner, place, target):
        lines = jnp.broadcast_to(corner[0:1], (levels, lanes))
        shift = target - (3 * ((place + 1) * levels - 1) + 2)
        return pltpu.roll(lines, shift % lanes, 1, stride=3, stride_axis=0)

    u_corner = spread(nw_uv, 0, lanes - 1)
    v_corner = spread(se_uv, 1, 0)
    u2_ref[...] = u_west + jnp.where(
        level_lane == lanes - 1, u_corner, pltpu.roll(u_west, lanes - 1, 1)
    )
    v_east = east_ref[pl.ds(5 * levels, levels), :]
    v2_ref[...] = v_east + jnp.where(level_lane == 0, v_corner, pltpu.roll(v_east, 1, 1))

    in_block = jnp.where(lane < 3 * levels, lane, lane - 3 * levels).astype(jnp.float32)
    v_south = jnp.where(lane < 3 * levels, at_south(south_uv, 3 * levels), south_uv)
    both = south + bottom
    face = v_south * (1.0 / 12.0) * (7.0 * both - pltpu.roll(both, 1, 1))
    face = face - TRACER_DIFF * (bottom - south)
    wet_south = jnp.minimum(
        south[:, count_at : count_at + 1], bottom[:, count_at : count_at + 1]
    )
    face_south = jnp.where(in_block > 3.0 * (levels - wet_south), face, 0.0)

    third = lax.rem(lane, 3)
    near, near_uv = (
        jnp.where(third == 0, pltpu.roll(s, 1, 1), n)
        for n, s in ((north, south), (north_uv, south_uv))
    )
    far = jnp.where(third == 2, face_south, north)
    for place in range(2):
        for k in range(levels):
            spot = 3 * ((place + 1) * levels - 1 - k) + 2
            near_ref[place * levels + k] = at_north(near, spot)
            near_ref[(place + 2) * levels + k] = at_north(near_uv, spot)
            far_ref[place * levels + k] = at_north(far, spot - 1)

    row_id = (lat * lanes + lane).astype(jnp.float32)
    total = float(lat_count * lanes)
    cor_u = 2.0 * (row_id + 0.5) / total - 1.0
    cor_v = 2.0 * (row_id + 1.0) / total - 1.0
    inner, last = mixing_constants(levels)
    gain = TIME_STEP * VERTICAL_VISC

    def masked(k, count, value):
        return jnp.where(float(k) < count, value, 0.0)

    px = jnp.zeros((SUB, lanes), jnp.float32)
    py = jnp.zeros((SUB, lanes), jnp.float32)
    above = None
    ratio = None
    values = None
    for k in range(levels):
        u = tall(u_ref[k])
        v = tall(v_ref[k])
        u_face = masked(k, d_u, u * (1.0 / 12.0))
        u_diff = masked(k, d_u, TRACER_DIFF)
        v_face = masked(k, d_v, v * (1.0 / 12.0))
        v_diff = masked(k, d_v, TRACER_DIFF)
        stars = []
        seen = []
        for place, field, gx_ref in ((0, t_ref, gx_t_ref), (2, s_ref, gx_s_ref)):
            near, far = place * levels + k, (place + 1) * levels + k
            c = tall(field[k])
            c_e = to_east(c, line(east_ref, near))
            c_ee = to_east(c_e, line(east_ref, far))
            c_w = to_west(c, line(west_ref, near))
            beyond = near_ref[place // 2 * levels + k]
            c_n = to_north(c, beyond)
            beyond_2 = far_ref[place // 2 * levels + k]
            c_nn = to_north(c_n, beyond_2)
            c_s = to_south(c, beyond)
            gx = u_face * (7.0 * (c + c_e) - (c_w + c_ee)) - u_diff * (c_e - c)
            gy = v_face * (7.0 * (c + c_n) - (c_s + c_nn)) - v_diff * (c_n - c)
            gx_w = to_west(gx, line(gx_ref, k))
            gy_s = to_south(gy, beyond_2)
            stars.append(c - TIME_STEP * masked(k, depth, (gx - gx_w) + (gy - gy_s)))
            seen.append((c, c_e, c_n))
        weights = THERMAL_EXPANSION, HALINE_CONTRACTION
        b, b_e, b_n = (
            masked(k, d, weights[0] * warm - weights[1] * salt)
            for d, warm, salt in zip((depth, d_e, d_n), seen[0], seen[1])
        )
        bx = b_e - b
        by = b_n - b
        px = px + bx
        py = py + by

        u_e = to_east(u, line(east_ref, 4 * levels + k))
        u_w = to_west(u, line(west_ref, 4 * levels + k))
        u_n = to_north(u, near_ref[2 * levels + k])
        u_s = to_south(u, near_ref[2 * levels + k])
        v_e = to_east(v, line(east_ref, 5 * levels + k))
        v_w = to_west(v, line(west_ref, 5 * levels + k))
        v_n = to_north(v, near_ref[3 * levels + k])
        v_s = to_south(v, near_ref[3 * levels + k])
        v2 = v + v_s
        u2 = u + u_n
        v_bar = 0.25 * (v2 + to_east(v2, line(v2_ref, k)))
        u_bar = 0.25 * (u2 + to_west(u2, line(u2_ref, k)))
        u_visc = sum(masked(k, d, n - u) for d, n in zip(u_neighbours, (u_e, u_w, u_n, u_s)))
        v_visc = sum(masked(k, d, n - v) for d, n in zip(v_neighbours, (v_e, v_w, v_n, v_s)))
        u_star = u + TIME_STEP * (cor_u * v_bar - (px - 0.5 * bx) + MOMENTUM_VISC * u_visc)
        v_star = v + TIME_STEP * (-cor_v * u_bar - (py - 0.5 * by) + MOMENTUM_VISC * v_visc)
        if k == 0:
            u_star = u_star + TIME_STEP * WIND_GAIN * tall(wind_ref[0])
            v_star = v_star + TIME_STEP * WIND_GAIN * tall(wind_ref[1])

        if k < levels - 1:
            below = masked(k + 1, depth, TIME_STEP * tall(mix_ref[k]))
        else:
            below = None
        pivot = 1.0
        if above is not None:
            pivot = pivot + above * (1.0 - ratio)
        if below is not None:
            pivot = pivot + below
        inverse = 1.0 / pivot

        def momentum_weight(count):
            weight = jnp.where(float(k) < count, last[k], 0.0)
            if k < levels - 1:
                weight = jnp.where(float(k + 1) < count, inner[k], weight)
            return weight

        rights = stars + [u_star, v_star]
        scales = [inverse, inverse, momentum_weight(d_u), momentum_weight(d_v)]
        if k > 0:
            gains = [above, above, gain, gain]
            rights = [right + g * value for right, g, value in zip(rights, gains, values)]
        values = [right * scale for right, scale in zip(rights, scales)]
        for index, value in enumerate(values):
            val_ref[index, k] = value
        if below is not None:
            ratio = below * inverse
            val_ref[4, k] = ratio
        above = below

    outs = (t_out, s_out, u_out, v_out)
    for k in range(levels - 1, -1, -1):
        if k < levels - 1:
            ratios = [val_ref[4, k], val_ref[4, k], gain * inner[k], gain * inner[k]]
            values = [val_ref[i, k] + ratios[i] * values[i] for i in range(4)]
        for out, value in zip(outs, values):
            out[k] = value[:width]


def shards(
    thermal_anomaly,
    saltiness_anomaly,
    zonal_current,
    meridional_current,
    bottom_ocean_layer,
    seam_axis_meridian,
    interface_diffusivity,
    atmospheric_forcing,
):
    levels, width, lanes = thermal_anomaly.shape
    lon_count = lax.axis_size("lon")
    lat_count = lax.axis_size("lat")
    fields = (thermal_anomaly, saltiness_anomaly, zonal_current, meridional_current)
    wind = atmospheric_forcing
    f32 = jnp.float32
    row_message = jax.ShapeDtypeStruct((2 * width, lanes), f32)
    column_message = jax.ShapeDtypeStruct((6 * levels + 8, lanes), f32)

    fold_message = jax.ShapeDtypeStruct((6 * levels + 16, lanes), f32)
    lat_pairs = [
        [(a, b) for i in range(start, lat_count - 1, 2) for a, b in ((i, i + 1), (i + 1, i))]
        for start in (0, 1)
    ]
    lat_pairs = [pairs for pairs in lat_pairs if pairs]
    top, bottom, eastward, westward, counts, stress, *messages = pl.pallas_call(
        edges_kernel,
        out_shape=[row_message] * 2
        + [column_message] * 2
        + [jax.ShapeDtypeStruct((width, lanes), f32), jax.ShapeDtypeStruct(wind.shape, f32)]
        + [jax.ShapeDtypeStruct((4 * width, lanes), f32), row_message][: len(lat_pairs)],
        in_specs=[VMEM] * 6,
        out_specs=[VMEM] * (6 + len(lat_pairs)),
        compiler_params=FIRST,
    )(*[pltpu.with_memory_space_constraint(x, pltpu.HBM) for x in (*fields, bottom_ocean_layer, wind)])
    received = [
        lax.ppermute(message, "lat", pairs) for message, pairs in zip(messages, lat_pairs)
    ]

    north, south, eastward, fold, westward, rest = pl.pallas_call(
        corners_kernel,
        out_shape=[row_message] * 2
        + [column_message, fold_message, column_message]
        + [jax.ShapeDtypeStruct((SUB, lanes), jnp.int32)],
        in_specs=[VMEM] * 3 + [SMEM] + [VMEM] * len(received),
        out_specs=[VMEM] * 6,
        compiler_params=SMALL,
    )(top, eastward, westward, seam_axis_meridian, *received)

    code = seam_axis_meridian[0]
    tile = lax.rem(lax.div(code, width), lon_count)
    three = (lax.rem(code, width) == width - 1).astype(jnp.int32)
    ring = [(i, (i + 1) % lon_count) for i in range(lon_count)]
    trade = [(i, i ^ 1) for i in range(lon_count)]
    pairs = [(i, i ^ 1) for i in range(lat_count)]

    def fold_pairs(*mirrors):
        rows = [*mirrors] + [trade] * (lat_count - len(mirrors))
        return [
            (a * lat_count + lat_count - 1 - row, b * lat_count + lat_count - 1 - row)
            for row, mirror in enumerate(rows)
            for a, b in mirror
        ]

    from_west = lax.ppermute(eastward, "lon", ring)
    keep = pl.pallas_call(
        keep_kernel,
        out_shape=column_message,
        in_specs=[VMEM],
        out_specs=VMEM,
        compiler_params=SMALL,
    )

    def reflect(code):
        own = [i for i in range(lon_count) if (code - i) % lon_count == i]
        if len(own) != 2:
            return [(i, (code - i) % lon_count) for i in range(lon_count)], []
        trade = {own[0]: own[1], own[1]: own[0]}
        return [(i, trade.get(i, (code - i) % lon_count)) for i in range(lon_count)], own

    def exchange(first, count):
        direct = first % 2
        mirrors, own_tiles = zip(*(reflect(first - 1 + d) for d in range(3)))
        mirror = pl.pallas_call(
            functools.partial(mirror_kernel, own_tiles),
            out_shape=jax.ShapeDtypeStruct((2, 16, lanes), f32),
            in_specs=[VMEM] * (2 + count),
            out_specs=VMEM,
            scratch_shapes=[pltpu.VMEM((2, 3 * width, lanes), f32)],
            compiler_params=SMALL,
        )

        def branch(fold, westward, rest):
            both = ("lon", "lat")
            tile = lax.ppermute(fold, both, fold_pairs(mirrors[direct], mirrors[1 - direct]))
            tiles = [tile, lax.ppermute(tile[: 2 * width], "lat", pairs)]
            if direct == 1:
                tiles = tiles[::-1]
            if count == 3:
                tiles.append(lax.ppermute(fold, both, fold_pairs(mirrors[2])))
            return (
                keep(lax.ppermute(westward, "lon", [(b, a) for a, b in ring])),
                mirror(fold, rest, *tiles),
            )

        return branch

    branches = [exchange(first, count) for first in range(lon_count) for count in (2, 3)]
    from_east, mirrored = lax.switch(
        tile * 2 + three, branches, fold, westward, rest
    )

    whole = jax.ShapeDtypeStruct((levels, width, lanes), f32)
    return pl.pallas_call(
        step_kernel,
        out_shape=[whole] * 4,
        in_specs=[VMEM] * 13,
        out_specs=[VMEM] * 4,
        compiler_params=LARGE,
        scratch_shapes=[pltpu.VMEM((levels, lanes), f32)] * 4
        + [pltpu.VMEM((5, levels, SUB, lanes), f32)]
        + [pltpu.VMEM((count * levels, SUB, lanes), f32) for count in (4, 2)],
    )(
        *fields,
        counts,
        interface_diffusivity,
        stress,
        bottom,
        north,
        south,
        from_west,
        from_east,
        mirrored,
    )


def solution(mesh):
    split = P(None, "lon", "lat")
    return jax.shard_map(
        shards,
        mesh=mesh,
        in_specs=(split, split, split, split, P("lon", "lat"), P(), split, split),
        out_specs=(split, split, split, split),
        check_vma=False,
    )
```

```python
import functools

import jax
import jax.numpy as jnp
from jax import lax
from jax.experimental import pallas as pl
from jax.experimental.pallas import tpu as pltpu
from jax.sharding import PartitionSpec as P

TIME_STEP = 0.2
TRACER_DIFF = 0.2
MOMENTUM_VISC = 0.2
THERMAL_EXPANSION = 0.5
HALINE_CONTRACTION = 0.4
WIND_GAIN = 2.0
VERTICAL_VISC = 1.0

VMEM = pl.BlockSpec(memory_space=pltpu.VMEM)
SMEM = pl.BlockSpec(memory_space=pltpu.SMEM)
SUB = 8
SMALL = pltpu.CompilerParams(vmem_limit_bytes=4 * 2**20)
FIRST = pltpu.CompilerParams(vmem_limit_bytes=4 * 2**20)
LARGE = pltpu.CompilerParams(vmem_limit_bytes=8 * 2**20)


def lane_of(lanes):
    return lax.broadcasted_iota(jnp.int32, (SUB, lanes), 1)


def row_of(lanes):
    return lax.broadcasted_iota(jnp.int32, (SUB, lanes), 0)


def tall(value):
    missing = SUB - value.shape[0]
    if missing == 0:
        return value
    return jnp.concatenate([value, jnp.zeros((missing, value.shape[1]), value.dtype)], axis=0)


def edges_kernel(t_ref, s_ref, u_ref, v_ref, depth_ref, stress_ref, *outs):
    top_ref, bottom_ref, east_ref, west_ref, count_ref, wind_ref, first_ref = outs[:7]
    levels, width, lanes = t_ref.shape
    count_ref[...] = depth_ref[...].astype(jnp.float32)
    wind_ref[...] = stress_ref[...]
    even = lax.rem(lax.axis_index("lat"), 2) == 0
    lane = lane_of(lanes)
    for message, near, far in ((east_ref, width - 1, width - 2), (west_ref, 0, 1)):
        for place, field, column in (
            (0, t_ref, near),
            (1, t_ref, far),
            (2, s_ref, near),
            (3, s_ref, far),
            (4, u_ref, near),
            (5, v_ref, near),
        ):
            message[pl.ds(place * levels, levels), :] = field[:, column, :]
        depth = depth_ref[...].astype(jnp.float32)
        message[pl.ds(6 * levels, 8), :] = jnp.concatenate(
            [depth[near : near + 1], depth[far : far + 1]] * 4, axis=0
        )

    tops, bottoms = [], []
    for first, second, count in ((t_ref, s_ref, depth_ref), (u_ref, v_ref, None)):
        top = jnp.zeros((SUB, lanes), jnp.float32)
        bottom = jnp.zeros((SUB, lanes), jnp.float32)
        places = [(3 * (levels - 1 - k), first, k) for k in range(levels)]
        places += [(3 * (2 * levels - 1 - k), second, k) for k in range(levels)]
        if count is not None:
            places.append((6 * levels, count, None))
        for start, ref, k in places:
            value = depth_ref[...].astype(jnp.float32) if k is None else ref[k]
            value = tall(value)
            value = pltpu.roll(value, start + 3, 1)
            top = jnp.where(jnp.logical_and(lane >= start, lane < start + 3), value, top)
            bottom = jnp.where(jnp.logical_and(lane >= start + 3, lane < start + 6), value, bottom)
        bottom = jnp.where(
            lax.rem(lane, 3) == 2,
            pltpu.roll(bottom, lanes - 1, 1),
            pltpu.roll(bottom, lanes - 3, 1),
        )
        tops.append(top[:width])
        bottoms.append(bottom[:width])
    for index in range(2):
        rows = pl.ds(index * width, width)
        top_ref[rows, :] = tops[index]
        bottom_ref[rows, :] = bottoms[index]
        first_ref[rows, :] = jnp.where(even, tops[index], bottoms[index])
        first_ref[pl.ds((2 + index) * width, width), :] = tops[index]
        for second_ref in outs[7:]:
            second_ref[rows, :] = jnp.where(even, bottoms[index], tops[index])


def corners_kernel(top_ref, east_base_ref, west_base_ref, seam_ref, *refs):
    north_ref, south_ref, east_ref, fold_ref, west_ref, rest_ref = refs[-6:]
    received = refs[:-6]
    lanes = top_ref.shape[1]
    width = top_ref.shape[0] // 2
    lat = lax.axis_index("lat")
    even = lax.rem(lat, 2) == 0
    halo = pl.ds(0, 2 * width)
    from_first = received[0][halo, :]
    from_second = received[1][...] if len(received) > 1 else jnp.zeros_like(from_first)
    north = jnp.where(even, from_first, from_second)
    south = jnp.where(even, from_second, from_first)
    north_ref[...] = north
    south_ref[...] = south
    base = west_base_ref.shape[0] - 8
    near = width - 1
    east_ref[pl.ds(0, base), :] = east_base_ref[pl.ds(0, base), :]
    east_ref[pl.ds(base, 8), :] = jnp.concatenate(
        [
            east_base_ref[pl.ds(base, 2), :],
            north[near : near + 1],
            north[width + near : width + near + 1],
            jnp.zeros((4, lanes), jnp.float32),
        ],
        axis=0,
    )
    west_ref[pl.ds(0, base), :] = west_base_ref[pl.ds(0, base), :]
    west_ref[pl.ds(base, 8), :] = jnp.concatenate(
        [
            west_base_ref[pl.ds(base, 2), :],
            north[0:1],
            north[width : width + 1],
            south[0:1],
            south[width : width + 1],
            jnp.zeros((2, lanes), jnp.float32),
        ],
        axis=0,
    )
    is_top = lat == lax.axis_size("lat") - 1
    code = seam_ref[0]
    corner = lax.rem(code, 2) == 1
    for index in range(2):
        rows = pl.ds(index * width, width)
        theirs = received[0][pl.ds((2 + index) * width, width), :]
        top = tall(jnp.where(is_top, top_ref[rows, :], theirs))
        fold_ref[rows, :] = jnp.where(corner, top, pltpu.roll(top, 1, 1))[:width]
    unused = fold_ref.shape[0] - 2 * width
    fold_ref[pl.ds(2 * width, unused), :] = jnp.zeros((unused, lanes), jnp.float32)
    rest_ref[...] = jnp.full((SUB, lanes), lax.rem(code, width), jnp.int32)


def mixing_constants(levels):
    gain = TIME_STEP * VERTICAL_VISC
    inner, last, ratio = [], [], 0.0
    for k in range(levels):
        above = gain if k > 0 else 0.0
        last.append(1.0 / (1.0 + above + above * ratio))
        pivot = 1.0 + above + gain + above * ratio
        inner.append(1.0 / pivot)
        ratio = -gain / pivot
    return inner, last


def keep_kernel(message_ref, kept_ref):
    kept_ref[...] = message_ref[...]


def mirror_kernel(own_tiles, own_ref, rest_ref, *refs):
    tiles, (mirror_ref, tiles_ref) = refs[:-2], refs[-2:]
    width = tiles_ref.shape[1] // 3
    rest = rest_ref[0, 0]
    lon = lax.axis_index("lon")
    for index in range(2):
        half = pl.ds(index * width, width)
        for place, ref in enumerate(tiles):
            tile = ref[half, :]
            for device in own_tiles[place]:
                tile = jnp.where(lon == device, own_ref[half, :], tile)
            tiles_ref[index, pl.ds(place * width, width), :] = tile
        for i in range(-1, width + 1):
            mirror_ref[index, pl.ds(i + 1, 1), :] = tiles_ref[
                index, pl.ds(width + rest - i, 1), :
            ]


def step_kernel(
    t_ref,
    s_ref,
    u_ref,
    v_ref,
    depth_ref,
    mix_ref,
    wind_ref,
    bottom_ref,
    north_ref,
    south_ref,
    west_ref,
    east_ref,
    mirror_ref,
    t_out,
    s_out,
    u_out,
    v_out,
    gx_t_ref,
    gx_s_ref,
    u2_ref,
    v2_ref,
    val_ref,
    near_ref,
    far_ref,
):
    levels, width, lanes = t_ref.shape
    lat = lax.axis_index("lat")
    lat_count = lax.axis_size("lat")
    is_top = lat == lat_count - 1
    lane = lane_of(lanes)
    row = row_of(lanes)
    depth_at = 6 * levels
    count_at = 6 * levels + 2

    def half(ref, index):
        return tall(ref[pl.ds(index * width, width), :])

    north, north_uv = (
        jnp.where(
            is_top, sign * tall(mirror_ref[index, pl.ds(1, width), :]), half(north_ref, index)
        )
        for index, sign in ((0, 1.0), (1, -1.0))
    )
    south, south_uv = half(south_ref, 0), half(south_ref, 1)
    bottom = half(bottom_ref, 0)

    def line(ref, index):
        return jnp.broadcast_to(ref[pl.ds(index, 1), :], (SUB, lanes))

    def mirror_line(index, i):
        return jnp.broadcast_to(mirror_ref[index, pl.ds(i + 1, 1), :], (SUB, lanes))

    nw = jnp.where(is_top, mirror_line(0, -1), line(west_ref, depth_at + 2))
    nw_uv = jnp.where(is_top, -mirror_line(1, -1), line(west_ref, depth_at + 3))
    ne = jnp.where(is_top, mirror_line(0, width), line(east_ref, depth_at + 2))
    se = line(east_ref, depth_at + 4)
    se_uv = line(east_ref, depth_at + 5)

    def to_east(value, halo):
        return jnp.where(row == width - 1, halo, pltpu.roll(value, SUB - 1, 0))

    def to_west(value, halo):
        return jnp.where(row == 0, halo, pltpu.roll(value, 1, 0))

    def to_north(value, halo):
        return jnp.where(lane == lanes - 1, halo, pltpu.roll(value, lanes - 1, 1))

    def to_south(value, halo):
        return jnp.where(lane == 0, halo, pltpu.roll(value, 1, 1))

    def at_north(message, index):
        return pltpu.roll(message, lanes - 1 - index, 1)

    def at_south(message, index):
        return pltpu.roll(message, (lanes - index) % lanes, 1)

    depth = tall(depth_ref[...])
    d_n = to_north(depth, at_north(north, count_at))
    d_nn = to_north(d_n, at_north(north, count_at - 1))
    d_s = to_south(depth, at_south(south, count_at))
    d_e = to_east(depth, line(east_ref, depth_at))
    d_ee = to_east(d_e, line(east_ref, depth_at + 1))
    d_w = to_west(depth, line(west_ref, depth_at))
    east_line = line(east_ref, depth_at)
    west_line = line(west_ref, depth_at)
    d_ne = to_east(d_n, to_north(east_line, at_north(ne, count_at)))
    d_se = to_east(d_s, to_south(east_line, at_south(se, count_at)))
    d_nw = to_west(d_n, to_north(west_line, at_north(nw, count_at)))
    d_u = jnp.minimum(depth, d_e)
    d_v = jnp.minimum(depth, d_n)
    u_neighbours = [
        jnp.minimum(d_u, d)
        for d in (
            jnp.minimum(d_e, d_ee),
            d_w,
            jnp.minimum(d_n, d_ne),
            jnp.minimum(d_s, d_se),
        )
    ]
    v_neighbours = [
        jnp.minimum(d_v, d)
        for d in (
            jnp.minimum(d_e, d_ne),
            jnp.minimum(d_w, d_nw),
            jnp.minimum(d_n, d_nn),
            d_s,
        )
    ]

    level_row = lax.broadcasted_iota(jnp.int32, (levels, lanes), 0)
    level_lane = lax.broadcasted_iota(jnp.int32, (levels, lanes), 1)
    wet_row = jnp.minimum(
        west_ref[pl.ds(depth_at, 1), :], depth_ref[pl.ds(0, 1), :]
    )
    wet_face = level_row.astype(jnp.float32) < wet_row
    u_west = west_ref[pl.ds(4 * levels, levels), :]
    for place, field, target in ((0, t_ref, gx_t_ref), (2, s_ref, gx_s_ref)):
        near = west_ref[pl.ds(place * levels, levels), :]
        far = west_ref[pl.ds((place + 1) * levels, levels), :]
        own = field[:, 0, :]
        face = u_west * (1.0 / 12.0) * (7.0 * (near + own) - (far + field[:, 1, :]))
        target[...] = jnp.where(wet_face, face - TRACER_DIFF * (own - near), 0.0)

    def spread(corner, place, target):
        lines = jnp.broadcast_to(corner[0:1], (levels, lanes))
        shift = target - (3 * ((place + 1) * levels - 1) + 2)
        return pltpu.roll(lines, shift % lanes, 1, stride=3, stride_axis=0)

    u_corner = spread(nw_uv, 0, lanes - 1)
    v_corner = spread(se_uv, 1, 0)
    u2_ref[...] = u_west + jnp.where(
        level_lane == lanes - 1, u_corner, pltpu.roll(u_west, lanes - 1, 1)
    )
    v_east = east_ref[pl.ds(5 * levels, levels), :]
    v2_ref[...] = v_east + jnp.where(level_lane == 0, v_corner, pltpu.roll(v_east, 1, 1))

    in_block = jnp.where(lane < 3 * levels, lane, lane - 3 * levels).astype(jnp.float32)
    v_south = jnp.where(lane < 3 * levels, at_south(south_uv, 3 * levels), south_uv)
    both = south + bottom
    face = v_south * (1.0 / 12.0) * (7.0 * both - pltpu.roll(both, 1, 1))
    face = face - TRACER_DIFF * (bottom - south)
    wet_south = jnp.minimum(
        south[:, count_at : count_at + 1], bottom[:, count_at : count_at + 1]
    )
    face_south = jnp.where(in_block > 3.0 * (levels - wet_south), face, 0.0)

    third = lax.rem(lane, 3)
    near, near_uv = (
        jnp.where(third == 0, pltpu.roll(s, 1, 1), n)
        for n, s in ((north, south), (north_uv, south_uv))
    )
    far = jnp.where(third == 2, face_south, north)
    for place in range(2):
        for k in range(levels):
            spot = 3 * ((place + 1) * levels - 1 - k) + 2
            near_ref[place * levels + k] = at_north(near, spot)
            near_ref[(place + 2) * levels + k] = at_north(near_uv, spot)
            far_ref[place * levels + k] = at_north(far, spot - 1)

    row_id = (lat * lanes + lane).astype(jnp.float32)
    total = float(lat_count * lanes)
    cor_u = 2.0 * (row_id + 0.5) / total - 1.0
    cor_v = 2.0 * (row_id + 1.0) / total - 1.0
    inner, last = mixing_constants(levels)
    gain = TIME_STEP * VERTICAL_VISC

    def masked(k, count, value):
        return jnp.where(float(k) < count, value, 0.0)

    px = jnp.zeros((SUB, lanes), jnp.float32)
    py = jnp.zeros((SUB, lanes), jnp.float32)
    above = None
    ratio = None
    values = None
    for k in range(levels):
        u = tall(u_ref[k])
        v = tall(v_ref[k])
        u_face = masked(k, d_u, u * (1.0 / 12.0))
        u_diff = masked(k, d_u, TRACER_DIFF)
        v_face = masked(k, d_v, v * (1.0 / 12.0))
        v_diff = masked(k, d_v, TRACER_DIFF)
        stars = []
        seen = []
        for place, field, gx_ref in ((0, t_ref, gx_t_ref), (2, s_ref, gx_s_ref)):
            near, far = place * levels + k, (place + 1) * levels + k
            c = tall(field[k])
            c_e = to_east(c, line(east_ref, near))
            c_ee = to_east(c_e, line(east_ref, far))
            c_w = to_west(c, line(west_ref, near))
            beyond = near_ref[place // 2 * levels + k]
            c_n = to_north(c, beyond)
            beyond_2 = far_ref[place // 2 * levels + k]
            c_nn = to_north(c_n, beyond_2)
            c_s = to_south(c, beyond)
            gx = u_face * (7.0 * (c + c_e) - (c_w + c_ee)) - u_diff * (c_e - c)
            gy = v_face * (7.0 * (c + c_n) - (c_s + c_nn)) - v_diff * (c_n - c)
            gx_w = to_west(gx, line(gx_ref, k))
            gy_s = to_south(gy, beyond_2)
            stars.append(c - TIME_STEP * masked(k, depth, (gx - gx_w) + (gy - gy_s)))
            seen.append((c, c_e, c_n))
        weights = THERMAL_EXPANSION, HALINE_CONTRACTION
        b, b_e, b_n = (
            masked(k, d, weights[0] * warm - weights[1] * salt)
            for d, warm, salt in zip((depth, d_e, d_n), seen[0], seen[1])
        )
        bx = b_e - b
        by = b_n - b
        px = px + bx
        py = py + by

        u_e = to_east(u, line(east_ref, 4 * levels + k))
        u_w = to_west(u, line(west_ref, 4 * levels + k))
        u_n = to_north(u, near_ref[2 * levels + k])
        u_s = to_south(u, near_ref[2 * levels + k])
        v_e = to_east(v, line(east_ref, 5 * levels + k))
        v_w = to_west(v, line(west_ref, 5 * levels + k))
        v_n = to_north(v, near_ref[3 * levels + k])
        v_s = to_south(v, near_ref[3 * levels + k])
        v2 = v + v_s
        u2 = u + u_n
        v_bar = 0.25 * (v2 + to_east(v2, line(v2_ref, k)))
        u_bar = 0.25 * (u2 + to_west(u2, line(u2_ref, k)))
        u_visc = sum(masked(k, d, n - u) for d, n in zip(u_neighbours, (u_e, u_w, u_n, u_s)))
        v_visc = sum(masked(k, d, n - v) for d, n in zip(v_neighbours, (v_e, v_w, v_n, v_s)))
        u_star = u + TIME_STEP * (cor_u * v_bar - (px - 0.5 * bx) + MOMENTUM_VISC * u_visc)
        v_star = v + TIME_STEP * (-cor_v * u_bar - (py - 0.5 * by) + MOMENTUM_VISC * v_visc)
        if k == 0:
            u_star = u_star + TIME_STEP * WIND_GAIN * tall(wind_ref[0])
            v_star = v_star + TIME_STEP * WIND_GAIN * tall(wind_ref[1])

        if k < levels - 1:
            below = masked(k + 1, depth, TIME_STEP * tall(mix_ref[k]))
        else:
            below = None
        pivot = 1.0
        if above is not None:
            pivot = pivot + above * (1.0 - ratio)
        if below is not None:
            pivot = pivot + below
        inverse = 1.0 / pivot

        def momentum_weight(count):
            weight = jnp.where(float(k) < count, last[k], 0.0)
            if k < levels - 1:
                weight = jnp.where(float(k + 1) < count, inner[k], weight)
            return weight

        rights = stars + [u_star, v_star]
        scales = [inverse, inverse, momentum_weight(d_u), momentum_weight(d_v)]
        if k > 0:
            gains = [above, above, gain, gain]
            rights = [right + g * value for right, g, value in zip(rights, gains, values)]
        values = [right * scale for right, scale in zip(rights, scales)]
        for index, value in enumerate(values):
            val_ref[index, k] = value
        if below is not None:
            ratio = below * inverse
            val_ref[4, k] = ratio
        above = below

    outs = (t_out, s_out, u_out, v_out)
    for k in range(levels - 1, -1, -1):
        if k < levels - 1:
            ratios = [val_ref[4, k], val_ref[4, k], gain * inner[k], gain * inner[k]]
            values = [val_ref[i, k] + ratios[i] * values[i] for i in range(4)]
        for out, value in zip(outs, values):
            out[k] = value[:width]


def shards(
    thermal_anomaly,
    saltiness_anomaly,
    zonal_current,
    meridional_current,
    bottom_ocean_layer,
    seam_axis_meridian,
    interface_diffusivity,
    atmospheric_forcing,
):
    levels, width, lanes = thermal_anomaly.shape
    lon_count = lax.axis_size("lon")
    lat_count = lax.axis_size("lat")
    fields = (thermal_anomaly, saltiness_anomaly, zonal_current, meridional_current)
    wind = atmospheric_forcing
    f32 = jnp.float32
    row_message = jax.ShapeDtypeStruct((2 * width, lanes), f32)
    column_message = jax.ShapeDtypeStruct((6 * levels + 8, lanes), f32)

    fold_message = jax.ShapeDtypeStruct((6 * levels + 16, lanes), f32)
    lat_pairs = [
        [(a, b) for i in range(start, lat_count - 1, 2) for a, b in ((i, i + 1), (i + 1, i))]
        for start in (0, 1)
    ]
    lat_pairs = [pairs for pairs in lat_pairs if pairs]
    top, bottom, eastward, westward, counts, stress, *messages = pl.pallas_call(
        edges_kernel,
        out_shape=[row_message] * 2
        + [column_message] * 2
        + [jax.ShapeDtypeStruct((width, lanes), f32), jax.ShapeDtypeStruct(wind.shape, f32)]
        + [jax.ShapeDtypeStruct((4 * width, lanes), f32), row_message][: len(lat_pairs)],
        in_specs=[VMEM] * 6,
        out_specs=[VMEM] * (6 + len(lat_pairs)),
        compiler_params=FIRST,
    )(*[pltpu.with_memory_space_constraint(x, pltpu.HBM) for x in (*fields, bottom_ocean_layer, wind)])
    received = [
        lax.ppermute(message, "lat", pairs) for message, pairs in zip(messages, lat_pairs)
    ]

    north, south, eastward, fold, westward, rest = pl.pallas_call(
        corners_kernel,
        out_shape=[row_message] * 2
        + [column_message, fold_message, column_message]
        + [jax.ShapeDtypeStruct((SUB, lanes), jnp.int32)],
        in_specs=[VMEM] * 3 + [SMEM] + [VMEM] * len(received),
        out_specs=[VMEM] * 6,
        compiler_params=SMALL,
    )(top, eastward, westward, seam_axis_meridian, *received)

    code = seam_axis_meridian[0]
    tile = lax.rem(lax.div(code, width), lon_count)
    three = (lax.rem(code, width) == width - 1).astype(jnp.int32)
    ring = [(i, (i + 1) % lon_count) for i in range(lon_count)]
    trade = [(i, i ^ 1) for i in range(lon_count)]
    pairs = [(i, i ^ 1) for i in range(lat_count)]

    def fold_pairs(*mirrors):
        rows = [*mirrors] + [trade] * (lat_count - len(mirrors))
        return [
            (a * lat_count + lat_count - 1 - row, b * lat_count + lat_count - 1 - row)
            for row, mirror in enumerate(rows)
            for a, b in mirror
        ]

    from_west = lax.ppermute(eastward, "lon", ring)
    keep = pl.pallas_call(
        keep_kernel,
        out_shape=column_message,
        in_specs=[VMEM],
        out_specs=VMEM,
        compiler_params=SMALL,
    )

    def reflect(code):
        own = [i for i in range(lon_count) if (code - i) % lon_count == i]
        if len(own) != 2:
            return [(i, (code - i) % lon_count) for i in range(lon_count)], []
        trade = {own[0]: own[1], own[1]: own[0]}
        return [(i, trade.get(i, (code - i) % lon_count)) for i in range(lon_count)], own

    def exchange(first, count):
        direct = first % 2
        mirrors, own_tiles = zip(*(reflect(first - 1 + d) for d in range(3)))
        mirror = pl.pallas_call(
            functools.partial(mirror_kernel, own_tiles),
            out_shape=jax.ShapeDtypeStruct((2, 16, lanes), f32),
            in_specs=[VMEM] * (2 + count),
            out_specs=VMEM,
            scratch_shapes=[pltpu.VMEM((2, 3 * width, lanes), f32)],
            compiler_params=SMALL,
        )

        def branch(fold, westward, rest):
            both = ("lon", "lat")
            straight, handed = (2 - direct, 1 + direct) if count == 3 else (direct, 1 - direct)
            tile = lax.ppermute(fold, both, fold_pairs(mirrors[straight], mirrors[handed]))
            tiles = {straight: tile, handed: lax.ppermute(tile[: 2 * width], "lat", pairs)}
            if count == 3:
                tiles[0] = lax.ppermute(fold, both, fold_pairs(mirrors[0]))
            tiles = [tiles[d] for d in range(count)]
            return (
                keep(lax.ppermute(westward, "lon", [(b, a) for a, b in ring])),
                mirror(fold, rest, *tiles),
            )

        return branch

    branches = [exchange(first, count) for first in range(lon_count) for count in (2, 3)]
    from_east, mirrored = lax.switch(
        tile * 2 + three, branches, fold, westward, rest
    )

    whole = jax.ShapeDtypeStruct((levels, width, lanes), f32)
    return pl.pallas_call(
        step_kernel,
        out_shape=[whole] * 4,
        in_specs=[VMEM] * 13,
        out_specs=[VMEM] * 4,
        compiler_params=LARGE,
        scratch_shapes=[pltpu.VMEM((levels, lanes), f32)] * 4
        + [pltpu.VMEM((5, levels, SUB, lanes), f32)]
        + [pltpu.VMEM((count * levels, SUB, lanes), f32) for count in (4, 2)],
    )(
        *fields,
        counts,
        interface_diffusivity,
        stress,
        bottom,
        north,
        south,
        from_west,
        from_east,
        mirrored,
    )


def solution(mesh):
    split = P(None, "lon", "lat")
    return jax.shard_map(
        shards,
        mesh=mesh,
        in_specs=(split, split, split, split, P("lon", "lat"), P(), split, split),
        out_specs=(split, split, split, split),
        check_vma=False,
    )
```
